32 devices in a mesh: grp: 2 (over y), ep: 8 (over z, x), tp: 2 (over core).
Axes of the slice: x: 2, y: 2, z: 4, core: 2. Of those that a mesh axis runs over, the one named last changes fastest.
Arguments:
- residual: bfloat16 [128, 7168], P(('grp', 'ep')), parts along dimension 0, may hold values from -12 to 12
- queries: bfloat16 [128, 16384], P(('grp', 'ep'), 'tp'), parts along dimension 0, may hold values from -8 to 8
- new_kv: bfloat16 [128, 512], P(('grp', 'ep')), parts along dimension 0, may hold values from -4 to 4
- cache: bfloat16 [128, 384, 512], P(('grp', 'ep')), parts along dimension 0, may hold values from -8 to 8
- lengths: int32 [128], P(('grp', 'ep')), parts along dimension 0, may hold values from 2 to 384, as said below
- w_out: bfloat16 [16384, 7168], P('tp', 'ep'), may hold values from -0.046875 to 0.046875
- gain: float32 [7168], replicated, may hold values from 0.5 to 1.5
- route_ids: int32 [128, 3], P(('grp', 'ep')), parts along dimension 0, may hold values from 0 to 3, all different within a row; in each aligned block of 8 rows (0 to 7, 8 to 15, ...) at most 8 rows name the same one
- route_weights: float32 [128, 3], P(('grp', 'ep')), parts along dimension 0, may hold values from 0.2 to 1
- w_gate: bfloat16 [7168, 2560], P(None, ('ep', 'tp')), may hold values from -0.0625 to 0.0625
- w_up: bfloat16 [7168, 2560], P(None, ('ep', 'tp')), may hold values from -0.0625 to 0.0625
- w_down: bfloat16 [2560, 7168], P(('ep', 'tp')), may hold values from -0.25 to 0.25
Outputs:
- output: bfloat16 [128, 7168], P(('grp', 'ep'), 'tp'), parts along dimension 0
The draws below stay inside these ranges and needn't reach their ends.
There are 2 independent parts, one for each index of `grp`. The reference program is written for one: setup_inputs(seed, part) draws one part's arguments, and reference() takes and returns one part's arrays. A program takes and returns all parts, laid end to end along the dimension named above; an argument that names none is the same for every part. Nothing has to cross between parts.
Inputs may be any that keep to these rules, and one draw needn't show every extreme that they name: `route_ids`: a row names 3 different experts; in the rows of one device (aligned blocks of 8 rows) no expert is named by more than 8 rows. `lengths`: some row holds exactly 384 cached tokens.
All inputs are finite; a program needn't handle non-finite values.
Results may differ from the reference program's by a relative error of at most 0.006.
Values may be sent and summed in bfloat16 or wider, within the bound.
No kernel may reach another device: no remote copies, remote signals or barrier semaphores. Data moves between devices by JAX's collectives and lax.ppermute only.
A program may use at most 128 MiB of HBM per device.

```python
import math
import jax
import jax.numpy as jnp
import numpy as np
from jax import lax

D = 7168
HEADS = 64
HD = 256
TOPK = 3
EXPERTS = 4
ROWS_DEV = 8
CTX = 384
ROWS = 64
CAP = 8
FFW = 640


def draw_queries(key, part):
    key = jax.random.fold_in(key, 1)
    entries = jnp.clip(jax.random.normal(key, (ROWS, HEADS * HD), jnp.float32), -4.0, 4.0)
    return entries.astype(jnp.bfloat16)


def draw_cache(key, part):
    key = jax.random.fold_in(key, 2)
    entries = jnp.clip(jax.random.normal(key, (ROWS, CTX, 2 * HD), jnp.float32), -4.0, 4.0)
    return entries.astype(jnp.bfloat16)


def draw_lengths(key, part):
    key = jax.random.fold_in(key, 3)
    drawn = jax.random.randint(key, (ROWS,), 2, CTX + 1)
    full_row = jax.random.randint(jax.random.fold_in(key, 4), (), 0, ROWS)
    return jnp.where(jnp.arange(ROWS) == full_row, CTX, drawn).astype(jnp.int32)


def draw_residual(key, part):
    key = jax.random.fold_in(key, 5)
    entries = jnp.clip(jax.random.normal(key, (ROWS, D), jnp.float32), -4.0, 4.0)
    return entries.astype(jnp.bfloat16)


def level_of(rng, shape, split, least, largest):
    def one(dim, parts):
        heights = jax.random.uniform(jax.random.fold_in(jax.random.fold_in(rng, 6), dim), (parts,), jnp.float32, least / len(split), largest / len(split))
        return jnp.repeat(jnp.exp(heights), shape[dim] // parts).reshape((-1,) + (1,) * (len(shape) - dim - 1))

    loudness = one(*split[0])
    for cut in split[1:]:
        loudness = loudness * one(*cut)
    return loudness


def routed_block(stream_key, own, number, rows, number_of, top, bound, skew):
    ranking = jax.random.permutation(stream_key, number_of)
    heavy_load, common = shares(number_of, rows * top, bound, skew, True), shares(number_of, rows * top, bound, skew, False)
    places = jnp.arange(number_of)

    def named(tallies, offset_by):
        used = int((tallies > 0).sum())
        fixed = max(1, used // 4)
        shifted = fixed + (places - fixed + offset_by * (used - fixed)) % max(1, number_of - fixed)
        return jnp.zeros((number_of,), jnp.int32).at[ranking[jnp.where(places < fixed, places, shifted)]].set(jnp.asarray(tallies, jnp.int32))

    tallies = jnp.where(number % 4 == 0, named(heavy_load, number // 4), named(common, number - number // 4 - 1))
    mixed = jax.random.permutation(jax.random.fold_in(own, 3), number_of)
    donor, taker = mixed[0:number_of // 2 * 2:2], mixed[1:number_of // 2 * 2:2]
    room = jnp.minimum(tallies[donor] - 1, bound - tallies[taker]) // 2
    room = jnp.where((donor == ranking[0]) | (taker == ranking[0]) | (tallies[taker] == 0), 0, jnp.maximum(room, 0))
    shifted = jax.random.randint(jax.random.fold_in(own, 4), (number_of // 2,), 0, 1 << 20) % (room + 1)
    tallies = tallies.at[donor].add(-shifted).at[taker].add(shifted)
    labels = jnp.searchsorted(jnp.cumsum(tallies), jnp.arange(rows * top), side="right").astype(jnp.int32)
    grid = labels.reshape(top, rows).T
    grid = grid[jax.random.permutation(jax.random.fold_in(own, 1), rows)]
    offset_by = jax.random.randint(jax.random.fold_in(own, 2), (rows, 1), 0, top)
    return jnp.take_along_axis(grid, (jnp.arange(top)[None, :] + offset_by) % top, axis=1)


def shares(count, total, limit, lean, full):
    portions = [(1 << 20) // math.isqrt(standing ** lean) + 1 for standing in range(1, count + 1)]
    largest = limit if full else min(limit, max(-(-total // count), total * portions[0] // sum(portions)))
    least = 1 if total - largest >= count - 1 else 0
    counts, surplus = [largest] + [least] * (count - 1), total - largest - least * (count - 1)
    while surplus > 0:
        movable = [i for i in range(1, count) if counts[i] < largest] or [i for i in range(1, count) if counts[i] < limit]
        mass, remaining = sum([portions[i] for i in movable]), surplus
        for i in movable:
            more = min(limit - counts[i], max(1, remaining * portions[i] // mass), surplus)
            counts[i] = counts[i] + more
            surplus = surplus - more
    return np.array(counts)


def scatter_about(stream_key, extent, deviation, limit, split=(), kind=jnp.bfloat16):
    loudness = level_of(stream_key, extent, split, -0.22, 0.18) if split else 1.0
    array = jax.random.normal(stream_key, extent, jnp.float32) * deviation * loudness
    return jnp.minimum(jnp.maximum(array, -limit), limit).astype(kind)


def setup_inputs(seed: int = 0, part: int = 0) -> dict:
    seeds = jax.random.split(jax.random.key(seed), 13)
    part_keys = jax.random.split(jax.random.fold_in(seeds[12], part), 13)
    residual = draw_residual(jax.random.fold_in(jax.random.fold_in(seeds[12], part), 71), part)
    queries = draw_queries(jax.random.fold_in(jax.random.fold_in(seeds[12], part), 71), part)
    new_kv = scatter_about(part_keys[2], (ROWS, 2 * HD), 1.0, 4.0, ((0, 8),))
    cache = draw_cache(jax.random.fold_in(jax.random.fold_in(seeds[12], part), 71), part)
    lengths = draw_lengths(jax.random.fold_in(jax.random.fold_in(seeds[12], part), 71), part)
    w_out = scatter_about(seeds[5], (HEADS * HD, D), (HEADS * HD) ** -0.5, 0.046875, ((0, 2), (1, 8)))
    gain = jnp.clip(1.0 + 0.1 * jax.random.normal(seeds[6], (D,), jnp.float32), 0.5, 1.5)
    route_ids_keys = jax.random.split(jax.random.fold_in(part_keys[7], 1), ROWS // ROWS_DEV)
    route_ids_turns = jax.random.permutation(jax.random.fold_in(part_keys[7], 3), ROWS // ROWS_DEV)
    route_ids = jax.vmap(lambda own, number: routed_block(jax.random.fold_in(part_keys[7], 2), own, number, ROWS_DEV, EXPERTS, TOPK, CAP, 2))(route_ids_keys, route_ids_turns).reshape((ROWS, TOPK))
    route_weights = jnp.clip(0.2 + 0.8 * jax.random.uniform(part_keys[8], (ROWS, TOPK), jnp.float32) ** level_of(part_keys[8], (ROWS, TOPK), ((0, 8),), -0.2, 0.2), 0.2, 1.0)
    w_gate = scatter_about(seeds[9], (D, EXPERTS * FFW), D ** -0.5, 0.0625, ((1, 16),))
    w_up = scatter_about(seeds[10], (D, EXPERTS * FFW), D ** -0.5, 0.0625, ((1, 16),))
    w_down = scatter_about(seeds[11], (EXPERTS * FFW, D), FFW ** -0.5, 0.25, ((0, 16),))
    return {"residual": residual, "queries": queries, "new_kv": new_kv, "cache": cache, "lengths": lengths, "w_out": w_out, "gain": gain, "route_ids": route_ids, "route_weights": route_weights, "w_gate": w_gate, "w_up": w_up, "w_down": w_down}


def attend_single(query_row, cache_rows, own_pair, length_value):
    scaling = HD ** (-0.5)
    query_heads = query_row.astype(jnp.float32).reshape(HEADS, HD)
    key_rows = cache_rows[:, :HD].astype(jnp.float32)
    value_rows = cache_rows[:, HD:].astype(jnp.float32)
    scores = jnp.einsum('hd,pd->hp', query_heads, key_rows) * scaling
    usable = jnp.arange(CTX, dtype=jnp.int32) < length_value
    scores = jnp.where(usable[None, :], scores, -jnp.inf)
    own_score = jnp.einsum('hd,d->h', query_heads, own_pair[:HD].astype(jnp.float32)) * scaling
    peak_score = jnp.maximum(lax.optimization_barrier(jnp.max(scores, axis=1)), own_score)
    cache_weight = jnp.exp(scores - peak_score[:, None])
    own_weight = jnp.exp(own_score - peak_score)
    denominator = lax.optimization_barrier(jnp.sum(cache_weight, axis=1)) + own_weight
    probabilities = lax.optimization_barrier((cache_weight / denominator[:, None]).astype(jnp.bfloat16))
    own_prob = lax.optimization_barrier((own_weight / denominator).astype(jnp.bfloat16))
    context = jnp.einsum('hp,pd->hd', probabilities.astype(jnp.float32), value_rows)
    context = context + own_prob.astype(jnp.float32)[:, None] * own_pair[HD:].astype(jnp.float32)[None, :]
    return context.astype(jnp.bfloat16).reshape(HEADS * HD)

def reference(residual, queries, new_kv, cache, lengths, w_out, gain, route_ids, route_weights, w_gate, w_up, w_down):

    def single(packed):
        return attend_single(packed[0], packed[1], packed[2], packed[3])
    context = lax.map(single, (queries, cache, new_kv, lengths))
    attention_out = jnp.dot(context, w_out, preferred_element_type=jnp.float32)
    stream = residual.astype(jnp.float32) + attention_out
    mean_square = lax.optimization_barrier(jnp.mean(stream * stream, axis=1, keepdims=True))
    normed = (stream * lax.rsqrt(mean_square + 1e-06) * gain[None, :]).astype(jnp.bfloat16)
    expert_range = jnp.arange(EXPERTS, dtype=jnp.int32)
    coefficient = lax.optimization_barrier(jnp.sum((route_ids[:, :, None] == expert_range[None, None, :]).astype(jnp.float32) * route_weights[:, :, None], axis=1))
    mixture = jnp.zeros(stream.shape, jnp.float32)
    for expert in range(EXPERTS):
        first = expert * FFW
        gate_act = jnp.dot(normed, w_gate[:, first:first + FFW], preferred_element_type=jnp.float32)
        up_act = jnp.dot(normed, w_up[:, first:first + FFW], preferred_element_type=jnp.float32)
        expert_hidden = (jax.nn.silu(gate_act) * up_act).astype(jnp.bfloat16)
        expert_out = jnp.dot(expert_hidden, w_down[first:first + FFW, :], preferred_element_type=jnp.float32)
        mixture = mixture + coefficient[:, expert:expert + 1] * expert_out
    return (stream + mixture).astype(jnp.bfloat16)
```

```python
import jax
import jax.numpy as jnp
from jax import lax
from jax.sharding import PartitionSpec as P

HD = 256
EXPERTS = 4


def grid_of(ep_size):
    x_size = 1 << ((ep_size.bit_length() - 1) // 3)
    return ep_size // x_size, x_size


def shift_z(arr, step, z_size, x_size):
    pairs = [
        (z * x_size + x, (z + step) % z_size * x_size + x)
        for z in range(z_size)
        for x in range(x_size)
    ]
    return lax.ppermute(arr, "ep", pairs)


def shift_x(arr, step, z_size, x_size):
    pairs = [
        (z * x_size + x, z * x_size + (x + step) % x_size)
        for z in range(z_size)
        for x in range(x_size)
    ]
    return lax.ppermute(arr, "ep", pairs)


def swap(arr):
    return lax.ppermute(arr, "tp", [(0, 1), (1, 0)])


def spread(own, z_size, x_size):
    column = [own]
    for _ in range(1, z_size):
        column.append(shift_z(column[-1], 1, z_size, x_size))
    return [
        [chunk] + [shift_x(chunk, u, z_size, x_size) for u in range(1, x_size)] for chunk in column
    ]


def attend(queries, new_kv, cache, lengths):
    row_count = queries.shape[0]
    head_count = queries.shape[1] // HD
    scaling = HD ** (-0.5)
    query_heads = queries.reshape(row_count, head_count, HD)
    key_rows = cache[:, :, :HD]
    value_rows = cache[:, :, HD:]
    scores = (
        jnp.einsum("rhd,rpd->rhp", query_heads, key_rows, preferred_element_type=jnp.float32)
        * scaling
    )
    usable = jnp.arange(cache.shape[1], dtype=jnp.int32)[None, :] < lengths[:, None]
    scores = jnp.where(usable[:, None, :], scores, -jnp.inf)
    own_score = (
        jnp.einsum("rhd,rd->rh", query_heads, new_kv[:, :HD], preferred_element_type=jnp.float32)
        * scaling
    )
    peak_score = jnp.maximum(jnp.max(scores, axis=2), own_score)
    cache_weight = jnp.exp(scores - peak_score[:, :, None])
    own_weight = jnp.exp(own_score - peak_score)
    denominator = jnp.sum(cache_weight, axis=2) + own_weight
    probabilities = (cache_weight / denominator[:, :, None]).astype(jnp.bfloat16)
    own_prob = (own_weight / denominator).astype(jnp.bfloat16)
    context = jnp.einsum(
        "rhp,rpd->rhd", probabilities, value_rows, preferred_element_type=jnp.float32
    )
    context = context + own_prob.astype(jnp.float32)[:, :, None] * new_kv[:, None, HD:].astype(
        jnp.float32
    )
    return context.astype(jnp.bfloat16).reshape(row_count, head_count * HD)


def body(
    residual,
    queries,
    new_kv,
    cache,
    lengths,
    w_out,
    gain,
    route_ids,
    route_weights,
    w_gate,
    w_up,
    w_down,
):
    ep_size = lax.axis_size("ep")
    z_size, x_size = grid_of(ep_size)
    me = lax.axis_index("ep")
    z_me, x_me = me // x_size, me % x_size
    core = lax.axis_index("tp")
    rows = residual.shape[0]
    width = residual.shape[1]
    cols = w_out.shape[1]
    half = cols // 2

    experts = jnp.arange(EXPERTS, dtype=jnp.int32)
    coefficient = jnp.sum(
        (route_ids[:, :, None] == experts[None, None, :]).astype(jnp.float32)
        * route_weights[:, :, None],
        axis=1,
    )
    mine = lax.dynamic_slice_in_dim(residual.reshape(rows, ep_size, cols), core * half, half, 2)
    residual_cols = lax.all_to_all(mine, "ep", split_axis=1, concat_axis=0, tiled=True)
    residual_cols = residual_cols.reshape(ep_size, rows, half)
    first = lax.all_gather(coefficient, "ep", axis=0, tiled=True)
    weight = lax.dynamic_slice_in_dim(first, me * EXPERTS // ep_size, 1, 1)

    context = attend(queries, new_kv, cache, lengths)
    chunks = spread(context, z_size, x_size)
    gathered = jnp.concatenate([c for line in chunks for c in line], axis=0)
    attn = jnp.dot(gathered, w_out, preferred_element_type=jnp.float32)
    attn = attn.reshape(z_size, x_size, rows, cols)
    z_order = (z_me - jnp.arange(z_size)) % z_size
    x_order = (x_me - jnp.arange(x_size)) % x_size
    attn = jnp.take(jnp.take(attn, z_order, axis=0), x_order, axis=1)
    attn = attn.reshape(ep_size, rows, cols)
    theirs = lax.dynamic_slice_in_dim(attn, (1 - core) * half, half, 2)
    ours = lax.dynamic_slice_in_dim(attn, core * half, half, 2)
    stream_cols = residual_cols.astype(jnp.float32) + (ours + swap(theirs))
    stream_cols = stream_cols.astype(jnp.bfloat16).reshape(ep_size * rows, half)

    blocks = spread(stream_cols, z_size, x_size)
    stream_half = jnp.stack([b for line in blocks for b in line]).reshape(
        z_size, x_size, ep_size * rows, half
    )
    stream_half = jnp.take(jnp.take(stream_half, z_order, axis=0), x_order, axis=1)
    stream_half = stream_half.reshape(ep_size, ep_size * rows, half)
    other_half = swap(stream_half)
    low = jnp.where(core == 0, stream_half, other_half)
    high = jnp.where(core == 0, other_half, stream_half)
    stream = jnp.concatenate([low, high], axis=2).transpose(1, 0, 2).reshape(ep_size * rows, width)
    stream = stream.astype(jnp.float32)
    mean_square = jnp.mean(stream * stream, axis=1, keepdims=True)
    normed = (stream * lax.rsqrt(mean_square + 1e-06) * gain[None, :]).astype(jnp.bfloat16)

    gate_act = jnp.dot(normed, w_gate, preferred_element_type=jnp.float32)
    up_act = jnp.dot(normed, w_up, preferred_element_type=jnp.float32)
    hidden = (jax.nn.silu(gate_act) * up_act).astype(jnp.bfloat16)
    partial_value = weight * jnp.dot(hidden, w_down, preferred_element_type=jnp.float32)
    out_width = width // 2
    ours = lax.dynamic_slice_in_dim(partial_value, core * out_width, out_width, 1)
    theirs = lax.dynamic_slice_in_dim(partial_value, (1 - core) * out_width, out_width, 1)
    mixed = ours + swap(theirs.astype(jnp.bfloat16)).astype(jnp.float32)
    mixed = mixed.reshape(z_size, x_size, rows, out_width)
    total = lax.dynamic_index_in_dim(mixed, x_me, 1, keepdims=False)
    for u in range(1, x_size):
        leaving = lax.dynamic_index_in_dim(mixed, (x_me + u) % x_size, 1, keepdims=False)
        total = total + shift_x(leaving.astype(jnp.bfloat16), u, z_size, x_size).astype(jnp.float32)
    result = lax.dynamic_index_in_dim(total, z_me, 0, keepdims=False)
    for s in range(1, z_size):
        leaving = lax.dynamic_index_in_dim(total, (z_me + s) % z_size, 0, keepdims=False)
        result = result + shift_z(leaving.astype(jnp.bfloat16), s, z_size, x_size).astype(
            jnp.float32
        )
    home = lax.dynamic_slice(stream, (me * rows, core * out_width), (rows, out_width))
    return (home + result).astype(jnp.bfloat16)


def solution(mesh):
    placed = (
        P(("grp", "ep"), None),
        P(("grp", "ep"), "tp"),
        P(("grp", "ep"), None),
        P(("grp", "ep"), None, None),
        P(("grp", "ep")),
        P("tp", "ep"),
        P(),
        P(("grp", "ep"), None),
        P(("grp", "ep"), None),
        P(None, ("ep", "tp")),
        P(None, ("ep", "tp")),
        P(("ep", "tp"), None),
    )
    return jax.shard_map(
        body, mesh=mesh, in_specs=placed, out_specs=P(("grp", "ep"), "tp"), check_vma=False
    )
```

```python
import functools

import jax
import jax.numpy as jnp
from jax import lax
from jax.experimental import pallas as pl
from jax.experimental.pallas import tpu as pltpu
from jax.sharding import PartitionSpec as P

HD = 256
TOPK = 3
EXPERTS = 4
CAP = 8
LANES = 128
VMEM_BYTES = 48 * 1024 * 1024


def params():
    return pltpu.CompilerParams(vmem_limit_bytes=VMEM_BYTES)


def vmem():
    return pl.BlockSpec(memory_space=pltpu.VMEM)


def shape_of(shape, dtype):
    return jax.ShapeDtypeStruct(shape, dtype)


class Grid:
    def __init__(self, ep_size, x_size):
        self.ep, self.x, self.z = ep_size, x_size, ep_size // x_size
        self.steps = [(s, u) for s in range(self.z) for u in range(x_size)]

    def send(self, arr, s, u):
        pairs = [
            (z * self.x + x, (z + s) % self.z * self.x + (x + u) % self.x)
            for z in range(self.z)
            for x in range(self.x)
        ]
        return lax.ppermute(arr, "ep", pairs)

    def spread(self, own):
        got = {(0, 0): own}
        for s in range(1, self.z):
            got[s, 0] = self.send(own, s, 0)
        for s in range(self.z):
            for u in range(1, self.x):
                got[s, u] = self.send(got[s, 0], 0, u)
        return [got[step] for step in self.steps]

    def source(self, step):
        me = lax.axis_index("ep")
        z = lax.rem(me // self.x - step[0] + self.z, self.z)
        return z * self.x + lax.rem(lax.rem(me, self.x) - step[1] + self.x, self.x)

    def target(self, step):
        return self.source((-step[0] % self.z, -step[1] % self.x))


def swap(arr):
    return lax.ppermute(arr, "tp", [(0, 1), (1, 0)])


def nt_dot(a, b):
    return lax.dot_general(a, b, (((1,), (1,)), ((), ())), preferred_element_type=jnp.float32)


def attention(grid, piece, cols, queries, new_kv, cache, lengths, residual, route_ids, route_weights):
    rows, width = queries.shape
    heads = width // HD
    ctx = cache.shape[1]
    tall = rows * heads
    scaling = HD ** (-0.5)

    def kernel(len_ref, q_ref, kv_ref, cache_ref, res_ref, ids_ref, wts_ref, *rest):
        out_refs, msg_refs = rest[:2], rest[2 : 2 + grid.ep]
        kept, score, sems = rest[2 + grid.ep :]
        copies = [
            pltpu.make_async_copy(cache_ref.at[r], kept.at[r], sems.at[r]) for r in range(rows)
        ]
        for copy in copies:
            copy.start()

        other = lax.axis_index("tp") * (cols - piece)
        lane = lax.broadcasted_iota(jnp.int32, (rows, LANES), 1)
        for i, step in enumerate(grid.steps):
            to = grid.target(step)
            begin = pl.multiple_of(to * cols + other, LANES)
            msg_refs[i][:, :piece] = res_ref[:, pl.ds(begin, piece)]
            expert = to * EXPERTS // grid.ep
            weight = jnp.sum(jnp.where(ids_ref[...] == expert, wts_ref[...], 0.0), axis=1, keepdims=True)
            high = weight.astype(jnp.bfloat16)
            left = weight - high.astype(jnp.float32)
            middle = left.astype(jnp.bfloat16)
            low = (left - middle.astype(jnp.float32)).astype(jnp.bfloat16)
            tile = jnp.where(
                lane == 0,
                high.astype(jnp.float32),
                jnp.where(
                    lane == 1,
                    middle.astype(jnp.float32),
                    jnp.where(lane == 2, low.astype(jnp.float32), 0.0),
                ),
            )
            msg_refs[i][:, piece:] = tile.astype(jnp.bfloat16)

        q = q_ref[...].astype(jnp.float32)
        stacked = jnp.concatenate([q[:, h * HD : (h + 1) * HD] for h in range(heads)], axis=0)
        narrow = stacked.astype(jnp.bfloat16)
        new_kv_f = kv_ref[...].astype(jnp.float32)
        new_k = jnp.concatenate([new_kv_f[:, :HD]] * heads, axis=0)
        new_v = jnp.concatenate([new_kv_f[:, HD:]] * heads, axis=0)
        own = jnp.sum(stacked * new_k, axis=1, keepdims=True) * scaling
        row_of = lax.rem(lax.broadcasted_iota(jnp.int32, (tall, 1), 0), rows)
        row_wide = lax.rem(lax.broadcasted_iota(jnp.int32, (tall, ctx), 0), rows)
        length = jnp.zeros((tall, 1), jnp.int32)
        for r in range(rows):
            length = jnp.where(row_of == r, len_ref[r], length)
        for r in range(rows):
            copies[r].wait()
            part = nt_dot(narrow, kept[r, :, :HD])
            score[...] = jnp.where(row_wide == r, part, score[...]) if r else part
        place = lax.broadcasted_iota(jnp.int32, (tall, ctx), 1)
        scores = jnp.where(place < length, score[...] * scaling, -jnp.inf)
        peak = jnp.maximum(jnp.max(scores, axis=1, keepdims=True), own)
        exps = jnp.exp(scores - peak)
        own_exp = jnp.exp(own - peak)
        denominator = jnp.sum(exps, axis=1, keepdims=True) + own_exp
        prob = exps / denominator
        own_prob = (own_exp / denominator).astype(jnp.bfloat16).astype(jnp.float32)
        total = own_prob * new_v
        for r in range(rows):
            only = jnp.where(row_wide == r, prob, 0.0).astype(jnp.bfloat16)
            total = total + jnp.dot(only, kept[r, :, HD:], preferred_element_type=jnp.float32)
        for h in range(heads):
            part, at = divmod(h, heads // 2)
            out_refs[part][:, at * HD : (at + 1) * HD] = total[h * rows : (h + 1) * rows].astype(
                jnp.bfloat16
            )

    outs = pl.pallas_call(
        kernel,
        name="attention",
        out_shape=[shape_of((rows, width // 2), jnp.bfloat16)] * 2
        + [shape_of((rows, piece + LANES), jnp.bfloat16)] * grid.ep,
        in_specs=[pl.BlockSpec(memory_space=pltpu.SMEM), vmem(), vmem(), pl.BlockSpec(memory_space=pl.ANY)]
        + [vmem()] * 3,
        out_specs=[vmem()] * (2 + grid.ep),
        scratch_shapes=[
            pltpu.VMEM(cache.shape[:2] + (2 * HD,), jnp.bfloat16),
            pltpu.VMEM((tall, ctx), jnp.float32),
            pltpu.SemaphoreType.DMA((rows,)),
        ],
        compiler_params=params(),
    )(lengths, queries, new_kv, cache, residual, route_ids, route_weights)
    return outs[0], outs[1], outs[2:]


def project(grid, piece, part, chunks, w_out, before=None, messages=()):
    rows, depth = chunks[0].shape
    cols = w_out.shape[1]
    count = len(chunks)
    tall = rows * count
    block = depth // 4
    last = before is not None

    def kernel(*refs):
        chunk_refs, rest = refs[:count], refs[count:]
        w_ref, rest = rest[0], rest[1:]
        if last:
            before_ref, message_refs, rest = rest[0], rest[1 : 1 + count], rest[1 + count :]
            ours_ref, theirs_ref, weight_ref = rest[:3]
            stacked, total = rest[3:]
        else:
            out_ref, stacked, total = rest
        k = pl.program_id(0)

        @pl.when(k == 0)
        def _():
            both = jnp.concatenate([ref[...] for ref in chunk_refs], axis=0)
            for i in range(depth // block):
                stacked[i] = both[:, i * block : (i + 1) * block]

        product = jnp.dot(stacked[k], w_ref[...], preferred_element_type=jnp.float32)

        @pl.when(k == 0)
        def _():
            total[...] = product + before_ref[...] if last else product

        @pl.when(k > 0)
        def _():
            total[...] += product

        @pl.when(k == depth // block - 1)
        def _():
            if not last:
                out_ref[...] = total[...]
                return
            core = lax.axis_index("tp")
            mine = pl.multiple_of(core * (cols - piece), LANES)
            other = pl.multiple_of((1 - core) * (cols - piece), LANES)
            for i, step in enumerate(grid.steps):
                here = pl.ds(pl.multiple_of(grid.source(step) * rows, rows), rows)
                message = message_refs[i][...].astype(jnp.float32)
                ours_ref[here, :] = total[i * rows : (i + 1) * rows, pl.ds(mine, piece)] + message[:, :piece]
                theirs_ref[here, :] = total[i * rows : (i + 1) * rows, pl.ds(other, piece)]
                weight_ref[here, :] = jnp.broadcast_to(
                    jnp.sum(message[:, piece:], axis=1, keepdims=True), (rows, LANES)
                )

    def whole(arr):
        return pl.BlockSpec(arr.shape, lambda k: (0, 0))

    outs = (
        [shape_of((tall, piece), jnp.float32)] * 2 + [shape_of((tall, LANES), jnp.float32)]
        if last
        else [shape_of((tall, cols), jnp.float32)]
    )
    extra = ([before] if last else []) + list(messages)
    result = pl.pallas_call(
        kernel,
        name="project",
        grid=(depth // block,),
        out_shape=outs,
        in_specs=[whole(c) for c in chunks]
        + [pl.BlockSpec((block, cols), lambda k: (part * (depth // block) + k, 0))]
        + [whole(e) for e in extra],
        out_specs=[whole(o) for o in outs],
        scratch_shapes=[
            pltpu.VMEM((depth // block, tall, block), jnp.bfloat16),
            pltpu.VMEM((tall, cols), jnp.float32),
        ],
        compiler_params=params(),
    )(*chunks, w_out, *extra)
    return result if last else result[0]


def pack_weights(grid, piece, cols, gate_t, up_t, w_down):
    units, width = gate_t.shape
    out_width = width // 2

    def kernel(gate_ref, up_ref, down_ref, pack_ref, half_ref, sems):
        other = 1 - lax.axis_index("tp")
        copies = []
        for j in range(grid.ep):
            begin = pl.multiple_of(j * cols + other * (cols - piece), LANES)
            for i, ref in enumerate((gate_ref, up_ref)):
                copies.append(
                    pltpu.make_async_copy(
                        ref.at[:, pl.ds(begin, piece)],
                        pack_ref.at[j, pl.ds(i * units, units), :],
                        sems.at[len(copies)],
                    )
                )
        begin = pl.multiple_of(other * out_width, LANES)
        copies.append(
            pltpu.make_async_copy(down_ref.at[:, pl.ds(begin, out_width)], half_ref, sems.at[len(copies)])
        )
        for copy in copies:
            copy.start()
        for copy in copies:
            copy.wait()

    anywhere = pl.BlockSpec(memory_space=pl.ANY)
    return pl.pallas_call(
        kernel,
        name="pack_weights",
        out_shape=[
            shape_of((grid.ep, 2 * units, piece), jnp.bfloat16),
            shape_of((units, out_width), jnp.bfloat16),
        ],
        in_specs=[anywhere] * 3,
        out_specs=[anywhere] * 2,
        scratch_shapes=[pltpu.SemaphoreType.DMA((2 * grid.ep + 1,))],
        compiler_params=params(),
    )(gate_t, up_t, w_down)


def gate_up(grid, piece, cols, rows, pieces, gain, gate_t, up_t, other):
    tall = pieces[0].shape[0]
    units = gate_t.shape[0]
    slot = -(-units // LANES) * LANES
    count = grid.ep
    dup = 2 * piece - cols
    per_half = count // 2

    def kernel(*refs):
        piece_refs, rest = refs[:count], refs[count:]
        gain_ref, gate_ref, up_ref, other_ref, sums_ref, home_ref, held = rest
        core = lax.axis_index("tp")
        me = lax.axis_index("ep")
        fresh = lax.broadcasted_iota(jnp.int32, (tall, piece), 1) >= core * dup
        square = jnp.zeros((tall, 1), jnp.float32)
        own_gate = jnp.zeros((tall, units), jnp.float32)
        own_up = jnp.zeros((tall, units), jnp.float32)
        far = jnp.zeros((tall, 2 * units), jnp.float32)
        for i, step in enumerate(grid.steps):
            j = grid.source(step)
            lanes = pl.ds(pl.multiple_of(j * cols + core * (cols - piece), LANES), piece)
            stream = piece_refs[i][...].astype(jnp.float32)
            held[...] = stream
            mine = held[pl.ds(pl.multiple_of(me * rows, rows), rows), :]
            side = lax.rem(j // per_half + core, 2)
            at = pl.multiple_of(lax.rem(j, per_half) * piece, LANES)
            home_ref[side, :, pl.ds(at, piece)] = mine.astype(jnp.bfloat16)
            stream = jnp.where(fresh, stream, 0.0)
            square = square + jnp.sum(stream * stream, axis=1, keepdims=True)
            scaled = (stream * gain_ref[:, lanes]).astype(jnp.bfloat16)
            own_gate = own_gate + nt_dot(scaled, gate_ref[:, lanes])
            own_up = own_up + nt_dot(scaled, up_ref[:, lanes])
            far = far + nt_dot(scaled, other_ref[j])
        sums_ref[0, :, :units] = own_gate
        sums_ref[1, :, :units] = own_up
        sums_ref[2, :, :units] = far[:, :units]
        sums_ref[3, :, :units] = far[:, units:]
        sums_ref[4] = jnp.broadcast_to(square, (tall, slot))

    return pl.pallas_call(
        kernel,
        name="gate_up",
        out_shape=[
            shape_of((5, tall, slot), jnp.float32),
            shape_of((2, rows, per_half * piece), jnp.bfloat16),
        ],
        in_specs=[vmem()] * (count + 4),
        out_specs=[vmem()] * 2,
        scratch_shapes=[pltpu.VMEM((tall, piece), jnp.float32)],
        compiler_params=params(),
    )(*pieces, gain, gate_t, up_t, other)


def down(grid, rows, sums, far_sums, weight, w_down, far_down):
    tall = weight.shape[0]
    units, width = w_down.shape
    out_width = width // 2
    count = grid.ep

    def kernel(sums_ref, far_ref, weight_ref, down_ref, far_down_ref, *rest):
        out_refs, total, down_half, sem = rest[:count], rest[count], rest[count + 1], rest[count + 2]
        begin = pl.multiple_of(lax.axis_index("tp") * out_width, LANES)
        copy = pltpu.make_async_copy(down_ref.at[:, pl.ds(begin, out_width)], down_half, sem)
        copy.start()
        square = sums_ref[4][:, :1] + far_ref[4][:, :1]
        scale = lax.rsqrt(square / width + 1e-06)

        def hidden(a, b):
            gate = (sums_ref[a][:, :units] + far_ref[b][:, :units]) * scale
            up = (sums_ref[a + 1][:, :units] + far_ref[b + 1][:, :units]) * scale
            return (gate / (1.0 + jnp.exp(-gate)) * up).astype(jnp.bfloat16)

        near, far = hidden(0, 2), hidden(2, 0)
        copy.wait()
        value = jnp.dot(near, down_half[...], preferred_element_type=jnp.float32)
        value = value + jnp.dot(far, far_down_ref[...], preferred_element_type=jnp.float32)
        total[...] = value * weight_ref[:, :1]
        for i, step in enumerate(grid.steps):
            there = pl.ds(pl.multiple_of(grid.target(step) * rows, rows), rows)
            out_refs[i][...] = total[there, :].astype(out_refs[i].dtype)

    return pl.pallas_call(
        kernel,
        name="down",
        out_shape=[
            shape_of((rows, out_width), jnp.bfloat16 if i else jnp.float32) for i in range(count)
        ],
        in_specs=[vmem()] * 3 + [pl.BlockSpec(memory_space=pl.ANY), vmem()],
        out_specs=[vmem()] * count,
        scratch_shapes=[
            pltpu.VMEM((tall, out_width), jnp.float32),
            pltpu.VMEM((units, out_width), jnp.bfloat16),
            pltpu.SemaphoreType.DMA(()),
        ],
        compiler_params=params(),
    )(sums, far_sums, weight, w_down, far_down)


def finish(piece, cols, near, far, parts):
    rows, out_width = parts[0].shape
    dup = 2 * piece - cols

    def kernel(near_ref, far_ref, *rest):
        part_refs, out_ref = rest[:-1], rest[-1]
        first = lax.axis_index("tp") == 0
        for c in range(out_width // cols):
            span = slice(c * piece, (c + 1) * piece)
            a = near_ref[:, span].astype(jnp.float32)
            b = far_ref[:, span].astype(jnp.float32)
            low = jnp.where(first, a, b)
            high = jnp.where(first, b, a)[:, dup:]
            value = jnp.concatenate([low, high], axis=1)
            for ref in part_refs:
                value = value + ref[:, c * cols : (c + 1) * cols].astype(jnp.float32)
            out_ref[:, c * cols : (c + 1) * cols] = value.astype(jnp.bfloat16)

    return pl.pallas_call(
        kernel,
        name="finish",
        out_shape=shape_of((rows, out_width), jnp.bfloat16),
        in_specs=[vmem()] * (2 + len(parts)),
        out_specs=vmem(),
        compiler_params=params(),
    )(near, far, *parts)


def tuned_body(
    grid,
    residual,
    queries,
    new_kv,
    cache,
    lengths,
    w_out,
    gain,
    route_ids,
    route_weights,
    w_gate,
    w_up,
    w_down,
):
    rows, width = residual.shape
    cols = w_out.shape[1]
    piece = -(-cols // (2 * LANES)) * LANES
    first, second, messages = attention(
        grid, piece, cols, queries, new_kv, cache, lengths, residual, route_ids, route_weights
    )
    first_chunks = grid.spread(first)
    second_chunks = grid.spread(second)
    arrived = [grid.send(m, s, u) if s or u else m for m, (s, u) in zip(messages, grid.steps)]
    gate_t, up_t = w_gate.T, w_up.T
    late = lax.optimization_barrier((gate_t, up_t, w_down, first))
    packed, down_half = pack_weights(grid, piece, cols, *late[:3])
    far_weights, far_down = swap(packed), swap(down_half)
    before = project(grid, piece, 0, first_chunks, w_out)
    ours, theirs, weight = project(grid, piece, 1, second_chunks, w_out, before, arrived)
    stream = (ours + swap(theirs)).astype(jnp.bfloat16)
    pieces = grid.spread(stream)
    sums, home = gate_up(
        grid, piece, cols, rows, pieces, gain.reshape(1, width), gate_t, up_t, far_weights
    )
    far_home = swap(home[1])
    parts = down(grid, rows, sums, swap(sums), weight, w_down, far_down)
    shares = [grid.send(p, s, u) if s or u else p for p, (s, u) in zip(parts, grid.steps)]
    return finish(piece, cols, home[0], far_home, shares)


def general_body(
    residual,
    queries,
    new_kv,
    cache,
    lengths,
    w_out,
    gain,
    route_ids,
    route_weights,
    w_gate,
    w_up,
    w_down,
):
    row_count = queries.shape[0]
    head_count = queries.shape[1] // HD
    scaling = HD ** (-0.5)
    query_heads = queries.reshape(row_count, head_count, HD)
    key_rows = cache[:, :, :HD]
    value_rows = cache[:, :, HD:]
    scores = (
        jnp.einsum("rhd,rpd->rhp", query_heads, key_rows, preferred_element_type=jnp.float32)
        * scaling
    )
    usable = jnp.arange(cache.shape[1], dtype=jnp.int32)[None, :] < lengths[:, None]
    scores = jnp.where(usable[:, None, :], scores, -jnp.inf)
    own_score = (
        jnp.einsum("rhd,rd->rh", query_heads, new_kv[:, :HD], preferred_element_type=jnp.float32)
        * scaling
    )
    peak_score = jnp.maximum(jnp.max(scores, axis=2), own_score)
    cache_weight = jnp.exp(scores - peak_score[:, :, None])
    own_weight = jnp.exp(own_score - peak_score)
    denominator = jnp.sum(cache_weight, axis=2) + own_weight
    probabilities = (cache_weight / denominator[:, :, None]).astype(jnp.bfloat16)
    own_prob = (own_weight / denominator).astype(jnp.bfloat16)
    context = jnp.einsum(
        "rhp,rpd->rhd", probabilities, value_rows, preferred_element_type=jnp.float32
    )
    context = context + own_prob.astype(jnp.float32)[:, :, None] * new_kv[:, None, HD:].astype(
        jnp.float32
    )
    context = context.astype(jnp.bfloat16).reshape(row_count, head_count * HD)
    attn_cols = jnp.dot(
        lax.all_gather(context, "ep", axis=0, tiled=True), w_out, preferred_element_type=jnp.float32
    )
    attn_rows = lax.all_to_all(attn_cols, "ep", split_axis=0, concat_axis=1, tiled=True)
    attention = lax.psum(attn_rows, "tp")
    stream = residual.astype(jnp.float32) + attention
    mean_square = jnp.mean(stream * stream, axis=1, keepdims=True)
    normed = (stream * lax.rsqrt(mean_square + 1e-06) * gain[None, :]).astype(jnp.bfloat16)
    width = normed.shape[1]
    ep_size = lax.axis_size("ep")
    members = ep_size // EXPERTS
    slot_count = EXPERTS * CAP
    flat_ids = route_ids.reshape(-1)
    one_hot = (flat_ids[:, None] == jnp.arange(EXPERTS, dtype=jnp.int32)[None, :]).astype(jnp.int32)
    earlier = jnp.cumsum(one_hot, axis=0) - one_hot
    slot_index = jnp.sum(earlier * one_hot, axis=1)
    target = (flat_ids * CAP + slot_index).reshape(row_count, TOPK)
    placed = (target[:, :, None] == jnp.arange(slot_count, dtype=jnp.int32)[None, None, :]).astype(
        jnp.float32
    )
    chosen = jnp.sum(placed, axis=1).reshape(row_count, EXPERTS, CAP).astype(jnp.bfloat16)
    mixing = jnp.sum(placed * route_weights[:, :, None], axis=1).reshape(row_count, EXPERTS, CAP)
    outgoing = jnp.einsum("rec,rd->ecd", chosen, normed, preferred_element_type=jnp.float32).astype(
        jnp.bfloat16
    )
    outgoing = jnp.broadcast_to(outgoing[:, None], (EXPERTS, members, CAP, width)).reshape(
        ep_size * CAP, width
    )
    arrived = lax.all_to_all(outgoing, "ep", split_axis=0, concat_axis=0, tiled=True)
    gate_act = jnp.dot(arrived, w_gate, preferred_element_type=jnp.float32)
    up_act = jnp.dot(arrived, w_up, preferred_element_type=jnp.float32)
    hidden = (jax.nn.silu(gate_act) * up_act).astype(jnp.bfloat16)
    partial_value = jnp.dot(hidden, w_down, preferred_element_type=jnp.float32)
    halves = lax.psum_scatter(partial_value, "tp", scatter_dimension=1, tiled=True)
    returned = lax.all_to_all(halves, "ep", split_axis=0, concat_axis=0, tiled=True)
    returned = returned.reshape(EXPERTS, members, CAP, returned.shape[1])
    mixed = jnp.einsum("rec,egcw->rw", mixing, returned, precision=lax.Precision.HIGHEST)
    tp_start = lax.axis_index("tp") * mixed.shape[1]
    stream_part = lax.dynamic_slice_in_dim(stream, tp_start, mixed.shape[1], 1)
    return (stream_part + mixed).astype(jnp.bfloat16)


def body(*args):
    ep_size, cols, heads_width = lax.axis_size("ep"), args[5].shape[1], args[5].shape[0]
    if ep_size == 8 and lax.axis_size("tp") == 2 and cols % LANES == 0 and heads_width % (8 * HD) == 0:
        return tuned_body(Grid(ep_size, 2), *args)
    return general_body(*args)


def solution(mesh):
    placed = (
        P(("grp", "ep"), None),
        P(("grp", "ep"), "tp"),
        P(("grp", "ep"), None),
        P(("grp", "ep"), None, None),
        P(("grp", "ep")),
        P("tp", "ep"),
        P(),
        P(("grp", "ep"), None),
        P(("grp", "ep"), None),
        P(None, ("ep", "tp")),
        P(None, ("ep", "tp")),
        P(("ep", "tp"), None),
    )
    return jax.shard_map(
        body, mesh=mesh, in_specs=placed, out_specs=P(("grp", "ep"), "tp"), check_vma=False
    )
```

```python
import functools

import jax
import jax.numpy as jnp
from jax import lax
from jax.experimental import pallas as pl
from jax.experimental.pallas import tpu as pltpu
from jax.sharding import PartitionSpec as P

HD = 256
TOPK = 3
EXPERTS = 4
CAP = 8
LANES = 128


def params(mebibytes):
    return pltpu.CompilerParams(vmem_limit_bytes=mebibytes * 1024 * 1024)


def vmem():
    return pl.BlockSpec(memory_space=pltpu.VMEM)


def anywhere():
    return pl.BlockSpec(memory_space=pl.ANY)


def shape_of(shape, dtype):
    return jax.ShapeDtypeStruct(shape, dtype)


class Grid:
    def __init__(self, ep_size, x_size):
        self.ep, self.x, self.z = ep_size, x_size, ep_size // x_size
        self.steps = [(s, u) for s in range(self.z) for u in range(x_size)]

    def send(self, arr, s, u):
        pairs = [
            (z * self.x + x, (z + s) % self.z * self.x + (x + u) % self.x)
            for z in range(self.z)
            for x in range(self.x)
        ]
        return lax.ppermute(arr, "ep", pairs)

    def spread(self, own):
        got = {(0, 0): own[0]}
        for s in range(1, self.z):
            got[s, 0] = self.send(own[s], s, 0)
        for s in range(self.z):
            for u in range(1, self.x):
                got[s, u] = self.send(got[s, 0], 0, u)
        return [got[step] for step in self.steps]

    def source(self, step):
        me = lax.axis_index("ep")
        z = lax.rem(me // self.x - step[0] + self.z, self.z)
        return z * self.x + lax.rem(lax.rem(me, self.x) - step[1] + self.x, self.x)

    def target(self, step):
        return self.source((-step[0] % self.z, -step[1] % self.x))


def swap(arr):
    return lax.ppermute(arr, "tp", [(0, 1), (1, 0)])


def nt_dot(a, b):
    return lax.dot_general(a, b, (((1,), (1,)), ((), ())), preferred_element_type=jnp.float32)


def in_hbm():
    return pl.BlockSpec(memory_space=pltpu.HBM)


def attention(
    grid,
    piece,
    cols,
    queries,
    new_kv,
    cache,
    lengths,
    residual,
    route_ids,
    route_weights,
    gate_t,
    up_t,
    w_down,
):
    rows, width = queries.shape
    heads = width // HD
    ctx = cache.shape[1]
    tall = rows * heads
    note = piece + LANES
    scaling = HD ** (-0.5)
    units, features = gate_t.shape
    out_width = features // 2
    down_blocks = out_width // piece
    packed_rows = (2 * grid.ep + down_blocks) * units

    def kernel(*refs):
        sources, rest = refs[:7], refs[7:]
        gate_ref, up_ref, down_ref, rest = rest[0], rest[1], rest[2], rest[3:]
        out_refs, pack_ref, rest = rest[: grid.z], rest[grid.z], rest[grid.z + 1 :]
        q_ref, kv_ref, res_ref, ids_ref, wts_ref, len_ref, kept, score, sems, row_sems, pack_sems = rest
        cache_ref = sources[6]
        copies = [
            pltpu.make_async_copy(src, dst, sems.at[i])
            for i, (src, dst) in enumerate(
                zip(sources[:6], (q_ref, kv_ref, res_ref, ids_ref, wts_ref, len_ref))
            )
        ]
        row_copies = [
            pltpu.make_async_copy(cache_ref.at[r], kept.at[r], row_sems.at[r]) for r in range(rows)
        ]
        other = 1 - lax.axis_index("tp")
        blocks = []
        for j in range(grid.ep):
            begin = pl.multiple_of(j * cols + other * (cols - piece), LANES)
            blocks += [ref.at[:, pl.ds(begin, piece)] for ref in (gate_ref, up_ref)]
        for b in range(down_blocks):
            begin = pl.multiple_of(other * out_width + b * piece, LANES)
            blocks.append(down_ref.at[:, pl.ds(begin, piece)])
        packs = [
            pltpu.make_async_copy(block, pack_ref.at[pl.ds(i * units, units), :], pack_sems.at[i])
            for i, block in enumerate(blocks)
        ]
        for copy in copies[:2] + row_copies + copies[2:] + packs:
            copy.start()

        copies[0].wait()
        copies[1].wait()
        q = q_ref[...].astype(jnp.float32)
        stacked = jnp.concatenate([q[:, h * HD : (h + 1) * HD] for h in range(heads)], axis=0)
        narrow = stacked.astype(jnp.bfloat16)
        new_kv_f = kv_ref[...].astype(jnp.float32)
        new_k = jnp.concatenate([new_kv_f[:, :HD]] * heads, axis=0)
        new_v = jnp.concatenate([new_kv_f[:, HD:]] * heads, axis=0)
        own = jnp.sum(stacked * new_k, axis=1, keepdims=True) * scaling
        row_of = lax.rem(lax.broadcasted_iota(jnp.int32, (tall, 1), 0), rows)
        row_wide = lax.rem(lax.broadcasted_iota(jnp.int32, (tall, ctx), 0), rows)
        for r in range(rows):
            row_copies[r].wait()
            part = nt_dot(narrow, kept[r, :, :HD])
            score[...] = jnp.where(row_wide == r, part, score[...]) if r else part

        for copy in copies[2:]:
            copy.wait()
        lane = lax.broadcasted_iota(jnp.int32, (rows, LANES), 1)
        square = (rows, rows)
        diagonal = lax.broadcasted_iota(jnp.int32, square, 0) == lax.broadcasted_iota(jnp.int32, square, 1)
        skip = lax.axis_index("tp") * (cols - piece)
        for s, u in grid.steps:
            to = grid.target((s, u))
            begin = pl.multiple_of(to * cols + skip, LANES)
            at = width + u * note
            out_refs[s][:, at : at + piece] = res_ref[:, pl.ds(begin, piece)]
            chosen = ids_ref[...] == to * EXPERTS // grid.ep
            across = jnp.sum(jnp.where(chosen, wts_ref[...], 0.0), axis=0, keepdims=True)
            weight = jnp.sum(
                jnp.where(diagonal, jnp.broadcast_to(across, square), 0.0), axis=1, keepdims=True
            )
            high = weight.astype(jnp.bfloat16).astype(jnp.float32)
            middle = (weight - high).astype(jnp.bfloat16).astype(jnp.float32)
            low = weight - high - middle
            tile = jnp.where(lane == 0, high, 0.0)
            tile = jnp.where(lane == 1, middle, tile)
            tile = jnp.where(lane == 2, low, tile)
            out_refs[s][:, at + piece : at + note] = tile.astype(jnp.bfloat16)

        length = jnp.zeros((tall, 1), jnp.int32)
        for r in range(rows):
            length = jnp.where(row_of == r, len_ref[r], length)
        place = lax.broadcasted_iota(jnp.int32, (tall, ctx), 1)
        scores = jnp.where(place < length, score[...] * scaling, -jnp.inf)
        peak = jnp.maximum(jnp.max(scores, axis=1, keepdims=True), own)
        exps = jnp.exp(scores - peak)
        own_exp = jnp.exp(own - peak)
        denominator = jnp.sum(exps, axis=1, keepdims=True) + own_exp
        prob = exps / denominator
        own_prob = (own_exp / denominator).astype(jnp.bfloat16).astype(jnp.float32)
        total = own_prob * new_v
        for r in range(rows):
            only = jnp.where(row_wide == r, prob, 0.0).astype(jnp.bfloat16)
            total = total + jnp.dot(only, kept[r, :, HD:], preferred_element_type=jnp.float32)
        for h in range(heads):
            value = total[h * rows : (h + 1) * rows].astype(jnp.bfloat16)
            for ref in out_refs:
                ref[:, h * HD : (h + 1) * HD] = value
        for copy in packs:
            copy.wait()

    return pl.pallas_call(
        kernel,
        name="attention",
        out_shape=[shape_of((rows, width + grid.x * note), jnp.bfloat16)] * grid.z
        + [shape_of((packed_rows, piece), jnp.bfloat16)],
        in_specs=[in_hbm()] * 10,
        out_specs=[vmem()] * grid.z + [in_hbm()],
        scratch_shapes=[
            pltpu.VMEM(queries.shape, jnp.bfloat16),
            pltpu.VMEM(new_kv.shape, jnp.bfloat16),
            pltpu.VMEM(residual.shape, jnp.bfloat16),
            pltpu.VMEM(route_ids.shape, jnp.int32),
            pltpu.VMEM(route_weights.shape, jnp.float32),
            pltpu.SMEM(lengths.shape, jnp.int32),
            pltpu.VMEM(cache.shape, jnp.bfloat16),
            pltpu.VMEM((tall, ctx), jnp.float32),
            pltpu.SemaphoreType.DMA((6,)),
            pltpu.SemaphoreType.DMA((rows,)),
            pltpu.SemaphoreType.DMA((2 * grid.ep + down_blocks,)),
        ],
        compiler_params=params(60),
    )(
        queries,
        new_kv,
        residual,
        route_ids,
        route_weights,
        lengths,
        cache,
        gate_t,
        up_t,
        w_down,
    )


def project(grid, piece, chunks, w_out):
    rows = chunks[0].shape[0]
    depth, cols = w_out.shape
    count = len(chunks)
    tall = rows * count
    blocks = 8
    block = depth // blocks
    note = piece + LANES

    def kernel(*refs):
        chunk_refs, rest = refs[:count], refs[count:]
        w_ref, ours_ref, theirs_ref, weight_ref, stacked, total = rest
        k = pl.program_id(0)

        @pl.when(k == 0)
        def _():
            both = jnp.concatenate([ref[:, :depth] for ref in chunk_refs], axis=0)
            for i in range(blocks):
                stacked[i] = both[:, i * block : (i + 1) * block]

        product = jnp.dot(stacked[k], w_ref[...], preferred_element_type=jnp.float32)

        @pl.when(k == 0)
        def _():
            total[...] = product

        @pl.when(k > 0)
        def _():
            total[...] += product

        @pl.when(k == blocks - 1)
        def _():
            core = lax.axis_index("tp")
            mine = pl.multiple_of(core * (cols - piece), LANES)
            other = pl.multiple_of((1 - core) * (cols - piece), LANES)
            for i, (s, u) in enumerate(grid.steps):
                here = pl.ds(pl.multiple_of(grid.source((s, u)) * rows, rows), rows)
                at = depth + u * note
                beside = chunk_refs[i][:, at : at + note].astype(jnp.float32)
                block_rows = slice(i * rows, (i + 1) * rows)
                ours_ref[here, :] = total[block_rows, pl.ds(mine, piece)] + beside[:, :piece]
                theirs_ref[here, :] = total[block_rows, pl.ds(other, piece)]
                weight_ref[here, :] = jnp.broadcast_to(
                    jnp.sum(beside[:, piece:], axis=1, keepdims=True), (rows, LANES)
                )

    def whole(arr):
        return pl.BlockSpec(arr.shape, lambda k: (0, 0))

    outs = [shape_of((tall, piece), jnp.float32)] * 2 + [shape_of((tall, LANES), jnp.float32)]
    return pl.pallas_call(
        kernel,
        name="project",
        grid=(blocks,),
        out_shape=outs,
        in_specs=[whole(c) for c in chunks] + [pl.BlockSpec((block, cols), lambda k: (k, 0))],
        out_specs=[whole(o) for o in outs],
        scratch_shapes=[
            pltpu.VMEM((blocks, tall, block), jnp.bfloat16),
            pltpu.VMEM((tall, cols), jnp.float32),
        ],
        cost_estimate=pl.CostEstimate(
            flops=2 * tall * depth * cols,
            bytes_accessed=2 * depth * cols + 2 * tall * depth + 8 * tall * piece,
            transcendentals=0,
        ),
        compiler_params=params(48),
    )(*chunks, w_out)


def gate_up(grid, piece, cols, rows, pieces, gain, gate_t, up_t, other):
    tall = pieces[0].shape[0]
    units = gate_t.shape[0]
    count = grid.ep
    dup = 2 * piece - cols
    per_half = count // 2
    sums_width = 4 * units + LANES
    extra = -(-per_half * piece // sums_width)

    def kernel(*refs):
        piece_refs, rest = refs[:count], refs[count:]
        gain_ref, gate_ref, up_ref, other_ref, sums_ref, home_ref, held, home = rest
        home[1] = jnp.zeros((rows, extra * sums_width), jnp.float32)
        core = lax.axis_index("tp")
        me = lax.axis_index("ep")
        fresh = lax.broadcasted_iota(jnp.int32, (tall, piece), 1) >= core * dup
        square = jnp.zeros((tall, 1), jnp.float32)
        own_gate = jnp.zeros((units, tall), jnp.float32)
        own_up = jnp.zeros((units, tall), jnp.float32)
        far = jnp.zeros((2 * units, tall), jnp.float32)
        for i, step in enumerate(grid.steps):
            j = grid.source(step)
            lanes = pl.ds(pl.multiple_of(j * cols + core * (cols - piece), LANES), piece)
            stream = piece_refs[i][...].astype(jnp.float32)
            held[...] = stream
            mine = held[pl.ds(pl.multiple_of(me * rows, rows), rows), :]
            side = lax.rem(j // per_half + core, 2)
            at = pl.multiple_of(lax.rem(j, per_half) * piece, LANES)
            home[side, :, pl.ds(at, piece)] = mine
            stream = jnp.where(fresh, stream, 0.0)
            square = square + jnp.sum(stream * stream, axis=1, keepdims=True)
            scaled = (stream * gain_ref[:, lanes]).astype(jnp.bfloat16)
            own_gate = own_gate + nt_dot(gate_ref[:, lanes], scaled)
            own_up = own_up + nt_dot(up_ref[:, lanes], scaled)
            block = pl.ds(pl.multiple_of(j * 2 * units, 2 * units), 2 * units)
            far = far + nt_dot(other_ref[block, :], scaled)
        sums_ref[:tall, : 4 * units] = jnp.concatenate([own_gate, own_up, far], axis=0).T
        sums_ref[:tall, 4 * units :] = jnp.broadcast_to(square, (tall, LANES))
        for b in range(extra):
            at = tall + b * rows
            sums_ref[at : at + rows, :] = home[1, :, b * sums_width : (b + 1) * sums_width]
        home_ref[...] = home[0, :, : per_half * piece]

    return pl.pallas_call(
        kernel,
        name="gate_up",
        out_shape=[
            shape_of((tall + extra * rows, sums_width), jnp.float32),
            shape_of((rows, per_half * piece), jnp.float32),
        ],
        in_specs=[vmem()] * (count + 4),
        out_specs=[vmem()] * 2,
        scratch_shapes=[
            pltpu.VMEM((tall, piece), jnp.float32),
            pltpu.VMEM((2, rows, extra * sums_width), jnp.float32),
        ],
        compiler_params=params(8),
    )(*pieces, gain, gate_t, up_t, other)


def down(grid, piece, rows, sums, far_sums, weight, w_down, far_weights):
    tall = weight.shape[0]
    units, width = w_down.shape
    out_width = width // 2
    count = grid.ep

    def kernel(sums_ref, far_ref, weight_ref, down_ref, packed_ref, *rest):
        out_refs, total, down_half, sem = rest[:count], rest[count], rest[count + 1], rest[count + 2]
        begin = pl.multiple_of(lax.axis_index("tp") * out_width, LANES)
        copy = pltpu.make_async_copy(down_ref.at[:, pl.ds(begin, out_width)], down_half, sem)
        copy.start()
        square = (
            sums_ref[:tall, 4 * units : 4 * units + 1] + far_ref[:tall, 4 * units : 4 * units + 1]
        )
        scale = lax.rsqrt(square / width + 1e-06)

        def hidden(a, b):
            both = (
                sums_ref[:tall, a * units : (a + 2) * units]
                + far_ref[:tall, b * units : (b + 2) * units]
            )
            gate, up = both[:, :units] * scale, both[:, units:] * scale
            return (gate / (1.0 + jnp.exp(-gate)) * up).astype(jnp.bfloat16)

        near, far = hidden(0, 2), hidden(2, 0)
        copy.wait()
        for b in range(out_width // piece):
            span = slice(b * piece, (b + 1) * piece)
            block = slice((2 * count + b) * units, (2 * count + b + 1) * units)
            value = jnp.dot(near, down_half[:, span], preferred_element_type=jnp.float32)
            value = value + jnp.dot(far, packed_ref[block, :], preferred_element_type=jnp.float32)
            total[:, span] = value * weight_ref[:, :1]
        for i, step in enumerate(grid.steps):
            there = pl.ds(pl.multiple_of(grid.target(step) * rows, rows), rows)
            out_refs[i][...] = total[there, :].astype(out_refs[i].dtype)

    return pl.pallas_call(
        kernel,
        name="down",
        out_shape=[
            shape_of((rows, out_width), jnp.bfloat16 if i else jnp.float32) for i in range(count)
        ],
        in_specs=[vmem()] * 3 + [pl.BlockSpec(memory_space=pl.ANY), vmem()],
        out_specs=[vmem()] * count,
        scratch_shapes=[
            pltpu.VMEM((tall, out_width), jnp.float32),
            pltpu.VMEM((units, out_width), jnp.bfloat16),
            pltpu.SemaphoreType.DMA(()),
        ],
        compiler_params=params(8),
    )(sums, far_sums, weight, w_down, far_weights)


def finish(piece, cols, near, far_sums, parts):
    rows, out_width = parts[0].shape
    extra = -(-near.shape[1] // far_sums.shape[1])
    top = far_sums.shape[0] - extra * rows
    dup = 2 * piece - cols

    def kernel(near_ref, far_ref, *rest):
        part_refs, out_ref = rest[:-1], rest[-1]
        first = lax.axis_index("tp") == 0
        far = jnp.concatenate(
            [far_ref[top + b * rows : top + (b + 1) * rows, :] for b in range(extra)], axis=1
        )
        for c in range(out_width // cols):
            span = slice(c * piece, (c + 1) * piece)
            a, b = near_ref[:, span], far[:, span]
            low = jnp.where(first, a, b)
            high = jnp.where(first, b, a)[:, dup:]
            value = jnp.concatenate([low, high], axis=1)
            for ref in part_refs:
                value = value + ref[:, c * cols : (c + 1) * cols].astype(jnp.float32)
            out_ref[:, c * cols : (c + 1) * cols] = value.astype(jnp.bfloat16)

    return pl.pallas_call(
        kernel,
        name="finish",
        out_shape=shape_of((rows, out_width), jnp.bfloat16),
        in_specs=[vmem()] * (2 + len(parts)),
        out_specs=vmem(),
        compiler_params=params(4),
    )(near, far_sums, *parts)


def tuned_body(
    grid,
    residual,
    queries,
    new_kv,
    cache,
    lengths,
    w_out,
    gain,
    route_ids,
    route_weights,
    w_gate,
    w_up,
    w_down,
):
    rows, width = residual.shape
    cols = w_out.shape[1]
    piece = -(-cols // (2 * LANES)) * LANES
    gate_t, up_t = w_gate.T, w_up.T
    *outgoing, packed = attention(
        grid,
        piece,
        cols,
        queries,
        new_kv,
        cache,
        lengths,
        residual,
        route_ids.T,
        route_weights.T,
        gate_t,
        up_t,
        w_down,
    )
    chunks = grid.spread(outgoing)
    packed, *_ = lax.optimization_barrier((packed, *chunks))
    far_weights = swap(packed)
    ours, theirs, weight = project(grid, piece, chunks, w_out)
    stream = (ours + swap(theirs)).astype(jnp.bfloat16)
    stream, far_weights = lax.optimization_barrier((stream, far_weights))
    pieces = grid.spread([stream] * grid.z)
    sums, home = gate_up(
        grid, piece, cols, rows, pieces, gain.reshape(1, width), gate_t, up_t, far_weights
    )
    far_sums = swap(sums)
    parts = down(grid, piece, rows, sums, far_sums, weight, w_down, far_weights)
    shares = [grid.send(p, s, u) if s or u else p for p, (s, u) in zip(parts, grid.steps)]
    return finish(piece, cols, home, far_sums, shares)


def general_body(
    residual,
    queries,
    new_kv,
    cache,
    lengths,
    w_out,
    gain,
    route_ids,
    route_weights,
    w_gate,
    w_up,
    w_down,
):
    row_count = queries.shape[0]
    head_count = queries.shape[1] // HD
    scaling = HD ** (-0.5)
    query_heads = queries.reshape(row_count, head_count, HD)
    key_rows = cache[:, :, :HD]
    value_rows = cache[:, :, HD:]
    scores = (
        jnp.einsum("rhd,rpd->rhp", query_heads, key_rows, preferred_element_type=jnp.float32)
        * scaling
    )
    usable = jnp.arange(cache.shape[1], dtype=jnp.int32)[None, :] < lengths[:, None]
    scores = jnp.where(usable[:, None, :], scores, -jnp.inf)
    own_score = (
        jnp.einsum("rhd,rd->rh", query_heads, new_kv[:, :HD], preferred_element_type=jnp.float32)
        * scaling
    )
    peak_score = jnp.maximum(jnp.max(scores, axis=2), own_score)
    cache_weight = jnp.exp(scores - peak_score[:, :, None])
    own_weight = jnp.exp(own_score - peak_score)
    denominator = jnp.sum(cache_weight, axis=2) + own_weight
    probabilities = (cache_weight / denominator[:, :, None]).astype(jnp.bfloat16)
    own_prob = (own_weight / denominator).astype(jnp.bfloat16)
    context = jnp.einsum(
        "rhp,rpd->rhd", probabilities, value_rows, preferred_element_type=jnp.float32
    )
    context = context + own_prob.astype(jnp.float32)[:, :, None] * new_kv[:, None, HD:].astype(
        jnp.float32
    )
    context = context.astype(jnp.bfloat16).reshape(row_count, head_count * HD)
    attn_cols = jnp.dot(
        lax.all_gather(context, "ep", axis=0, tiled=True), w_out, preferred_element_type=jnp.float32
    )
    attn_rows = lax.all_to_all(attn_cols, "ep", split_axis=0, concat_axis=1, tiled=True)
    attention = lax.psum(attn_rows, "tp")
    stream = residual.astype(jnp.float32) + attention
    mean_square = jnp.mean(stream * stream, axis=1, keepdims=True)
    normed = (stream * lax.rsqrt(mean_square + 1e-06) * gain[None, :]).astype(jnp.bfloat16)
    width = normed.shape[1]
    ep_size = lax.axis_size("ep")
    members = ep_size // EXPERTS
    slot_count = EXPERTS * CAP
    flat_ids = route_ids.reshape(-1)
    one_hot = (flat_ids[:, None] == jnp.arange(EXPERTS, dtype=jnp.int32)[None, :]).astype(jnp.int32)
    earlier = jnp.cumsum(one_hot, axis=0) - one_hot
    slot_index = jnp.sum(earlier * one_hot, axis=1)
    target = (flat_ids * CAP + slot_index).reshape(row_count, TOPK)
    placed = (target[:, :, None] == jnp.arange(slot_count, dtype=jnp.int32)[None, None, :]).astype(
        jnp.float32
    )
    chosen = jnp.sum(placed, axis=1).reshape(row_count, EXPERTS, CAP).astype(jnp.bfloat16)
    mixing = jnp.sum(placed * route_weights[:, :, None], axis=1).reshape(row_count, EXPERTS, CAP)
    outgoing = jnp.einsum("rec,rd->ecd", chosen, normed, preferred_element_type=jnp.float32).astype(
        jnp.bfloat16
    )
    outgoing = jnp.broadcast_to(outgoing[:, None], (EXPERTS, members, CAP, width)).reshape(
        ep_size * CAP, width
    )
    arrived = lax.all_to_all(outgoing, "ep", split_axis=0, concat_axis=0, tiled=True)
    gate_act = jnp.dot(arrived, w_gate, preferred_element_type=jnp.float32)
    up_act = jnp.dot(arrived, w_up, preferred_element_type=jnp.float32)
    hidden = (jax.nn.silu(gate_act) * up_act).astype(jnp.bfloat16)
    partial_value = jnp.dot(hidden, w_down, preferred_element_type=jnp.float32)
    halves = lax.psum_scatter(partial_value, "tp", scatter_dimension=1, tiled=True)
    returned = lax.all_to_all(halves, "ep", split_axis=0, concat_axis=0, tiled=True)
    returned = returned.reshape(EXPERTS, members, CAP, returned.shape[1])
    mixed = jnp.einsum("rec,egcw->rw", mixing, returned, precision=lax.Precision.HIGHEST)
    tp_start = lax.axis_index("tp") * mixed.shape[1]
    stream_part = lax.dynamic_slice_in_dim(stream, tp_start, mixed.shape[1], 1)
    return (stream_part + mixed).astype(jnp.bfloat16)


def body(*args):
    ep_size, cols, heads_width = lax.axis_size("ep"), args[5].shape[1], args[5].shape[0]
    if ep_size == 8 and lax.axis_size("tp") == 2 and cols % LANES == 0 and heads_width % (8 * HD) == 0:
        return tuned_body(Grid(ep_size, 2), *args)
    return general_body(*args)


def solution(mesh):
    placed = (
        P(("grp", "ep"), None),
        P(("grp", "ep"), "tp"),
        P(("grp", "ep"), None),
        P(("grp", "ep"), None, None),
        P(("grp", "ep")),
        P("tp", "ep"),
        P(),
        P(("grp", "ep"), None),
        P(("grp", "ep"), None),
        P(None, ("ep", "tp")),
        P(None, ("ep", "tp")),
        P(("ep", "tp"), None),
    )
    return jax.shard_map(
        body, mesh=mesh, in_specs=placed, out_specs=P(("grp", "ep"), "tp"), check_vma=False
    )
```

```python
import functools

import jax
import jax.numpy as jnp
from jax import lax
from jax.experimental import pallas as pl
from jax.experimental.pallas import tpu as pltpu
from jax.sharding import PartitionSpec as P

HD = 256
TOPK = 3
EXPERTS = 4
CAP = 8
LANES = 128


def params(mebibytes):
    return pltpu.CompilerParams(vmem_limit_bytes=mebibytes * 1024 * 1024)


def vmem():
    return pl.BlockSpec(memory_space=pltpu.VMEM)


def anywhere():
    return pl.BlockSpec(memory_space=pl.ANY)


def shape_of(shape, dtype):
    return jax.ShapeDtypeStruct(shape, dtype)


class Grid:
    def __init__(self, ep_size, x_size):
        self.ep, self.x, self.z = ep_size, x_size, ep_size // x_size
        self.steps = [(s, u) for s in range(self.z) for u in range(x_size)]

    def send(self, arr, s, u):
        pairs = [
            (z * self.x + x, (z + s) % self.z * self.x + (x + u) % self.x)
            for z in range(self.z)
            for x in range(self.x)
        ]
        return lax.ppermute(arr, "ep", pairs)

    def spread(self, own, spaced=False):
        got = {(0, 0): own[0]}
        near_first = sorted(range(self.z), key=lambda s: min(s, self.z - s))
        for s in near_first:
            block = own[s]
            if spaced and min(s, self.z - s) > 1:
                block, *_ = lax.optimization_barrier((block, got[1, 0], got[0, self.x - 1]))
            if s:
                got[s, 0] = self.send(block, s, 0)
            for u in range(1, self.x):
                got[s, u] = self.send(got[s, 0], 0, u)
        return [got[step] for step in self.steps]

    def source(self, step):
        me = lax.axis_index("ep")
        z = lax.rem(me // self.x - step[0] + self.z, self.z)
        return z * self.x + lax.rem(lax.rem(me, self.x) - step[1] + self.x, self.x)

    def target(self, step):
        return self.source((-step[0] % self.z, -step[1] % self.x))


def swap(arr):
    return lax.ppermute(arr, "tp", [(0, 1), (1, 0)])


def nt_dot(a, b):
    return lax.dot_general(a, b, (((1,), (1,)), ((), ())), preferred_element_type=jnp.float32)


def in_hbm():
    return pl.BlockSpec(memory_space=pltpu.HBM)


def attention(
    grid,
    piece,
    cols,
    queries,
    new_kv,
    cache,
    lengths,
    residual,
    route_ids,
    route_weights,
    gate_t,
    up_t,
    w_down,
):
    rows, width = queries.shape
    heads = width // HD
    ctx = cache.shape[1]
    tall = rows * heads
    note = piece + LANES
    scaling = HD ** (-0.5)
    units, features = gate_t.shape
    out_width = features // 2
    down_blocks = out_width // piece
    packed_rows = (2 * grid.ep + down_blocks) * units

    def kernel(*refs):
        sources, rest = refs[:7], refs[7:]
        gate_ref, up_ref, down_ref, rest = rest[0], rest[1], rest[2], rest[3:]
        out_refs, pack_ref, rest = rest[: grid.z], rest[grid.z], rest[grid.z + 1 :]
        q_ref, kv_ref, res_ref, ids_ref, wts_ref, len_ref, kept, score, packed, sems, row_sems, pack_sems = rest
        cache_ref = sources[6]
        copies = [
            pltpu.make_async_copy(src, dst, sems.at[i])
            for i, (src, dst) in enumerate(
                zip(sources[:6], (q_ref, kv_ref, res_ref, ids_ref, wts_ref, len_ref))
            )
        ]
        row_copies = [
            pltpu.make_async_copy(cache_ref.at[r], kept.at[r], row_sems.at[r]) for r in range(rows)
        ]
        other = 1 - lax.axis_index("tp")
        blocks = []
        for j in range(grid.ep):
            begin = pl.multiple_of(j * cols + other * (cols - piece), LANES)
            blocks += [ref.at[:, pl.ds(begin, piece)] for ref in (gate_ref, up_ref)]
        for b in range(down_blocks):
            begin = pl.multiple_of(other * out_width + b * piece, LANES)
            blocks.append(down_ref.at[:, pl.ds(begin, piece)])
        packs = [
            pltpu.make_async_copy(block, packed.at[pl.ds(i * units, units), :], pack_sems.at[i])
            for i, block in enumerate(blocks)
        ]
        pack_out = pltpu.make_async_copy(packed, pack_ref, pack_sems.at[len(blocks)])
        for copy in copies[:2] + row_copies + copies[2:] + packs:
            copy.start()

        copies[0].wait()
        copies[1].wait()
        q = q_ref[...].astype(jnp.float32)
        stacked = jnp.concatenate([q[:, h * HD : (h + 1) * HD] for h in range(heads)], axis=0)
        narrow = stacked.astype(jnp.bfloat16)
        new_kv_f = kv_ref[...].astype(jnp.float32)
        new_k = jnp.concatenate([new_kv_f[:, :HD]] * heads, axis=0)
        new_v = jnp.concatenate([new_kv_f[:, HD:]] * heads, axis=0)
        own = jnp.sum(stacked * new_k, axis=1, keepdims=True) * scaling
        row_of = lax.rem(lax.broadcasted_iota(jnp.int32, (tall, 1), 0), rows)
        row_wide = lax.rem(lax.broadcasted_iota(jnp.int32, (tall, ctx), 0), rows)
        for r in range(rows):
            row_copies[r].wait()
            part = nt_dot(narrow, kept[r, :, :HD])
            score[...] = jnp.where(row_wide == r, part, score[...]) if r else part

        for copy in copies[2:] + packs:
            copy.wait()
        pack_out.start()
        lane = lax.broadcasted_iota(jnp.int32, (rows, LANES), 1)
        square = (rows, rows)
        diagonal = lax.broadcasted_iota(jnp.int32, square, 0) == lax.broadcasted_iota(jnp.int32, square, 1)
        skip = lax.axis_index("tp") * (cols - piece)
        for s, u in grid.steps:
            to = grid.target((s, u))
            begin = pl.multiple_of(to * cols + skip, LANES)
            at = width + u * note
            out_refs[s][:, at : at + piece] = res_ref[:, pl.ds(begin, piece)]
            chosen = ids_ref[...] == to * EXPERTS // grid.ep
            across = jnp.sum(jnp.where(chosen, wts_ref[...], 0.0), axis=0, keepdims=True)
            weight = jnp.sum(
                jnp.where(diagonal, jnp.broadcast_to(across, square), 0.0), axis=1, keepdims=True
            )
            high = weight.astype(jnp.bfloat16).astype(jnp.float32)
            middle = (weight - high).astype(jnp.bfloat16).astype(jnp.float32)
            low = weight - high - middle
            tile = jnp.where(lane == 0, high, 0.0)
            tile = jnp.where(lane == 1, middle, tile)
            tile = jnp.where(lane == 2, low, tile)
            out_refs[s][:, at + piece : at + note] = tile.astype(jnp.bfloat16)

        length = jnp.zeros((tall, 1), jnp.int32)
        for r in range(rows):
            length = jnp.where(row_of == r, len_ref[r], length)
        place = lax.broadcasted_iota(jnp.int32, (tall, ctx), 1)
        scores = jnp.where(place < length, score[...] * scaling, -jnp.inf)
        peak = jnp.maximum(jnp.max(scores, axis=1, keepdims=True), own)
        exps = jnp.exp(scores - peak)
        own_exp = jnp.exp(own - peak)
        denominator = jnp.sum(exps, axis=1, keepdims=True) + own_exp
        prob = exps / denominator
        own_prob = (own_exp / denominator).astype(jnp.bfloat16).astype(jnp.float32)
        total = own_prob * new_v
        for r in range(rows):
            only = jnp.where(row_wide == r, prob, 0.0).astype(jnp.bfloat16)
            total = total + jnp.dot(only, kept[r, :, HD:], preferred_element_type=jnp.float32)
        for h in range(heads):
            value = total[h * rows : (h + 1) * rows].astype(jnp.bfloat16)
            for ref in out_refs:
                ref[:, h * HD : (h + 1) * HD] = value
        pack_out.wait()

    return pl.pallas_call(
        kernel,
        name="attention",
        out_shape=[shape_of((rows, width + grid.x * note), jnp.bfloat16)] * grid.z
        + [shape_of((packed_rows, piece), jnp.bfloat16)],
        in_specs=[in_hbm()] * 10,
        out_specs=[vmem()] * grid.z + [in_hbm()],
        scratch_shapes=[
            pltpu.VMEM(queries.shape, jnp.bfloat16),
            pltpu.VMEM(new_kv.shape, jnp.bfloat16),
            pltpu.VMEM(residual.shape, jnp.bfloat16),
            pltpu.VMEM(route_ids.shape, jnp.int32),
            pltpu.VMEM(route_weights.shape, jnp.float32),
            pltpu.SMEM(lengths.shape, jnp.int32),
            pltpu.VMEM(cache.shape, jnp.bfloat16),
            pltpu.VMEM((tall, ctx), jnp.float32),
            pltpu.VMEM((packed_rows, piece), jnp.bfloat16),
            pltpu.SemaphoreType.DMA((6,)),
            pltpu.SemaphoreType.DMA((rows,)),
            pltpu.SemaphoreType.DMA((2 * grid.ep + down_blocks + 1,)),
        ],
        compiler_params=params(60),
    )(
        queries,
        new_kv,
        residual,
        route_ids,
        route_weights,
        lengths,
        cache,
        gate_t,
        up_t,
        w_down,
    )


def project(grid, piece, chunks, w_out):
    rows = chunks[0].shape[0]
    depth, cols = w_out.shape
    count = len(chunks)
    tall = rows * count
    blocks = 8
    block = depth // blocks
    note = piece + LANES

    def kernel(*refs):
        chunk_refs, rest = refs[:count], refs[count:]
        w_ref, ours_ref, theirs_ref, weight_ref, stacked, total = rest
        k = pl.program_id(0)

        @pl.when(k == 0)
        def _():
            both = jnp.concatenate([ref[:, :depth] for ref in chunk_refs], axis=0)
            for i in range(blocks):
                stacked[i] = both[:, i * block : (i + 1) * block]

        product = jnp.dot(stacked[k], w_ref[...], preferred_element_type=jnp.float32)

        @pl.when(k == 0)
        def _():
            total[...] = product

        @pl.when(k > 0)
        def _():
            total[...] += product

        @pl.when(k == blocks - 1)
        def _():
            core = lax.axis_index("tp")
            mine = pl.multiple_of(core * (cols - piece), LANES)
            other = pl.multiple_of((1 - core) * (cols - piece), LANES)
            for i, (s, u) in enumerate(grid.steps):
                here = pl.ds(pl.multiple_of(grid.source((s, u)) * rows, rows), rows)
                at = depth + u * note
                beside = chunk_refs[i][:, at : at + note].astype(jnp.float32)
                block_rows = slice(i * rows, (i + 1) * rows)
                ours_ref[here, :] = total[block_rows, pl.ds(mine, piece)] + beside[:, :piece]
                theirs_ref[here, :] = total[block_rows, pl.ds(other, piece)]
                weight_ref[here, :] = jnp.broadcast_to(
                    jnp.sum(beside[:, piece:], axis=1, keepdims=True), (rows, LANES)
                )

    def whole(arr):
        return pl.BlockSpec(arr.shape, lambda k: (0, 0))

    outs = [shape_of((tall, piece), jnp.float32)] * 2 + [shape_of((tall, LANES), jnp.float32)]
    return pl.pallas_call(
        kernel,
        name="project",
        grid=(blocks,),
        out_shape=outs,
        in_specs=[whole(c) for c in chunks] + [pl.BlockSpec((block, cols), lambda k: (k, 0))],
        out_specs=[whole(o) for o in outs],
        scratch_shapes=[
            pltpu.VMEM((blocks, tall, block), jnp.bfloat16),
            pltpu.VMEM((tall, cols), jnp.float32),
        ],
        cost_estimate=pl.CostEstimate(
            flops=2 * tall * depth * cols,
            bytes_accessed=2 * depth * cols + 2 * tall * depth + 8 * tall * piece,
            transcendentals=0,
        ),
        compiler_params=params(48),
    )(*chunks, w_out)


def gate_up(grid, piece, cols, rows, pieces, gain, gate_t, up_t, other):
    tall = pieces[0].shape[0]
    units = gate_t.shape[0]
    count = grid.ep
    dup = 2 * piece - cols
    per_half = count // 2
    sums_width = 4 * units + LANES
    extra = -(-per_half * piece // sums_width)

    def kernel(*refs):
        piece_refs, rest = refs[:count], refs[count:]
        gain_ref, gate_ref, up_ref, other_ref, sums_ref, home_ref, held, home = rest
        home[1] = jnp.zeros((rows, extra * sums_width), jnp.float32)
        core = lax.axis_index("tp")
        me = lax.axis_index("ep")
        fresh = lax.broadcasted_iota(jnp.int32, (tall, piece), 1) >= core * dup
        square = jnp.zeros((tall, 1), jnp.float32)
        own_gate = jnp.zeros((units, tall), jnp.float32)
        own_up = jnp.zeros((units, tall), jnp.float32)
        far = jnp.zeros((2 * units, tall), jnp.float32)
        for i, step in enumerate(grid.steps):
            j = grid.source(step)
            lanes = pl.ds(pl.multiple_of(j * cols + core * (cols - piece), LANES), piece)
            stream = piece_refs[i][...].astype(jnp.float32)
            held[...] = stream
            mine = held[pl.ds(pl.multiple_of(me * rows, rows), rows), :]
            side = lax.rem(j // per_half + core, 2)
            at = pl.multiple_of(lax.rem(j, per_half) * piece, LANES)
            home[side, :, pl.ds(at, piece)] = mine
            stream = jnp.where(fresh, stream, 0.0)
            square = square + jnp.sum(stream * stream, axis=1, keepdims=True)
            scaled = (stream * gain_ref[:, lanes]).astype(jnp.bfloat16)
            own_gate = own_gate + nt_dot(gate_ref[:, lanes], scaled)
            own_up = own_up + nt_dot(up_ref[:, lanes], scaled)
            block = pl.ds(pl.multiple_of(j * 2 * units, 2 * units), 2 * units)
            far = far + nt_dot(other_ref[block, :], scaled)
        sums_ref[:tall, : 4 * units] = jnp.concatenate([own_gate, own_up, far], axis=0).T
        sums_ref[:tall, 4 * units :] = jnp.broadcast_to(square, (tall, LANES))
        for b in range(extra):
            at = tall + b * rows
            sums_ref[at : at + rows, :] = home[1, :, b * sums_width : (b + 1) * sums_width]
        home_ref[...] = home[0, :, : per_half * piece]

    return pl.pallas_call(
        kernel,
        name="gate_up",
        out_shape=[
            shape_of((tall + extra * rows, sums_width), jnp.float32),
            shape_of((rows, per_half * piece), jnp.float32),
        ],
        in_specs=[vmem()] * (count + 4),
        out_specs=[vmem()] * 2,
        scratch_shapes=[
            pltpu.VMEM((tall, piece), jnp.float32),
            pltpu.VMEM((2, rows, extra * sums_width), jnp.float32),
        ],
        compiler_params=params(8),
    )(*pieces, gain, gate_t, up_t, other)


def down(grid, piece, rows, sums, far_sums, weight, w_down, far_weights):
    tall = weight.shape[0]
    units, width = w_down.shape
    out_width = width // 2
    count = grid.ep

    def kernel(sums_ref, far_ref, weight_ref, down_ref, packed_ref, *rest):
        out_refs, total, down_half, sem = rest[:count], rest[count], rest[count + 1], rest[count + 2]
        begin = pl.multiple_of(lax.axis_index("tp") * out_width, LANES)
        copy = pltpu.make_async_copy(down_ref.at[:, pl.ds(begin, out_width)], down_half, sem)
        copy.start()
        square = (
            sums_ref[:tall, 4 * units : 4 * units + 1] + far_ref[:tall, 4 * units : 4 * units + 1]
        )
        scale = lax.rsqrt(square / width + 1e-06)

        def hidden(a, b):
            both = (
                sums_ref[:tall, a * units : (a + 2) * units]
                + far_ref[:tall, b * units : (b + 2) * units]
            )
            gate, up = both[:, :units] * scale, both[:, units:] * scale
            return (gate / (1.0 + jnp.exp(-gate)) * up).astype(jnp.bfloat16)

        near, far = hidden(0, 2), hidden(2, 0)
        copy.wait()
        for b in range(out_width // piece):
            span = slice(b * piece, (b + 1) * piece)
            block = slice((2 * count + b) * units, (2 * count + b + 1) * units)
            value = jnp.dot(near, down_half[:, span], preferred_element_type=jnp.float32)
            value = value + jnp.dot(far, packed_ref[block, :], preferred_element_type=jnp.float32)
            total[:, span] = value * weight_ref[:, :1]
        for i, step in enumerate(grid.steps):
            there = pl.ds(pl.multiple_of(grid.target(step) * rows, rows), rows)
            out_refs[i][...] = total[there, :].astype(out_refs[i].dtype)

    return pl.pallas_call(
        kernel,
        name="down",
        out_shape=[
            shape_of((rows, out_width), jnp.bfloat16 if i else jnp.float32) for i in range(count)
        ],
        in_specs=[vmem()] * 3 + [pl.BlockSpec(memory_space=pl.ANY), vmem()],
        out_specs=[vmem()] * count,
        scratch_shapes=[
            pltpu.VMEM((tall, out_width), jnp.float32),
            pltpu.VMEM((units, out_width), jnp.bfloat16),
            pltpu.SemaphoreType.DMA(()),
        ],
        compiler_params=params(8),
    )(sums, far_sums, weight, w_down, far_weights)


def finish(piece, cols, near, far_sums, parts):
    rows, out_width = parts[0].shape
    extra = -(-near.shape[1] // far_sums.shape[1])
    top = far_sums.shape[0] - extra * rows
    dup = 2 * piece - cols

    def kernel(near_ref, far_ref, *rest):
        part_refs, out_ref = rest[:-1], rest[-1]
        first = lax.axis_index("tp") == 0
        far = jnp.concatenate(
            [far_ref[top + b * rows : top + (b + 1) * rows, :] for b in range(extra)], axis=1
        )
        for c in range(out_width // cols):
            span = slice(c * piece, (c + 1) * piece)
            a, b = near_ref[:, span], far[:, span]
            low = jnp.where(first, a, b)
            high = jnp.where(first, b, a)[:, dup:]
            value = jnp.concatenate([low, high], axis=1)
            for ref in part_refs:
                value = value + ref[:, c * cols : (c + 1) * cols].astype(jnp.float32)
            out_ref[:, c * cols : (c + 1) * cols] = value.astype(jnp.bfloat16)

    return pl.pallas_call(
        kernel,
        name="finish",
        out_shape=shape_of((rows, out_width), jnp.bfloat16),
        in_specs=[vmem()] * (2 + len(parts)),
        out_specs=vmem(),
        compiler_params=params(4),
    )(near, far_sums, *parts)


def tuned_body(
    grid,
    residual,
    queries,
    new_kv,
    cache,
    lengths,
    w_out,
    gain,
    route_ids,
    route_weights,
    w_gate,
    w_up,
    w_down,
):
    rows, width = residual.shape
    cols = w_out.shape[1]
    piece = -(-cols // (2 * LANES)) * LANES
    gate_t, up_t = w_gate.T, w_up.T
    *outgoing, packed = attention(
        grid,
        piece,
        cols,
        queries,
        new_kv,
        cache,
        lengths,
        residual,
        route_ids.T,
        route_weights.T,
        gate_t,
        up_t,
        w_down,
    )
    chunks = grid.spread(outgoing, spaced=True)
    packed, *_ = lax.optimization_barrier((packed, *chunks))
    far_weights = swap(packed)
    ours, theirs, weight = project(grid, piece, chunks, w_out)
    stream = (ours + swap(theirs)).astype(jnp.bfloat16)
    stream, far_weights = lax.optimization_barrier((stream, far_weights))
    pieces = grid.spread([stream] * grid.z)
    sums, home = gate_up(
        grid, piece, cols, rows, pieces, gain.reshape(1, width), gate_t, up_t, far_weights
    )
    far_sums = swap(sums)
    parts = down(grid, piece, rows, sums, far_sums, weight, w_down, far_weights)
    shares = [grid.send(p, s, u) if s or u else p for p, (s, u) in zip(parts, grid.steps)]
    return finish(piece, cols, home, far_sums, shares)


def general_body(
    residual,
    queries,
    new_kv,
    cache,
    lengths,
    w_out,
    gain,
    route_ids,
    route_weights,
    w_gate,
    w_up,
    w_down,
):
    row_count = queries.shape[0]
    head_count = queries.shape[1] // HD
    scaling = HD ** (-0.5)
    query_heads = queries.reshape(row_count, head_count, HD)
    key_rows = cache[:, :, :HD]
    value_rows = cache[:, :, HD:]
    scores = (
        jnp.einsum("rhd,rpd->rhp", query_heads, key_rows, preferred_element_type=jnp.float32)
        * scaling
    )
    usable = jnp.arange(cache.shape[1], dtype=jnp.int32)[None, :] < lengths[:, None]
    scores = jnp.where(usable[:, None, :], scores, -jnp.inf)
    own_score = (
        jnp.einsum("rhd,rd->rh", query_heads, new_kv[:, :HD], preferred_element_type=jnp.float32)
        * scaling
    )
    peak_score = jnp.maximum(jnp.max(scores, axis=2), own_score)
    cache_weight = jnp.exp(scores - peak_score[:, :, None])
    own_weight = jnp.exp(own_score - peak_score)
    denominator = jnp.sum(cache_weight, axis=2) + own_weight
    probabilities = (cache_weight / denominator[:, :, None]).astype(jnp.bfloat16)
    own_prob = (own_weight / denominator).astype(jnp.bfloat16)
    context = jnp.einsum(
        "rhp,rpd->rhd", probabilities, value_rows, preferred_element_type=jnp.float32
    )
    context = context + own_prob.astype(jnp.float32)[:, :, None] * new_kv[:, None, HD:].astype(
        jnp.float32
    )
    context = context.astype(jnp.bfloat16).reshape(row_count, head_count * HD)
    attn_cols = jnp.dot(
        lax.all_gather(context, "ep", axis=0, tiled=True), w_out, preferred_element_type=jnp.float32
    )
    attn_rows = lax.all_to_all(attn_cols, "ep", split_axis=0, concat_axis=1, tiled=True)
    attention = lax.psum(attn_rows, "tp")
    stream = residual.astype(jnp.float32) + attention
    mean_square = jnp.mean(stream * stream, axis=1, keepdims=True)
    normed = (stream * lax.rsqrt(mean_square + 1e-06) * gain[None, :]).astype(jnp.bfloat16)
    width = normed.shape[1]
    ep_size = lax.axis_size("ep")
    members = ep_size // EXPERTS
    slot_count = EXPERTS * CAP
    flat_ids = route_ids.reshape(-1)
    one_hot = (flat_ids[:, None] == jnp.arange(EXPERTS, dtype=jnp.int32)[None, :]).astype(jnp.int32)
    earlier = jnp.cumsum(one_hot, axis=0) - one_hot
    slot_index = jnp.sum(earlier * one_hot, axis=1)
    target = (flat_ids * CAP + slot_index).reshape(row_count, TOPK)
    placed = (target[:, :, None] == jnp.arange(slot_count, dtype=jnp.int32)[None, None, :]).astype(
        jnp.float32
    )
    chosen = jnp.sum(placed, axis=1).reshape(row_count, EXPERTS, CAP).astype(jnp.bfloat16)
    mixing = jnp.sum(placed * route_weights[:, :, None], axis=1).reshape(row_count, EXPERTS, CAP)
    outgoing = jnp.einsum("rec,rd->ecd", chosen, normed, preferred_element_type=jnp.float32).astype(
        jnp.bfloat16
    )
    outgoing = jnp.broadcast_to(outgoing[:, None], (EXPERTS, members, CAP, width)).reshape(
        ep_size * CAP, width
    )
    arrived = lax.all_to_all(outgoing, "ep", split_axis=0, concat_axis=0, tiled=True)
    gate_act = jnp.dot(arrived, w_gate, preferred_element_type=jnp.float32)
    up_act = jnp.dot(arrived, w_up, preferred_element_type=jnp.float32)
    hidden = (jax.nn.silu(gate_act) * up_act).astype(jnp.bfloat16)
    partial_value = jnp.dot(hidden, w_down, preferred_element_type=jnp.float32)
    halves = lax.psum_scatter(partial_value, "tp", scatter_dimension=1, tiled=True)
    returned = lax.all_to_all(halves, "ep", split_axis=0, concat_axis=0, tiled=True)
    returned = returned.reshape(EXPERTS, members, CAP, returned.shape[1])
    mixed = jnp.einsum("rec,egcw->rw", mixing, returned, precision=lax.Precision.HIGHEST)
    tp_start = lax.axis_index("tp") * mixed.shape[1]
    stream_part = lax.dynamic_slice_in_dim(stream, tp_start, mixed.shape[1], 1)
    return (stream_part + mixed).astype(jnp.bfloat16)


def body(*args):
    ep_size, cols, heads_width = lax.axis_size("ep"), args[5].shape[1], args[5].shape[0]
    if ep_size == 8 and lax.axis_size("tp") == 2 and cols % LANES == 0 and heads_width % (8 * HD) == 0:
        return tuned_body(Grid(ep_size, 2), *args)
    return general_body(*args)


def solution(mesh):
    placed = (
        P(("grp", "ep"), None),
        P(("grp", "ep"), "tp"),
        P(("grp", "ep"), None),
        P(("grp", "ep"), None, None),
        P(("grp", "ep")),
        P("tp", "ep"),
        P(),
        P(("grp", "ep"), None),
        P(("grp", "ep"), None),
        P(None, ("ep", "tp")),
        P(None, ("ep", "tp")),
        P(("ep", "tp"), None),
    )
    return jax.shard_map(
        body, mesh=mesh, in_specs=placed, out_specs=P(("grp", "ep"), "tp"), check_vma=False
    )
```

```python
import functools

import jax
import jax.numpy as jnp
from jax import lax
from jax.experimental import pallas as pl
from jax.experimental.pallas import tpu as pltpu
from jax.sharding import PartitionSpec as P

HD = 256
TOPK = 3
EXPERTS = 4
CAP = 8
LANES = 128


def params(mebibytes):
    return pltpu.CompilerParams(vmem_limit_bytes=mebibytes * 1024 * 1024)


def vmem():
    return pl.BlockSpec(memory_space=pltpu.VMEM)


def anywhere():
    return pl.BlockSpec(memory_space=pl.ANY)


def shape_of(shape, dtype):
    return jax.ShapeDtypeStruct(shape, dtype)


class Grid:
    def __init__(self, ep_size, x_size):
        self.ep, self.x, self.z = ep_size, x_size, ep_size // x_size
        self.steps = [(s, u) for s in range(self.z) for u in range(x_size)]

    def send(self, arr, s, u):
        pairs = [
            (z * self.x + x, (z + s) % self.z * self.x + (x + u) % self.x)
            for z in range(self.z)
            for x in range(self.x)
        ]
        return lax.ppermute(arr, "ep", pairs)

    def near(self, own):
        got = {(0, 0): own[0]}
        for s in range(1, self.z):
            if min(s, self.z - s) == 1:
                got[s, 0] = self.send(own[s], s, 0)
        for u in range(1, self.x):
            got[0, u] = self.send(own[0], 0, u)
        return got

    def far(self, own, got):
        for s in range(1, self.z):
            if (s, 0) not in got:
                got[s, 0] = self.send(own[s], s, 0)

    def forward(self, got):
        for s, u in self.steps:
            if (s, u) not in got:
                got[s, u] = self.send(got[s, 0], 0, u)
        return [got[step] for step in self.steps]

    def spread(self, own):
        got = self.near([own] * self.z)
        self.far([own] * self.z, got)
        return self.forward(got)

    def source(self, step):
        me = lax.axis_index("ep")
        z = lax.rem(me // self.x - step[0] + self.z, self.z)
        return z * self.x + lax.rem(lax.rem(me, self.x) - step[1] + self.x, self.x)

    def target(self, step):
        return self.source((-step[0] % self.z, -step[1] % self.x))


def swap(arr):
    return lax.ppermute(arr, "tp", [(0, 1), (1, 0)])


def nt_dot(a, b):
    return lax.dot_general(a, b, (((1,), (1,)), ((), ())), preferred_element_type=jnp.float32)


def in_hbm():
    return pl.BlockSpec(memory_space=pltpu.HBM)


def attention(
    grid,
    piece,
    cols,
    queries,
    new_kv,
    cache,
    lengths,
    residual,
    route_ids,
    route_weights,
    gate_t,
    up_t,
    w_down,
):
    rows, width = queries.shape
    heads = width // HD
    ctx = cache.shape[1]
    parts = HD // LANES
    half = width // 2
    note = piece + LANES
    scaling = HD ** (-0.5)
    units, features = gate_t.shape
    out_width = features // 2
    down_blocks = out_width // piece
    packed_rows = (2 * grid.ep + down_blocks) * units

    def kernel(*refs):
        sources, rest = refs[:7], refs[7:]
        gate_ref, up_ref, down_ref, rest = rest[0], rest[1], rest[2], rest[3:]
        lead_refs, tail_ref, pack_ref, rest = rest[: grid.z], rest[grid.z], rest[grid.z + 1], rest[grid.z + 2 :]
        q_ref, kv_ref, res_ref, ids_ref, wts_ref, len_ref, kept, turned, packed, sems, row_sems, pack_sems = rest
        cache_ref = sources[6]
        copies = [
            pltpu.make_async_copy(src, dst, sems.at[i])
            for i, (src, dst) in enumerate(
                zip(sources[:6], (q_ref, kv_ref, res_ref, ids_ref, wts_ref, len_ref))
            )
        ]
        row_copies = [
            pltpu.make_async_copy(cache_ref.at[r], kept.at[r], row_sems.at[r]) for r in range(rows)
        ]
        other = 1 - lax.axis_index("tp")
        blocks = []
        for j in range(grid.ep):
            begin = pl.multiple_of(j * cols + other * (cols - piece), LANES)
            blocks += [ref.at[:, pl.ds(begin, piece)] for ref in (gate_ref, up_ref)]
        for b in range(down_blocks):
            begin = pl.multiple_of(other * out_width + b * piece, LANES)
            blocks.append(down_ref.at[:, pl.ds(begin, piece)])
        packs = [
            pltpu.make_async_copy(block, packed.at[pl.ds(i * units, units), :], pack_sems.at[i])
            for i, block in enumerate(blocks)
        ]
        pack_out = pltpu.make_async_copy(packed, pack_ref, pack_sems.at[len(blocks)])
        for copy in copies[:2] + row_copies + copies[2:] + packs:
            copy.start()

        copies[0].wait()
        copies[1].wait()
        for h in range(heads):
            for c in range(parts):
                at = h * HD + c * LANES
                turned[c, h * rows : (h + 1) * rows, :] = q_ref[:, at : at + LANES].astype(jnp.float32)
        new_k = kv_ref[:, :HD].astype(jnp.float32)
        new_v = kv_ref[:, HD:].astype(jnp.float32)
        scores, owns = [], []
        for r in range(rows):
            q = jnp.concatenate(
                [turned[c, pl.ds(r, heads, stride=rows), :] for c in range(parts)], axis=1
            )
            owns.append(jnp.sum(q * new_k[r : r + 1], axis=1, keepdims=True) * scaling)
            row_copies[r].wait()
            scores.append(nt_dot(q.astype(jnp.bfloat16), kept[r, :, :HD]) * scaling)

        for copy in copies[2:] + packs:
            copy.wait()
        pack_out.start()
        lane = lax.broadcasted_iota(jnp.int32, (rows, LANES), 1)
        square = (rows, rows)
        diagonal = lax.broadcasted_iota(jnp.int32, square, 0) == lax.broadcasted_iota(jnp.int32, square, 1)
        skip = lax.axis_index("tp") * (cols - piece)
        for s, u in grid.steps:
            to = grid.target((s, u))
            begin = pl.multiple_of(to * cols + skip, LANES)
            at = half + u * note
            lead_refs[s][:, at : at + piece] = res_ref[:, pl.ds(begin, piece)]
            chosen = ids_ref[...] == to * EXPERTS // grid.ep
            across = jnp.sum(jnp.where(chosen, wts_ref[...], 0.0), axis=0, keepdims=True)
            weight = jnp.sum(
                jnp.where(diagonal, jnp.broadcast_to(across, square), 0.0), axis=1, keepdims=True
            )
            high = weight.astype(jnp.bfloat16).astype(jnp.float32)
            middle = (weight - high).astype(jnp.bfloat16).astype(jnp.float32)
            low = weight - high - middle
            tile = jnp.where(lane == 0, high, 0.0)
            tile = jnp.where(lane == 1, middle, tile)
            tile = jnp.where(lane == 2, low, tile)
            lead_refs[s][:, at + piece : at + note] = tile.astype(jnp.bfloat16)

        place = lax.broadcasted_iota(jnp.int32, (heads, ctx), 1)
        probs, own_probs = [], []
        for r in range(rows):
            score = jnp.where(place < len_ref[r], scores[r], -jnp.inf)
            peak = jnp.maximum(jnp.max(score, axis=1, keepdims=True), owns[r])
            exps = jnp.exp(score - peak)
            own_exp = jnp.exp(owns[r] - peak)
            denominator = jnp.sum(exps, axis=1, keepdims=True) + own_exp
            probs.append((exps / denominator).astype(jnp.bfloat16))
            own_probs.append((own_exp / denominator).astype(jnp.bfloat16).astype(jnp.float32))
        for r in range(rows):
            mixed = jnp.dot(probs[r], kept[r, :, HD:], preferred_element_type=jnp.float32)
            mixed = mixed + own_probs[r] * new_v[r : r + 1]
            for c in range(parts):
                turned[c, r * heads : (r + 1) * heads, :] = mixed[:, c * LANES : (c + 1) * LANES]
        for h in range(heads):
            part, at = divmod(h, heads // 2)
            for c in range(parts):
                value = turned[c, pl.ds(h, rows, stride=heads), :].astype(jnp.bfloat16)
                begin = at * HD + c * LANES
                for ref in (tail_ref,) if part else lead_refs:
                    ref[:, begin : begin + LANES] = value
        pack_out.wait()

    return pl.pallas_call(
        kernel,
        name="attention",
        out_shape=[shape_of((rows, half + grid.x * note), jnp.bfloat16)] * grid.z
        + [shape_of((rows, half), jnp.bfloat16), shape_of((packed_rows, piece), jnp.bfloat16)],
        in_specs=[in_hbm()] * 10,
        out_specs=[vmem()] * (grid.z + 1) + [in_hbm()],
        scratch_shapes=[
            pltpu.VMEM(queries.shape, jnp.bfloat16),
            pltpu.VMEM(new_kv.shape, jnp.bfloat16),
            pltpu.VMEM(residual.shape, jnp.bfloat16),
            pltpu.VMEM(route_ids.shape, jnp.int32),
            pltpu.VMEM(route_weights.shape, jnp.float32),
            pltpu.SMEM(lengths.shape, jnp.int32),
            pltpu.VMEM(cache.shape, jnp.bfloat16),
            pltpu.VMEM((parts, rows * heads, LANES), jnp.float32),
            pltpu.VMEM((packed_rows, piece), jnp.bfloat16),
            pltpu.SemaphoreType.DMA((6,)),
            pltpu.SemaphoreType.DMA((rows,)),
            pltpu.SemaphoreType.DMA((2 * grid.ep + down_blocks + 1,)),
        ],
        compiler_params=params(60),
    )(
        queries,
        new_kv,
        residual,
        route_ids,
        route_weights,
        lengths,
        cache,
        gate_t,
        up_t,
        w_down,
    )


def project(grid, piece, chunks, w_out, before=None):
    rows = chunks[0].shape[0]
    depth, cols = w_out.shape[0] // 2, w_out.shape[1]
    count = len(chunks)
    tall = rows * count
    blocks = 4
    block = depth // blocks
    last = before is not None
    note = piece + LANES

    def kernel(*refs):
        chunk_refs, rest = refs[:count], refs[count:]
        w_ref, rest = rest[0], rest[1:]
        if last:
            before_ref, base_ref, ours_ref, theirs_ref, stacked, total = rest
        else:
            out_ref, base_ref, weight_ref, stacked, total = rest
        k = pl.program_id(0)

        @pl.when(k == 0)
        def _():
            both = jnp.concatenate([ref[:, :depth] for ref in chunk_refs], axis=0)
            for i in range(blocks):
                stacked[i] = both[:, i * block : (i + 1) * block]

        product = jnp.dot(stacked[k], w_ref[...], preferred_element_type=jnp.float32)

        @pl.when(k == 0)
        def _():
            total[...] = product + before_ref[...] if last else product

        @pl.when(k > 0)
        def _():
            total[...] += product

        @pl.when(k == blocks - 1)
        def _():
            core = lax.axis_index("tp")
            mine = pl.multiple_of(core * (cols - piece), LANES)
            other = pl.multiple_of((1 - core) * (cols - piece), LANES)
            if not last:
                out_ref[...] = total[...]
            for i, (s, u) in enumerate(grid.steps):
                here = pl.ds(pl.multiple_of(grid.source((s, u)) * rows, rows), rows)
                block_rows = slice(i * rows, (i + 1) * rows)
                if last:
                    ours_ref[here, :] = total[block_rows, pl.ds(mine, piece)] + base_ref[here, :]
                    theirs_ref[here, :] = total[block_rows, pl.ds(other, piece)]
                else:
                    at = depth + u * note
                    beside = chunk_refs[i][:, at : at + note].astype(jnp.float32)
                    base_ref[here, :] = beside[:, :piece]
                    weight_ref[here, :] = jnp.broadcast_to(
                        jnp.sum(beside[:, piece:], axis=1, keepdims=True), (rows, LANES)
                    )

    def whole(arr):
        return pl.BlockSpec(arr.shape, lambda k: (0, 0))

    pieces = shape_of((tall, piece), jnp.float32)
    if last:
        outs = [pieces] * 2
    else:
        outs = [shape_of((tall, cols), jnp.float32), pieces, shape_of((tall, LANES), jnp.float32)]
    extra = list(before) if last else []
    first_block = blocks if last else 0
    return pl.pallas_call(
        kernel,
        name="project",
        grid=(blocks,),
        out_shape=outs,
        in_specs=[whole(c) for c in chunks]
        + [pl.BlockSpec((block, cols), lambda k: (first_block + k, 0))]
        + [whole(e) for e in extra],
        out_specs=[whole(o) for o in outs],
        scratch_shapes=[
            pltpu.VMEM((blocks, tall, block), jnp.bfloat16),
            pltpu.VMEM((tall, cols), jnp.float32),
        ],
        cost_estimate=pl.CostEstimate(
            flops=8 * tall * depth * cols,
            bytes_accessed=4 * depth * cols,
            transcendentals=0,
        ),
        compiler_params=params(48),
    )(*chunks, w_out, *extra)


def gate_up(grid, piece, cols, rows, pieces, gain, gate_t, up_t, other):
    tall = pieces[0].shape[0]
    units = gate_t.shape[0]
    count = grid.ep
    dup = 2 * piece - cols
    per_half = count // 2
    sums_width = 4 * units + LANES
    extra = -(-per_half * piece // sums_width)

    def kernel(*refs):
        piece_refs, rest = refs[:count], refs[count:]
        gain_ref, gate_ref, up_ref, other_ref, sums_ref, home_ref, held, home = rest
        home[1] = jnp.zeros((rows, extra * sums_width), jnp.float32)
        core = lax.axis_index("tp")
        me = lax.axis_index("ep")
        fresh = lax.broadcasted_iota(jnp.int32, (tall, piece), 1) >= core * dup
        square = jnp.zeros((tall, 1), jnp.float32)
        own_gate = jnp.zeros((units, tall), jnp.float32)
        own_up = jnp.zeros((units, tall), jnp.float32)
        far = jnp.zeros((2 * units, tall), jnp.float32)
        for i, step in enumerate(grid.steps):
            j = grid.source(step)
            lanes = pl.ds(pl.multiple_of(j * cols + core * (cols - piece), LANES), piece)
            stream = piece_refs[i][...].astype(jnp.float32)
            held[...] = stream
            mine = held[pl.ds(pl.multiple_of(me * rows, rows), rows), :]
            side = lax.rem(j // per_half + core, 2)
            at = pl.multiple_of(lax.rem(j, per_half) * piece, LANES)
            home[side, :, pl.ds(at, piece)] = mine
            stream = jnp.where(fresh, stream, 0.0)
            square = square + jnp.sum(stream * stream, axis=1, keepdims=True)
            scaled = (stream * gain_ref[:, lanes]).astype(jnp.bfloat16)
            own_gate = own_gate + nt_dot(gate_ref[:, lanes], scaled)
            own_up = own_up + nt_dot(up_ref[:, lanes], scaled)
            block = pl.ds(pl.multiple_of(j * 2 * units, 2 * units), 2 * units)
            far = far + nt_dot(other_ref[block, :], scaled)
        sums_ref[:tall, : 4 * units] = jnp.concatenate([own_gate, own_up, far], axis=0).T
        sums_ref[:tall, 4 * units :] = jnp.broadcast_to(square, (tall, LANES))
        for b in range(extra):
            at = tall + b * rows
            sums_ref[at : at + rows, :] = home[1, :, b * sums_width : (b + 1) * sums_width]
        home_ref[...] = home[0, :, : per_half * piece]

    return pl.pallas_call(
        kernel,
        name="gate_up",
        out_shape=[
            shape_of((tall + extra * rows, sums_width), jnp.float32),
            shape_of((rows, per_half * piece), jnp.float32),
        ],
        in_specs=[vmem()] * (count + 4),
        out_specs=[vmem()] * 2,
        scratch_shapes=[
            pltpu.VMEM((tall, piece), jnp.float32),
            pltpu.VMEM((2, rows, extra * sums_width), jnp.float32),
        ],
        compiler_params=params(8),
    )(*pieces, gain, gate_t, up_t, other)


def down(grid, piece, rows, sums, far_sums, weight, w_down, far_weights):
    tall = weight.shape[0]
    units, width = w_down.shape
    out_width = width // 2
    count = grid.ep

    def kernel(sums_ref, far_ref, weight_ref, down_ref, packed_ref, *rest):
        out_refs, total, down_half, sem = rest[:count], rest[count], rest[count + 1], rest[count + 2]
        begin = pl.multiple_of(lax.axis_index("tp") * out_width, LANES)
        copy = pltpu.make_async_copy(down_ref.at[:, pl.ds(begin, out_width)], down_half, sem)
        copy.start()
        square = (
            sums_ref[:tall, 4 * units : 4 * units + 1] + far_ref[:tall, 4 * units : 4 * units + 1]
        )
        scale = lax.rsqrt(square / width + 1e-06)

        def hidden(a, b):
            both = (
                sums_ref[:tall, a * units : (a + 2) * units]
                + far_ref[:tall, b * units : (b + 2) * units]
            )
            gate, up = both[:, :units] * scale, both[:, units:] * scale
            return (gate / (1.0 + jnp.exp(-gate)) * up).astype(jnp.bfloat16)

        near, far = hidden(0, 2), hidden(2, 0)
        copy.wait()
        for b in range(out_width // piece):
            span = slice(b * piece, (b + 1) * piece)
            block = slice((2 * count + b) * units, (2 * count + b + 1) * units)
            value = jnp.dot(near, down_half[:, span], preferred_element_type=jnp.float32)
            value = value + jnp.dot(far, packed_ref[block, :], preferred_element_type=jnp.float32)
            total[:, span] = value * weight_ref[:, :1]
        for i, step in enumerate(grid.steps):
            there = pl.ds(pl.multiple_of(grid.target(step) * rows, rows), rows)
            out_refs[i][...] = total[there, :].astype(out_refs[i].dtype)

    return pl.pallas_call(
        kernel,
        name="down",
        out_shape=[
            shape_of((rows, out_width), jnp.bfloat16 if i else jnp.float32) for i in range(count)
        ],
        in_specs=[vmem()] * 3 + [pl.BlockSpec(memory_space=pl.ANY), vmem()],
        out_specs=[vmem()] * count,
        scratch_shapes=[
            pltpu.VMEM((tall, out_width), jnp.float32),
            pltpu.VMEM((units, out_width), jnp.bfloat16),
            pltpu.SemaphoreType.DMA(()),
        ],
        compiler_params=params(8),
    )(sums, far_sums, weight, w_down, far_weights)


def finish(piece, cols, near, far_sums, parts):
    rows, out_width = parts[0].shape
    extra = -(-near.shape[1] // far_sums.shape[1])
    top = far_sums.shape[0] - extra * rows
    dup = 2 * piece - cols

    def kernel(near_ref, far_ref, *rest):
        part_refs, out_ref = rest[:-1], rest[-1]
        first = lax.axis_index("tp") == 0
        far = jnp.concatenate(
            [far_ref[top + b * rows : top + (b + 1) * rows, :] for b in range(extra)], axis=1
        )
        for c in range(out_width // cols):
            span = slice(c * piece, (c + 1) * piece)
            a, b = near_ref[:, span], far[:, span]
            low = jnp.where(first, a, b)
            high = jnp.where(first, b, a)[:, dup:]
            value = jnp.concatenate([low, high], axis=1)
            for ref in part_refs:
                value = value + ref[:, c * cols : (c + 1) * cols].astype(jnp.float32)
            out_ref[:, c * cols : (c + 1) * cols] = value.astype(jnp.bfloat16)

    return pl.pallas_call(
        kernel,
        name="finish",
        out_shape=shape_of((rows, out_width), jnp.bfloat16),
        in_specs=[vmem()] * (2 + len(parts)),
        out_specs=vmem(),
        compiler_params=params(4),
    )(near, far_sums, *parts)


def tuned_body(
    grid,
    residual,
    queries,
    new_kv,
    cache,
    lengths,
    w_out,
    gain,
    route_ids,
    route_weights,
    w_gate,
    w_up,
    w_down,
):
    rows, width = residual.shape
    cols = w_out.shape[1]
    piece = -(-cols // (2 * LANES)) * LANES
    gate_t, up_t = w_gate.T, w_up.T
    *lead, tail, packed = attention(
        grid,
        piece,
        cols,
        queries,
        new_kv,
        cache,
        lengths,
        residual,
        route_ids.T,
        route_weights.T,
        gate_t,
        up_t,
        w_down,
    )
    first = grid.near(lead)
    arrived = (first[1, 0], first[0, grid.x - 1])
    *lead, tail, _, _ = lax.optimization_barrier((*lead, tail, *arrived))
    grid.far(lead, first)
    tails = [tail] * grid.z
    second = grid.near(tails)
    for s in range(2, grid.z - 1):
        first[s, 0], second = lax.optimization_barrier((first[s, 0], second))
    first_chunks = grid.forward(first)
    *tails, _, _ = lax.optimization_barrier((*tails, second[1, 0], second[0, grid.x - 1]))
    grid.far(tails, second)
    far_blocks = [second[s, 0] for s in range(2, grid.z - 1)]
    packed, first_chunks, far_blocks = lax.optimization_barrier((packed, first_chunks, far_blocks))
    for s, block in zip(range(2, grid.z - 1), far_blocks):
        second[s, 0] = block
    second_chunks = grid.forward(second)
    far_weights = swap(packed)
    before, base, weight = project(grid, piece, first_chunks, w_out)
    ours, theirs = project(grid, piece, second_chunks, w_out, (before, base))
    stream = (ours + swap(theirs)).astype(jnp.bfloat16)
    stream, far_weights = lax.optimization_barrier((stream, far_weights))
    pieces = grid.spread(stream)
    sums, home = gate_up(
        grid, piece, cols, rows, pieces, gain.reshape(1, width), gate_t, up_t, far_weights
    )
    far_sums = swap(sums)
    parts = down(grid, piece, rows, sums, far_sums, weight, w_down, far_weights)
    shares = [grid.send(p, s, u) if s or u else p for p, (s, u) in zip(parts, grid.steps)]
    return finish(piece, cols, home, far_sums, shares)


def general_body(
    residual,
    queries,
    new_kv,
    cache,
    lengths,
    w_out,
    gain,
    route_ids,
    route_weights,
    w_gate,
    w_up,
    w_down,
):
    row_count = queries.shape[0]
    head_count = queries.shape[1] // HD
    scaling = HD ** (-0.5)
    query_heads = queries.reshape(row_count, head_count, HD)
    key_rows = cache[:, :, :HD]
    value_rows = cache[:, :, HD:]
    scores = (
        jnp.einsum("rhd,rpd->rhp", query_heads, key_rows, preferred_element_type=jnp.float32)
        * scaling
    )
    usable = jnp.arange(cache.shape[1], dtype=jnp.int32)[None, :] < lengths[:, None]
    scores = jnp.where(usable[:, None, :], scores, -jnp.inf)
    own_score = (
        jnp.einsum("rhd,rd->rh", query_heads, new_kv[:, :HD], preferred_element_type=jnp.float32)
        * scaling
    )
    peak_score = jnp.maximum(jnp.max(scores, axis=2), own_score)
    cache_weight = jnp.exp(scores - peak_score[:, :, None])
    own_weight = jnp.exp(own_score - peak_score)
    denominator = jnp.sum(cache_weight, axis=2) + own_weight
    probabilities = (cache_weight / denominator[:, :, None]).astype(jnp.bfloat16)
    own_prob = (own_weight / denominator).astype(jnp.bfloat16)
    context = jnp.einsum(
        "rhp,rpd->rhd", probabilities, value_rows, preferred_element_type=jnp.float32
    )
    context = context + own_prob.astype(jnp.float32)[:, :, None] * new_kv[:, None, HD:].astype(
        jnp.float32
    )
    context = context.astype(jnp.bfloat16).reshape(row_count, head_count * HD)
    attn_cols = jnp.dot(
        lax.all_gather(context, "ep", axis=0, tiled=True), w_out, preferred_element_type=jnp.float32
    )
    attn_rows = lax.all_to_all(attn_cols, "ep", split_axis=0, concat_axis=1, tiled=True)
    attention = lax.psum(attn_rows, "tp")
    stream = residual.astype(jnp.float32) + attention
    mean_square = jnp.mean(stream * stream, axis=1, keepdims=True)
    normed = (stream * lax.rsqrt(mean_square + 1e-06) * gain[None, :]).astype(jnp.bfloat16)
    width = normed.shape[1]
    ep_size = lax.axis_size("ep")
    members = ep_size // EXPERTS
    slot_count = EXPERTS * CAP
    flat_ids = route_ids.reshape(-1)
    one_hot = (flat_ids[:, None] == jnp.arange(EXPERTS, dtype=jnp.int32)[None, :]).astype(jnp.int32)
    earlier = jnp.cumsum(one_hot, axis=0) - one_hot
    slot_index = jnp.sum(earlier * one_hot, axis=1)
    target = (flat_ids * CAP + slot_index).reshape(row_count, TOPK)
    placed = (target[:, :, None] == jnp.arange(slot_count, dtype=jnp.int32)[None, None, :]).astype(
        jnp.float32
    )
    chosen = jnp.sum(placed, axis=1).reshape(row_count, EXPERTS, CAP).astype(jnp.bfloat16)
    mixing = jnp.sum(placed * route_weights[:, :, None], axis=1).reshape(row_count, EXPERTS, CAP)
    outgoing = jnp.einsum("rec,rd->ecd", chosen, normed, preferred_element_type=jnp.float32).astype(
        jnp.bfloat16
    )
    outgoing = jnp.broadcast_to(outgoing[:, None], (EXPERTS, members, CAP, width)).reshape(
        ep_size * CAP, width
    )
    arrived = lax.all_to_all(outgoing, "ep", split_axis=0, concat_axis=0, tiled=True)
    gate_act = jnp.dot(arrived, w_gate, preferred_element_type=jnp.float32)
    up_act = jnp.dot(arrived, w_up, preferred_element_type=jnp.float32)
    hidden = (jax.nn.silu(gate_act) * up_act).astype(jnp.bfloat16)
    partial_value = jnp.dot(hidden, w_down, preferred_element_type=jnp.float32)
    halves = lax.psum_scatter(partial_value, "tp", scatter_dimension=1, tiled=True)
    returned = lax.all_to_all(halves, "ep", split_axis=0, concat_axis=0, tiled=True)
    returned = returned.reshape(EXPERTS, members, CAP, returned.shape[1])
    mixed = jnp.einsum("rec,egcw->rw", mixing, returned, precision=lax.Precision.HIGHEST)
    tp_start = lax.axis_index("tp") * mixed.shape[1]
    stream_part = lax.dynamic_slice_in_dim(stream, tp_start, mixed.shape[1], 1)
    return (stream_part + mixed).astype(jnp.bfloat16)


def body(*args):
    ep_size, cols, heads_width = lax.axis_size("ep"), args[5].shape[1], args[5].shape[0]
    if ep_size == 8 and lax.axis_size("tp") == 2 and cols % LANES == 0 and heads_width % (8 * HD) == 0:
        return tuned_body(Grid(ep_size, 2), *args)
    return general_body(*args)


def solution(mesh):
    placed = (
        P(("grp", "ep"), None),
        P(("grp", "ep"), "tp"),
        P(("grp", "ep"), None),
        P(("grp", "ep"), None, None),
        P(("grp", "ep")),
        P("tp", "ep"),
        P(),
        P(("grp", "ep"), None),
        P(("grp", "ep"), None),
        P(None, ("ep", "tp")),
        P(None, ("ep", "tp")),
        P(("ep", "tp"), None),
    )
    return jax.shard_map(
        body, mesh=mesh, in_specs=placed, out_specs=P(("grp", "ep"), "tp"), check_vma=False
    )
```

```python
import functools

import jax
import jax.numpy as jnp
from jax import lax
from jax.experimental import pallas as pl
from jax.experimental.pallas import tpu as pltpu
from jax.sharding import PartitionSpec as P

HD = 256
TOPK = 3
EXPERTS = 4
CAP = 8
LANES = 128


def params(mebibytes):
    return pltpu.CompilerParams(vmem_limit_bytes=mebibytes * 1024 * 1024)


def vmem():
    return pl.BlockSpec(memory_space=pltpu.VMEM)


def anywhere():
    return pl.BlockSpec(memory_space=pl.ANY)


def shape_of(shape, dtype):
    return jax.ShapeDtypeStruct(shape, dtype)


class Grid:
    def __init__(self, ep_size):
        self.ep, self.x, self.z = ep_size, ep_size // 4, 4
        self.steps = [(s, u) for s in range(self.z) for u in range(self.x)]

    def send(self, arr, s, u):
        pairs = [
            (z * self.x + x, (z ^ s) * self.x + (x + u) % self.x)
            for z in range(self.z)
            for x in range(self.x)
        ]
        return lax.ppermute(arr, "ep", pairs)

    def carried(self, step):
        s, u = step
        return (s, u) if s < 3 else (2, self.x + u)

    def block_sizes(self):
        return [self.x, self.x, 2 * self.x]

    def spread(self, blocks):
        got = {(0, 0): blocks[0]}
        got[2, 0] = self.send(blocks[2], 2, 0)
        got[1, 0] = self.send(blocks[1], 1, 0)
        for u in range(1, self.x):
            got[0, u] = self.send(got[0, 0], 0, u)
        leaving, *_ = lax.optimization_barrier((got[2, 0], got[1, 0], got[0, self.x - 1]))
        last = self.send(leaving, 1, 0)
        for u in range(1, self.x):
            got[1, u] = self.send(got[1, 0], 0, u)
        got[3, 0], *_ = lax.optimization_barrier((last, got[1, self.x - 1]))
        return self.forward(got)

    def spread_at_once(self, own):
        return self.forward({(s, 0): self.send(own, s, 0) if s else own for s in range(self.z)})

    def forward(self, got):
        for s, u in self.steps:
            if (s, u) not in got:
                got[s, u] = self.send(got[s, 0], 0, u)
        return [got[step] for step in self.steps]

    def source(self, step):
        me = lax.axis_index("ep")
        z = (me // self.x) ^ step[0]
        return z * self.x + lax.rem(lax.rem(me, self.x) - step[1] + self.x, self.x)

    def target(self, step):
        return self.source((step[0], -step[1] % self.x))


def swap(arr):
    return lax.ppermute(arr, "tp", [(0, 1), (1, 0)])


def nt_dot(a, b):
    return lax.dot_general(a, b, (((1,), (1,)), ((), ())), preferred_element_type=jnp.float32)


def in_hbm():
    return pl.BlockSpec(memory_space=pltpu.HBM)


def attention(
    grid,
    piece,
    cols,
    queries,
    new_kv,
    cache,
    lengths,
    residual,
    route_ids,
    route_weights,
    gate_t,
    up_t,
    w_down,
):
    rows, width = queries.shape
    heads = width // HD
    ctx = cache.shape[1]
    parts = HD // LANES
    sizes = grid.block_sizes()
    note = piece + LANES
    scaling = HD ** (-0.5)
    units, features = gate_t.shape
    out_width = features // 2
    down_blocks = out_width // piece
    packed_rows = (2 * grid.ep + down_blocks) * units

    def kernel(*refs):
        sources, rest = refs[:7], refs[7:]
        gate_ref, up_ref, down_ref, rest = rest[0], rest[1], rest[2], rest[3:]
        out_refs, pack_ref, rest = rest[: len(sizes)], rest[len(sizes)], rest[len(sizes) + 1 :]
        q_ref, kv_ref, res_ref, ids_ref, wts_ref, len_ref, kept, turned, packed, sems, row_sems, pack_sems = rest
        cache_ref = sources[6]
        copies = [
            pltpu.make_async_copy(src, dst, sems.at[i])
            for i, (src, dst) in enumerate(
                zip(sources[:6], (q_ref, kv_ref, res_ref, ids_ref, wts_ref, len_ref))
            )
        ]
        row_copies = [
            pltpu.make_async_copy(cache_ref.at[r], kept.at[r], row_sems.at[r]) for r in range(rows)
        ]
        other = 1 - lax.axis_index("tp")
        blocks = []
        for j in range(grid.ep):
            begin = pl.multiple_of(j * cols + other * (cols - piece), LANES)
            blocks += [ref.at[:, pl.ds(begin, piece)] for ref in (gate_ref, up_ref)]
        for b in range(down_blocks):
            begin = pl.multiple_of(other * out_width + b * piece, LANES)
            blocks.append(down_ref.at[:, pl.ds(begin, piece)])
        packs = [
            pltpu.make_async_copy(block, packed.at[pl.ds(i * units, units), :], pack_sems.at[i])
            for i, block in enumerate(blocks)
        ]
        pack_out = pltpu.make_async_copy(packed, pack_ref, pack_sems.at[len(blocks)])
        for copy in copies[:2] + row_copies + copies[2:] + packs:
            copy.start()

        copies[0].wait()
        copies[1].wait()
        for h in range(heads):
            for c in range(parts):
                at = h * HD + c * LANES
                turned[c, h * rows : (h + 1) * rows, :] = q_ref[:, at : at + LANES].astype(jnp.float32)
        new_k = kv_ref[:, :HD].astype(jnp.float32)
        new_v = kv_ref[:, HD:].astype(jnp.float32)
        scores, owns = [], []
        for r in range(rows):
            q = jnp.concatenate(
                [turned[c, pl.ds(r, heads, stride=rows), :] for c in range(parts)], axis=1
            )
            owns.append(jnp.sum(q * new_k[r : r + 1], axis=1, keepdims=True) * scaling)
            row_copies[r].wait()
            scores.append(nt_dot(q.astype(jnp.bfloat16), kept[r, :, :HD]) * scaling)

        for copy in copies[2:] + packs:
            copy.wait()
        pack_out.start()
        lane = lax.broadcasted_iota(jnp.int32, (rows, LANES), 1)
        square = (rows, rows)
        diagonal = lax.broadcasted_iota(jnp.int32, square, 0) == lax.broadcasted_iota(jnp.int32, square, 1)
        skip = lax.axis_index("tp") * (cols - piece)
        for s, u in grid.steps:
            to = grid.target((s, u))
            begin = pl.multiple_of(to * cols + skip, LANES)
            block, place_in = grid.carried((s, u))
            at = width + place_in * note
            out_refs[block][:, at : at + piece] = res_ref[:, pl.ds(begin, piece)]
            chosen = ids_ref[...] == to * EXPERTS // grid.ep
            across = jnp.sum(jnp.where(chosen, wts_ref[...], 0.0), axis=0, keepdims=True)
            weight = jnp.sum(
                jnp.where(diagonal, jnp.broadcast_to(across, square), 0.0), axis=1, keepdims=True
            )
            high = weight.astype(jnp.bfloat16).astype(jnp.float32)
            middle = (weight - high).astype(jnp.bfloat16).astype(jnp.float32)
            low = weight - high - middle
            tile = jnp.where(lane == 0, high, 0.0)
            tile = jnp.where(lane == 1, middle, tile)
            tile = jnp.where(lane == 2, low, tile)
            out_refs[block][:, at + piece : at + note] = tile.astype(jnp.bfloat16)

        place = lax.broadcasted_iota(jnp.int32, (heads, ctx), 1)
        probs, own_probs = [], []
        for r in range(rows):
            score = jnp.where(place < len_ref[r], scores[r], -jnp.inf)
            peak = jnp.maximum(jnp.max(score, axis=1, keepdims=True), owns[r])
            exps = jnp.exp(score - peak)
            own_exp = jnp.exp(owns[r] - peak)
            denominator = jnp.sum(exps, axis=1, keepdims=True) + own_exp
            probs.append((exps / denominator).astype(jnp.bfloat16))
            own_probs.append((own_exp / denominator).astype(jnp.bfloat16).astype(jnp.float32))
        for r in range(rows):
            mixed = jnp.dot(probs[r], kept[r, :, HD:], preferred_element_type=jnp.float32)
            mixed = mixed + own_probs[r] * new_v[r : r + 1]
            for c in range(parts):
                turned[c, r * heads : (r + 1) * heads, :] = mixed[:, c * LANES : (c + 1) * LANES]
        for h in range(heads):
            for c in range(parts):
                value = turned[c, pl.ds(h, rows, stride=heads), :].astype(jnp.bfloat16)
                begin = h * HD + c * LANES
                for ref in out_refs:
                    ref[:, begin : begin + LANES] = value
        pack_out.wait()

    return pl.pallas_call(
        kernel,
        name="attention",
        out_shape=[shape_of((rows, width + size * note), jnp.bfloat16) for size in sizes]
        + [shape_of((packed_rows, piece), jnp.bfloat16)],
        in_specs=[in_hbm()] * 10,
        out_specs=[vmem()] * len(sizes) + [in_hbm()],
        scratch_shapes=[
            pltpu.VMEM(queries.shape, jnp.bfloat16),
            pltpu.VMEM(new_kv.shape, jnp.bfloat16),
            pltpu.VMEM(residual.shape, jnp.bfloat16),
            pltpu.VMEM(route_ids.shape, jnp.int32),
            pltpu.VMEM(route_weights.shape, jnp.float32),
            pltpu.SMEM(lengths.shape, jnp.int32),
            pltpu.VMEM(cache.shape, jnp.bfloat16),
            pltpu.VMEM((parts, rows * heads, LANES), jnp.float32),
            pltpu.VMEM((packed_rows, piece), jnp.bfloat16),
            pltpu.SemaphoreType.DMA((6,)),
            pltpu.SemaphoreType.DMA((rows,)),
            pltpu.SemaphoreType.DMA((2 * grid.ep + down_blocks + 1,)),
        ],
        compiler_params=params(60),
    )(
        queries,
        new_kv,
        residual,
        route_ids,
        route_weights,
        lengths,
        cache,
        gate_t,
        up_t,
        w_down,
    )


def project(grid, piece, chunks, w_out):
    rows = chunks[0].shape[0]
    depth, cols = w_out.shape
    count = len(chunks)
    tall = rows * count
    blocks = 8
    block = depth // blocks
    note = piece + LANES

    def kernel(*refs):
        chunk_refs, rest = refs[:count], refs[count:]
        w_ref, ours_ref, theirs_ref, weight_ref, stacked, total = rest
        k = pl.program_id(0)

        @pl.when(k == 0)
        def _():
            both = jnp.concatenate([ref[:, :depth] for ref in chunk_refs], axis=0)
            for i in range(blocks):
                stacked[i] = both[:, i * block : (i + 1) * block]

        product = jnp.dot(stacked[k], w_ref[...], preferred_element_type=jnp.float32)

        @pl.when(k == 0)
        def _():
            total[...] = product

        @pl.when(k > 0)
        def _():
            total[...] += product

        @pl.when(k == blocks - 1)
        def _():
            core = lax.axis_index("tp")
            mine = pl.multiple_of(core * (cols - piece), LANES)
            other = pl.multiple_of((1 - core) * (cols - piece), LANES)
            for i, (s, u) in enumerate(grid.steps):
                here = pl.ds(pl.multiple_of(grid.source((s, u)) * rows, rows), rows)
                at = depth + grid.carried((s, u))[1] * note
                beside = chunk_refs[i][:, at : at + note].astype(jnp.float32)
                block_rows = slice(i * rows, (i + 1) * rows)
                ours_ref[here, :] = total[block_rows, pl.ds(mine, piece)] + beside[:, :piece]
                theirs_ref[here, :] = total[block_rows, pl.ds(other, piece)]
                weight_ref[here, :] = jnp.broadcast_to(
                    jnp.sum(beside[:, piece:], axis=1, keepdims=True), (rows, LANES)
                )

    def whole(arr):
        return pl.BlockSpec(arr.shape, lambda k: (0, 0))

    outs = [shape_of((tall, piece), jnp.float32)] * 2 + [shape_of((tall, LANES), jnp.float32)]
    return pl.pallas_call(
        kernel,
        name="project",
        grid=(blocks,),
        out_shape=outs,
        in_specs=[whole(c) for c in chunks] + [pl.BlockSpec((block, cols), lambda k: (k, 0))],
        out_specs=[whole(o) for o in outs],
        scratch_shapes=[
            pltpu.VMEM((blocks, tall, block), jnp.bfloat16),
            pltpu.VMEM((tall, cols), jnp.float32),
        ],
        cost_estimate=pl.CostEstimate(
            flops=2 * tall * depth * cols,
            bytes_accessed=2 * depth * cols + 2 * tall * depth + 8 * tall * piece,
            transcendentals=0,
        ),
        compiler_params=params(48),
    )(*chunks, w_out)


def gate_up(grid, piece, cols, rows, pieces, gain, gate_t, up_t, other):
    tall = pieces[0].shape[0]
    units = gate_t.shape[0]
    count = grid.ep
    dup = 2 * piece - cols
    per_half = count // 2
    sums_width = 4 * units + LANES
    extra = -(-per_half * piece // sums_width)

    def kernel(*refs):
        piece_refs, rest = refs[:count], refs[count:]
        gain_ref, gate_ref, up_ref, other_ref, sums_ref, home_ref, held, home = rest
        home[1] = jnp.zeros((rows, extra * sums_width), jnp.float32)
        core = lax.axis_index("tp")
        me = lax.axis_index("ep")
        fresh = lax.broadcasted_iota(jnp.int32, (tall, piece), 1) >= core * dup
        square = jnp.zeros((tall, 1), jnp.float32)
        own_gate = jnp.zeros((units, tall), jnp.float32)
        own_up = jnp.zeros((units, tall), jnp.float32)
        far = jnp.zeros((2 * units, tall), jnp.float32)
        for i, step in enumerate(grid.steps):
            j = grid.source(step)
            lanes = pl.ds(pl.multiple_of(j * cols + core * (cols - piece), LANES), piece)
            stream = piece_refs[i][...].astype(jnp.float32)
            held[...] = stream
            mine = held[pl.ds(pl.multiple_of(me * rows, rows), rows), :]
            side = lax.rem(j // per_half + core, 2)
            at = pl.multiple_of(lax.rem(j, per_half) * piece, LANES)
            home[side, :, pl.ds(at, piece)] = mine
            stream = jnp.where(fresh, stream, 0.0)
            square = square + jnp.sum(stream * stream, axis=1, keepdims=True)
            scaled = (stream * gain_ref[:, lanes]).astype(jnp.bfloat16)
            own_gate = own_gate + nt_dot(gate_ref[:, lanes], scaled)
            own_up = own_up + nt_dot(up_ref[:, lanes], scaled)
            block = pl.ds(pl.multiple_of(j * 2 * units, 2 * units), 2 * units)
            far = far + nt_dot(other_ref[block, :], scaled)
        sums_ref[:tall, : 4 * units] = jnp.concatenate([own_gate, own_up, far], axis=0).T
        sums_ref[:tall, 4 * units :] = jnp.broadcast_to(square, (tall, LANES))
        for b in range(extra):
            at = tall + b * rows
            sums_ref[at : at + rows, :] = home[1, :, b * sums_width : (b + 1) * sums_width]
        home_ref[...] = home[0, :, : per_half * piece]

    return pl.pallas_call(
        kernel,
        name="gate_up",
        out_shape=[
            shape_of((tall + extra * rows, sums_width), jnp.float32),
            shape_of((rows, per_half * piece), jnp.float32),
        ],
        in_specs=[vmem()] * (count + 4),
        out_specs=[vmem()] * 2,
        scratch_shapes=[
            pltpu.VMEM((tall, piece), jnp.float32),
            pltpu.VMEM((2, rows, extra * sums_width), jnp.float32),
        ],
        compiler_params=params(8),
    )(*pieces, gain, gate_t, up_t, other)


def down(grid, piece, rows, sums, far_sums, weight, w_down, far_weights):
    tall = weight.shape[0]
    units, width = w_down.shape
    out_width = width // 2
    count = grid.ep

    def kernel(sums_ref, far_ref, weight_ref, down_ref, packed_ref, *rest):
        out_refs, total, down_half, sem = rest[:count], rest[count], rest[count + 1], rest[count + 2]
        begin = pl.multiple_of(lax.axis_index("tp") * out_width, LANES)
        copy = pltpu.make_async_copy(down_ref.at[:, pl.ds(begin, out_width)], down_half, sem)
        copy.start()
        square = (
            sums_ref[:tall, 4 * units : 4 * units + 1] + far_ref[:tall, 4 * units : 4 * units + 1]
        )
        scale = lax.rsqrt(square / width + 1e-06)

        def hidden(a, b):
            both = (
                sums_ref[:tall, a * units : (a + 2) * units]
                + far_ref[:tall, b * units : (b + 2) * units]
            )
            gate, up = both[:, :units] * scale, both[:, units:] * scale
            return (gate / (1.0 + jnp.exp(-gate)) * up).astype(jnp.bfloat16)

        near, far = hidden(0, 2), hidden(2, 0)
        copy.wait()
        for b in range(out_width // piece):
            span = slice(b * piece, (b + 1) * piece)
            block = slice((2 * count + b) * units, (2 * count + b + 1) * units)
            value = jnp.dot(near, down_half[:, span], preferred_element_type=jnp.float32)
            value = value + jnp.dot(far, packed_ref[block, :], preferred_element_type=jnp.float32)
            total[:, span] = value * weight_ref[:, :1]
        for i, step in enumerate(grid.steps):
            there = pl.ds(pl.multiple_of(grid.target(step) * rows, rows), rows)
            out_refs[i][...] = total[there, :].astype(out_refs[i].dtype)

    return pl.pallas_call(
        kernel,
        name="down",
        out_shape=[
            shape_of((rows, out_width), jnp.bfloat16 if i else jnp.float32) for i in range(count)
        ],
        in_specs=[vmem()] * 3 + [pl.BlockSpec(memory_space=pl.ANY), vmem()],
        out_specs=[vmem()] * count,
        scratch_shapes=[
            pltpu.VMEM((tall, out_width), jnp.float32),
            pltpu.VMEM((units, out_width), jnp.bfloat16),
            pltpu.SemaphoreType.DMA(()),
        ],
        compiler_params=params(8),
    )(sums, far_sums, weight, w_down, far_weights)


def finish(piece, cols, near, far_sums, parts):
    rows, out_width = parts[0].shape
    extra = -(-near.shape[1] // far_sums.shape[1])
    top = far_sums.shape[0] - extra * rows
    dup = 2 * piece - cols

    def kernel(near_ref, far_ref, *rest):
        part_refs, out_ref = rest[:-1], rest[-1]
        first = lax.axis_index("tp") == 0
        far = jnp.concatenate(
            [far_ref[top + b * rows : top + (b + 1) * rows, :] for b in range(extra)], axis=1
        )
        for c in range(out_width // cols):
            span = slice(c * piece, (c + 1) * piece)
            a, b = near_ref[:, span], far[:, span]
            low = jnp.where(first, a, b)
            high = jnp.where(first, b, a)[:, dup:]
            value = jnp.concatenate([low, high], axis=1)
            for ref in part_refs:
                value = value + ref[:, c * cols : (c + 1) * cols].astype(jnp.float32)
            out_ref[:, c * cols : (c + 1) * cols] = value.astype(jnp.bfloat16)

    return pl.pallas_call(
        kernel,
        name="finish",
        out_shape=shape_of((rows, out_width), jnp.bfloat16),
        in_specs=[vmem()] * (2 + len(parts)),
        out_specs=vmem(),
        compiler_params=params(4),
    )(near, far_sums, *parts)


def tuned_body(
    grid,
    residual,
    queries,
    new_kv,
    cache,
    lengths,
    w_out,
    gain,
    route_ids,
    route_weights,
    w_gate,
    w_up,
    w_down,
):
    rows, width = residual.shape
    cols = w_out.shape[1]
    piece = -(-cols // (2 * LANES)) * LANES
    gate_t, up_t = w_gate.T, w_up.T
    *outgoing, packed = attention(
        grid,
        piece,
        cols,
        queries,
        new_kv,
        cache,
        lengths,
        residual,
        route_ids.T,
        route_weights.T,
        gate_t,
        up_t,
        w_down,
    )
    chunks = grid.spread(outgoing)
    packed, *_ = lax.optimization_barrier((packed, *chunks))
    far_weights = swap(packed)
    ours, theirs, weight = project(grid, piece, chunks, w_out)
    stream = (ours + swap(theirs)).astype(jnp.bfloat16)
    stream, far_weights = lax.optimization_barrier((stream, far_weights))
    pieces = grid.spread_at_once(stream)
    sums, home = gate_up(
        grid, piece, cols, rows, pieces, gain.reshape(1, width), gate_t, up_t, far_weights
    )
    far_sums = swap(sums)
    parts = down(grid, piece, rows, sums, far_sums, weight, w_down, far_weights)
    order = sorted(range(grid.ep), key=lambda i: (grid.steps[i] == (0, 0), -grid.steps[i][0]))
    shares = [grid.send(parts[i], *grid.steps[i]) if any(grid.steps[i]) else parts[i] for i in order]
    return finish(piece, cols, home, far_sums, shares)


def general_body(
    residual,
    queries,
    new_kv,
    cache,
    lengths,
    w_out,
    gain,
    route_ids,
    route_weights,
    w_gate,
    w_up,
    w_down,
):
    row_count = queries.shape[0]
    head_count = queries.shape[1] // HD
    scaling = HD ** (-0.5)
    query_heads = queries.reshape(row_count, head_count, HD)
    key_rows = cache[:, :, :HD]
    value_rows = cache[:, :, HD:]
    scores = (
        jnp.einsum("rhd,rpd->rhp", query_heads, key_rows, preferred_element_type=jnp.float32)
        * scaling
    )
    usable = jnp.arange(cache.shape[1], dtype=jnp.int32)[None, :] < lengths[:, None]
    scores = jnp.where(usable[:, None, :], scores, -jnp.inf)
    own_score = (
        jnp.einsum("rhd,rd->rh", query_heads, new_kv[:, :HD], preferred_element_type=jnp.float32)
        * scaling
    )
    peak_score = jnp.maximum(jnp.max(scores, axis=2), own_score)
    cache_weight = jnp.exp(scores - peak_score[:, :, None])
    own_weight = jnp.exp(own_score - peak_score)
    denominator = jnp.sum(cache_weight, axis=2) + own_weight
    probabilities = (cache_weight / denominator[:, :, None]).astype(jnp.bfloat16)
    own_prob = (own_weight / denominator).astype(jnp.bfloat16)
    context = jnp.einsum(
        "rhp,rpd->rhd", probabilities, value_rows, preferred_element_type=jnp.float32
    )
    context = context + own_prob.astype(jnp.float32)[:, :, None] * new_kv[:, None, HD:].astype(
        jnp.float32
    )
    context = context.astype(jnp.bfloat16).reshape(row_count, head_count * HD)
    attn_cols = jnp.dot(
        lax.all_gather(context, "ep", axis=0, tiled=True), w_out, preferred_element_type=jnp.float32
    )
    attn_rows = lax.all_to_all(attn_cols, "ep", split_axis=0, concat_axis=1, tiled=True)
    attention = lax.psum(attn_rows, "tp")
    stream = residual.astype(jnp.float32) + attention
    mean_square = jnp.mean(stream * stream, axis=1, keepdims=True)
    normed = (stream * lax.rsqrt(mean_square + 1e-06) * gain[None, :]).astype(jnp.bfloat16)
    width = normed.shape[1]
    ep_size = lax.axis_size("ep")
    members = ep_size // EXPERTS
    slot_count = EXPERTS * CAP
    flat_ids = route_ids.reshape(-1)
    one_hot = (flat_ids[:, None] == jnp.arange(EXPERTS, dtype=jnp.int32)[None, :]).astype(jnp.int32)
    earlier = jnp.cumsum(one_hot, axis=0) - one_hot
    slot_index = jnp.sum(earlier * one_hot, axis=1)
    target = (flat_ids * CAP + slot_index).reshape(row_count, TOPK)
    placed = (target[:, :, None] == jnp.arange(slot_count, dtype=jnp.int32)[None, None, :]).astype(
        jnp.float32
    )
    chosen = jnp.sum(placed, axis=1).reshape(row_count, EXPERTS, CAP).astype(jnp.bfloat16)
    mixing = jnp.sum(placed * route_weights[:, :, None], axis=1).reshape(row_count, EXPERTS, CAP)
    outgoing = jnp.einsum("rec,rd->ecd", chosen, normed, preferred_element_type=jnp.float32).astype(
        jnp.bfloat16
    )
    outgoing = jnp.broadcast_to(outgoing[:, None], (EXPERTS, members, CAP, width)).reshape(
        ep_size * CAP, width
    )
    arrived = lax.all_to_all(outgoing, "ep", split_axis=0, concat_axis=0, tiled=True)
    gate_act = jnp.dot(arrived, w_gate, preferred_element_type=jnp.float32)
    up_act = jnp.dot(arrived, w_up, preferred_element_type=jnp.float32)
    hidden = (jax.nn.silu(gate_act) * up_act).astype(jnp.bfloat16)
    partial_value = jnp.dot(hidden, w_down, preferred_element_type=jnp.float32)
    halves = lax.psum_scatter(partial_value, "tp", scatter_dimension=1, tiled=True)
    returned = lax.all_to_all(halves, "ep", split_axis=0, concat_axis=0, tiled=True)
    returned = returned.reshape(EXPERTS, members, CAP, returned.shape[1])
    mixed = jnp.einsum("rec,egcw->rw", mixing, returned, precision=lax.Precision.HIGHEST)
    tp_start = lax.axis_index("tp") * mixed.shape[1]
    stream_part = lax.dynamic_slice_in_dim(stream, tp_start, mixed.shape[1], 1)
    return (stream_part + mixed).astype(jnp.bfloat16)


def body(*args):
    ep_size, cols, heads_width = lax.axis_size("ep"), args[5].shape[1], args[5].shape[0]
    if ep_size == 8 and lax.axis_size("tp") == 2 and cols % LANES == 0 and heads_width % (8 * HD) == 0:
        return tuned_body(Grid(ep_size), *args)
    return general_body(*args)


def solution(mesh):
    placed = (
        P(("grp", "ep"), None),
        P(("grp", "ep"), "tp"),
        P(("grp", "ep"), None),
        P(("grp", "ep"), None, None),
        P(("grp", "ep")),
        P("tp", "ep"),
        P(),
        P(("grp", "ep"), None),
        P(("grp", "ep"), None),
        P(None, ("ep", "tp")),
        P(None, ("ep", "tp")),
        P(("ep", "tp"), None),
    )
    return jax.shard_map(
        body, mesh=mesh, in_specs=placed, out_specs=P(("grp", "ep"), "tp"), check_vma=False
    )
```

```python
import functools

import jax
import jax.numpy as jnp
from jax import lax
from jax.experimental import pallas as pl
from jax.experimental.pallas import tpu as pltpu
from jax.sharding import PartitionSpec as P

HD = 256
TOPK = 3
EXPERTS = 4
CAP = 8
LANES = 128


def params(mebibytes):
    return pltpu.CompilerParams(vmem_limit_bytes=mebibytes * 1024 * 1024)


def vmem():
    return pl.BlockSpec(memory_space=pltpu.VMEM)


def anywhere():
    return pl.BlockSpec(memory_space=pl.ANY)


def shape_of(shape, dtype):
    return jax.ShapeDtypeStruct(shape, dtype)


class Grid:
    def __init__(self, ep_size):
        self.ep, self.x, self.z = ep_size, ep_size // 4, 4
        self.steps = [(s, u) for s in range(self.z) for u in range(self.x)]

    def send(self, arr, s, u):
        pairs = [
            (z * self.x + x, (z + s) % self.z * self.x + (x + u) % self.x)
            for z in range(self.z)
            for x in range(self.x)
        ]
        return lax.ppermute(arr, "ep", pairs)

    def along_x(self, got, s):
        for u in range(1, self.x):
            got[s, u] = self.send(got[s, 0], 0, u)

    def spread(self, own, spaced):
        got = {(0, 0): own[0]}
        got[1, 0] = self.send(own[1], 1, 0)
        got[3, 0] = self.send(own[3], 3, 0)
        self.along_x(got, 0)
        far = own[2]
        if spaced:
            far, *_ = lax.optimization_barrier((far, got[1, 0], got[0, self.x - 1]))
        got[2, 0] = self.send(far, 2, 0)
        self.along_x(got, 1)
        self.along_x(got, 3)
        if not spaced:
            got[2, 0], *_ = lax.optimization_barrier((got[2, 0], got[1, self.x - 1]))
        self.along_x(got, 2)
        return [got[step] for step in self.steps]

    def source(self, step):
        me = lax.axis_index("ep")
        z = lax.rem(me // self.x - step[0] + self.z, self.z)
        return z * self.x + lax.rem(lax.rem(me, self.x) - step[1] + self.x, self.x)

    def target(self, step):
        return self.source((-step[0] % self.z, -step[1] % self.x))


def swap(arr):
    return lax.ppermute(arr, "tp", [(0, 1), (1, 0)])


def nt_dot(a, b):
    return lax.dot_general(a, b, (((1,), (1,)), ((), ())), preferred_element_type=jnp.float32)


def in_hbm():
    return pl.BlockSpec(memory_space=pltpu.HBM)


def attention(
    grid,
    piece,
    cols,
    queries,
    new_kv,
    cache,
    lengths,
    residual,
    route_ids,
    route_weights,
    gate_t,
    up_t,
    w_down,
):
    rows, width = queries.shape
    heads = width // HD
    ctx = cache.shape[1]
    parts = HD // LANES
    sizes = [grid.x] * grid.z
    note = piece + LANES
    scaling = HD ** (-0.5)
    units, features = gate_t.shape
    out_width = features // 2
    down_blocks = out_width // piece
    packed_rows = (2 * grid.ep + down_blocks) * units

    def kernel(*refs):
        sources, rest = refs[:7], refs[7:]
        gate_ref, up_ref, down_ref, rest = rest[0], rest[1], rest[2], rest[3:]
        out_refs, pack_ref, rest = rest[: len(sizes)], rest[len(sizes)], rest[len(sizes) + 1 :]
        q_ref, kv_ref, res_ref, ids_ref, wts_ref, len_ref, kept, turned, packed, sems, row_sems, pack_sems = rest
        cache_ref = sources[6]
        copies = [
            pltpu.make_async_copy(src, dst, sems.at[i])
            for i, (src, dst) in enumerate(
                zip(sources[:6], (q_ref, kv_ref, res_ref, ids_ref, wts_ref, len_ref))
            )
        ]
        row_copies = [
            pltpu.make_async_copy(cache_ref.at[r], kept.at[r], row_sems.at[r]) for r in range(rows)
        ]
        other = 1 - lax.axis_index("tp")
        blocks = []
        for j in range(grid.ep):
            begin = pl.multiple_of(j * cols + other * (cols - piece), LANES)
            blocks += [ref.at[:, pl.ds(begin, piece)] for ref in (gate_ref, up_ref)]
        for b in range(down_blocks):
            begin = pl.multiple_of(other * out_width + b * piece, LANES)
            blocks.append(down_ref.at[:, pl.ds(begin, piece)])
        packs = [
            pltpu.make_async_copy(block, packed.at[pl.ds(i * units, units), :], pack_sems.at[i])
            for i, block in enumerate(blocks)
        ]
        pack_out = pltpu.make_async_copy(packed, pack_ref, pack_sems.at[len(blocks)])
        for copy in copies[:2] + row_copies + copies[2:] + packs:
            copy.start()

        copies[0].wait()
        copies[1].wait()
        for h in range(heads):
            for c in range(parts):
                at = h * HD + c * LANES
                turned[c, h * rows : (h + 1) * rows, :] = q_ref[:, at : at + LANES].astype(jnp.float32)
        new_k = kv_ref[:, :HD].astype(jnp.float32)
        new_v = kv_ref[:, HD:].astype(jnp.float32)
        scores, owns = [], []
        for r in range(rows):
            q = jnp.concatenate(
                [turned[c, pl.ds(r, heads, stride=rows), :] for c in range(parts)], axis=1
            )
            owns.append(jnp.sum(q * new_k[r : r + 1], axis=1, keepdims=True) * scaling)
            row_copies[r].wait()
            scores.append(nt_dot(q.astype(jnp.bfloat16), kept[r, :, :HD]) * scaling)

        for copy in copies[2:] + packs:
            copy.wait()
        pack_out.start()
        lane = lax.broadcasted_iota(jnp.int32, (rows, LANES), 1)
        square = (rows, rows)
        diagonal = lax.broadcasted_iota(jnp.int32, square, 0) == lax.broadcasted_iota(jnp.int32, square, 1)
        skip = lax.axis_index("tp") * (cols - piece)
        for s, u in grid.steps:
            to = grid.target((s, u))
            begin = pl.multiple_of(to * cols + skip, LANES)
            at = width + u * note
            out_refs[s][:, at : at + piece] = res_ref[:, pl.ds(begin, piece)]
            chosen = ids_ref[...] == to * EXPERTS // grid.ep
            across = jnp.sum(jnp.where(chosen, wts_ref[...], 0.0), axis=0, keepdims=True)
            weight = jnp.sum(
                jnp.where(diagonal, jnp.broadcast_to(across, square), 0.0), axis=1, keepdims=True
            )
            high = weight.astype(jnp.bfloat16).astype(jnp.float32)
            middle = (weight - high).astype(jnp.bfloat16).astype(jnp.float32)
            low = weight - high - middle
            tile = jnp.where(lane == 0, high, 0.0)
            tile = jnp.where(lane == 1, middle, tile)
            tile = jnp.where(lane == 2, low, tile)
            out_refs[s][:, at + piece : at + note] = tile.astype(jnp.bfloat16)

        place = lax.broadcasted_iota(jnp.int32, (heads, ctx), 1)
        probs, own_probs = [], []
        for r in range(rows):
            score = jnp.where(place < len_ref[r], scores[r], -jnp.inf)
            peak = jnp.maximum(jnp.max(score, axis=1, keepdims=True), owns[r])
            exps = jnp.exp(score - peak)
            own_exp = jnp.exp(owns[r] - peak)
            denominator = jnp.sum(exps, axis=1, keepdims=True) + own_exp
            probs.append((exps / denominator).astype(jnp.bfloat16))
            own_probs.append((own_exp / denominator).astype(jnp.bfloat16).astype(jnp.float32))
        for r in range(rows):
            mixed = jnp.dot(probs[r], kept[r, :, HD:], preferred_element_type=jnp.float32)
            mixed = mixed + own_probs[r] * new_v[r : r + 1]
            for c in range(parts):
                turned[c, r * heads : (r + 1) * heads, :] = mixed[:, c * LANES : (c + 1) * LANES]
        for h in range(heads):
            for c in range(parts):
                value = turned[c, pl.ds(h, rows, stride=heads), :].astype(jnp.bfloat16)
                begin = h * HD + c * LANES
                for ref in out_refs:
                    ref[:, begin : begin + LANES] = value
        pack_out.wait()

    return pl.pallas_call(
        kernel,
        name="attention",
        out_shape=[shape_of((rows, width + size * note), jnp.bfloat16) for size in sizes]
        + [shape_of((packed_rows, piece), jnp.bfloat16)],
        in_specs=[in_hbm()] * 10,
        out_specs=[vmem()] * len(sizes) + [in_hbm()],
        scratch_shapes=[
            pltpu.VMEM(queries.shape, jnp.bfloat16),
            pltpu.VMEM(new_kv.shape, jnp.bfloat16),
            pltpu.VMEM(residual.shape, jnp.bfloat16),
            pltpu.VMEM(route_ids.shape, jnp.int32),
            pltpu.VMEM(route_weights.shape, jnp.float32),
            pltpu.SMEM(lengths.shape, jnp.int32),
            pltpu.VMEM(cache.shape, jnp.bfloat16),
            pltpu.VMEM((parts, rows * heads, LANES), jnp.float32),
            pltpu.VMEM((packed_rows, piece), jnp.bfloat16),
            pltpu.SemaphoreType.DMA((6,)),
            pltpu.SemaphoreType.DMA((rows,)),
            pltpu.SemaphoreType.DMA((2 * grid.ep + down_blocks + 1,)),
        ],
        compiler_params=params(60),
    )(
        queries,
        new_kv,
        residual,
        route_ids,
        route_weights,
        lengths,
        cache,
        gate_t,
        up_t,
        w_down,
    )


def project(grid, piece, chunks, w_out):
    rows = chunks[0].shape[0]
    depth, cols = w_out.shape
    count = len(chunks)
    tall = rows * count
    blocks = 8
    block = depth // blocks
    note = piece + LANES

    def kernel(*refs):
        chunk_refs, rest = refs[:count], refs[count:]
        w_ref, ours_ref, theirs_ref, weight_ref, stacked, total = rest
        k = pl.program_id(0)

        @pl.when(k == 0)
        def _():
            both = jnp.concatenate([ref[:, :depth] for ref in chunk_refs], axis=0)
            for i in range(blocks):
                stacked[i] = both[:, i * block : (i + 1) * block]

        product = jnp.dot(stacked[k], w_ref[...], preferred_element_type=jnp.float32)

        @pl.when(k == 0)
        def _():
            total[...] = product

        @pl.when(k > 0)
        def _():
            total[...] += product

        @pl.when(k == blocks - 1)
        def _():
            core = lax.axis_index("tp")
            mine = pl.multiple_of(core * (cols - piece), LANES)
            other = pl.multiple_of((1 - core) * (cols - piece), LANES)
            for i, (s, u) in enumerate(grid.steps):
                here = pl.ds(pl.multiple_of(grid.source((s, u)) * rows, rows), rows)
                at = depth + u * note
                beside = chunk_refs[i][:, at : at + note].astype(jnp.float32)
                block_rows = slice(i * rows, (i + 1) * rows)
                ours_ref[here, :] = total[block_rows, pl.ds(mine, piece)] + beside[:, :piece]
                theirs_ref[here, :] = total[block_rows, pl.ds(other, piece)]
                weight_ref[here, :] = jnp.broadcast_to(
                    jnp.sum(beside[:, piece:], axis=1, keepdims=True), (rows, LANES)
                )

    def whole(arr):
        return pl.BlockSpec(arr.shape, lambda k: (0, 0))

    outs = [shape_of((tall, piece), jnp.float32)] * 2 + [shape_of((tall, LANES), jnp.float32)]
    return pl.pallas_call(
        kernel,
        name="project",
        grid=(blocks,),
        out_shape=outs,
        in_specs=[whole(c) for c in chunks] + [pl.BlockSpec((block, cols), lambda k: (k, 0))],
        out_specs=[whole(o) for o in outs],
        scratch_shapes=[
            pltpu.VMEM((blocks, tall, block), jnp.bfloat16),
            pltpu.VMEM((tall, cols), jnp.float32),
        ],
        cost_estimate=pl.CostEstimate(
            flops=2 * tall * depth * cols,
            bytes_accessed=2 * depth * cols + 2 * tall * depth + 8 * tall * piece,
            transcendentals=0,
        ),
        compiler_params=params(48),
    )(*chunks, w_out)


def gate_up(grid, piece, cols, rows, pieces, gain, gate_t, up_t, other):
    tall = pieces[0].shape[0]
    units = gate_t.shape[0]
    count = grid.ep
    dup = 2 * piece - cols
    per_half = count // 2
    sums_width = 4 * units + LANES
    extra = -(-per_half * piece // sums_width)

    def kernel(*refs):
        piece_refs, rest = refs[:count], refs[count:]
        gain_ref, gate_ref, up_ref, other_ref, sums_ref, home_ref, held, home = rest
        home[1] = jnp.zeros((rows, extra * sums_width), jnp.float32)
        core = lax.axis_index("tp")
        me = lax.axis_index("ep")
        fresh = lax.broadcasted_iota(jnp.int32, (tall, piece), 1) >= core * dup
        square = jnp.zeros((tall, 1), jnp.float32)
        own_gate = jnp.zeros((units, tall), jnp.float32)
        own_up = jnp.zeros((units, tall), jnp.float32)
        far = jnp.zeros((2 * units, tall), jnp.float32)
        for i, step in enumerate(grid.steps):
            j = grid.source(step)
            lanes = pl.ds(pl.multiple_of(j * cols + core * (cols - piece), LANES), piece)
            stream = piece_refs[i][...].astype(jnp.float32)
            held[...] = stream
            mine = held[pl.ds(pl.multiple_of(me * rows, rows), rows), :]
            side = lax.rem(j // per_half + core, 2)
            at = pl.multiple_of(lax.rem(j, per_half) * piece, LANES)
            home[side, :, pl.ds(at, piece)] = mine
            stream = jnp.where(fresh, stream, 0.0)
            square = square + jnp.sum(stream * stream, axis=1, keepdims=True)
            scaled = (stream * gain_ref[:, lanes]).astype(jnp.bfloat16)
            own_gate = own_gate + nt_dot(gate_ref[:, lanes], scaled)
            own_up = own_up + nt_dot(up_ref[:, lanes], scaled)
            block = pl.ds(pl.multiple_of(j * 2 * units, 2 * units), 2 * units)
            far = far + nt_dot(other_ref[block, :], scaled)
        sums_ref[:tall, : 4 * units] = jnp.concatenate([own_gate, own_up, far], axis=0).T
        sums_ref[:tall, 4 * units :] = jnp.broadcast_to(square, (tall, LANES))
        for b in range(extra):
            at = tall + b * rows
            sums_ref[at : at + rows, :] = home[1, :, b * sums_width : (b + 1) * sums_width]
        home_ref[...] = home[0, :, : per_half * piece]

    return pl.pallas_call(
        kernel,
        name="gate_up",
        out_shape=[
            shape_of((tall + extra * rows, sums_width), jnp.float32),
            shape_of((rows, per_half * piece), jnp.float32),
        ],
        in_specs=[vmem()] * (count + 4),
        out_specs=[vmem()] * 2,
        scratch_shapes=[
            pltpu.VMEM((tall, piece), jnp.float32),
            pltpu.VMEM((2, rows, extra * sums_width), jnp.float32),
        ],
        compiler_params=params(8),
    )(*pieces, gain, gate_t, up_t, other)


def down(grid, piece, rows, sums, far_sums, weight, w_down, far_weights):
    tall = weight.shape[0]
    units, width = w_down.shape
    out_width = width // 2
    count = grid.ep

    def kernel(sums_ref, far_ref, weight_ref, down_ref, packed_ref, *rest):
        out_refs, total, down_half, sem = rest[:count], rest[count], rest[count + 1], rest[count + 2]
        begin = pl.multiple_of(lax.axis_index("tp") * out_width, LANES)
        copy = pltpu.make_async_copy(down_ref.at[:, pl.ds(begin, out_width)], down_half, sem)
        copy.start()
        square = (
            sums_ref[:tall, 4 * units : 4 * units + 1] + far_ref[:tall, 4 * units : 4 * units + 1]
        )
        scale = lax.rsqrt(square / width + 1e-06)

        def hidden(a, b):
            both = (
                sums_ref[:tall, a * units : (a + 2) * units]
                + far_ref[:tall, b * units : (b + 2) * units]
            )
            gate, up = both[:, :units] * scale, both[:, units:] * scale
            return (gate / (1.0 + jnp.exp(-gate)) * up).astype(jnp.bfloat16)

        near, far = hidden(0, 2), hidden(2, 0)
        copy.wait()
        for b in range(out_width // piece):
            span = slice(b * piece, (b + 1) * piece)
            block = slice((2 * count + b) * units, (2 * count + b + 1) * units)
            value = jnp.dot(near, down_half[:, span], preferred_element_type=jnp.float32)
            value = value + jnp.dot(far, packed_ref[block, :], preferred_element_type=jnp.float32)
            total[:, span] = value * weight_ref[:, :1]
        for i, step in enumerate(grid.steps):
            there = pl.ds(pl.multiple_of(grid.target(step) * rows, rows), rows)
            out_refs[i][...] = total[there, :].astype(out_refs[i].dtype)

    return pl.pallas_call(
        kernel,
        name="down",
        out_shape=[
            shape_of((rows, out_width), jnp.bfloat16 if i else jnp.float32) for i in range(count)
        ],
        in_specs=[vmem()] * 3 + [pl.BlockSpec(memory_space=pl.ANY), vmem()],
        out_specs=[vmem()] * count,
        scratch_shapes=[
            pltpu.VMEM((tall, out_width), jnp.float32),
            pltpu.VMEM((units, out_width), jnp.bfloat16),
            pltpu.SemaphoreType.DMA(()),
        ],
        compiler_params=params(8),
    )(sums, far_sums, weight, w_down, far_weights)


def finish(piece, cols, near, far_sums, parts):
    rows, out_width = parts[0].shape
    extra = -(-near.shape[1] // far_sums.shape[1])
    top = far_sums.shape[0] - extra * rows
    dup = 2 * piece - cols

    def kernel(near_ref, far_ref, *rest):
        part_refs, out_ref = rest[:-1], rest[-1]
        first = lax.axis_index("tp") == 0
        far = jnp.concatenate(
            [far_ref[top + b * rows : top + (b + 1) * rows, :] for b in range(extra)], axis=1
        )
        for c in range(out_width // cols):
            span = slice(c * piece, (c + 1) * piece)
            a, b = near_ref[:, span], far[:, span]
            low = jnp.where(first, a, b)
            high = jnp.where(first, b, a)[:, dup:]
            value = jnp.concatenate([low, high], axis=1)
            for ref in part_refs:
                value = value + ref[:, c * cols : (c + 1) * cols].astype(jnp.float32)
            out_ref[:, c * cols : (c + 1) * cols] = value.astype(jnp.bfloat16)

    return pl.pallas_call(
        kernel,
        name="finish",
        out_shape=shape_of((rows, out_width), jnp.bfloat16),
        in_specs=[vmem()] * (2 + len(parts)),
        out_specs=vmem(),
        compiler_params=params(4),
    )(near, far_sums, *parts)


def tuned_body(
    grid,
    residual,
    queries,
    new_kv,
    cache,
    lengths,
    w_out,
    gain,
    route_ids,
    route_weights,
    w_gate,
    w_up,
    w_down,
):
    rows, width = residual.shape
    cols = w_out.shape[1]
    piece = -(-cols // (2 * LANES)) * LANES
    gate_t, up_t = w_gate.T, w_up.T
    *outgoing, packed = attention(
        grid,
        piece,
        cols,
        queries,
        new_kv,
        cache,
        lengths,
        residual,
        route_ids.T,
        route_weights.T,
        gate_t,
        up_t,
        w_down,
    )
    chunks = grid.spread(outgoing, spaced=True)
    packed, *_ = lax.optimization_barrier((packed, *chunks))
    far_weights = swap(packed)
    ours, theirs, weight = project(grid, piece, chunks, w_out)
    stream = (ours + swap(theirs)).astype(jnp.bfloat16)
    stream, far_weights = lax.optimization_barrier((stream, far_weights))
    pieces = grid.spread([stream] * grid.z, spaced=False)
    sums, home = gate_up(
        grid, piece, cols, rows, pieces, gain.reshape(1, width), gate_t, up_t, far_weights
    )
    far_sums = swap(sums)
    parts = down(grid, piece, rows, sums, far_sums, weight, w_down, far_weights)
    order = sorted(range(grid.ep), key=lambda i: (grid.steps[i][0] == 0, grid.steps[i][0] != 2))
    shares = [grid.send(parts[i], *grid.steps[i]) if any(grid.steps[i]) else parts[i] for i in order]
    return finish(piece, cols, home, far_sums, shares)


def general_body(
    residual,
    queries,
    new_kv,
    cache,
    lengths,
    w_out,
    gain,
    route_ids,
    route_weights,
    w_gate,
    w_up,
    w_down,
):
    row_count = queries.shape[0]
    head_count = queries.shape[1] // HD
    scaling = HD ** (-0.5)
    query_heads = queries.reshape(row_count, head_count, HD)
    key_rows = cache[:, :, :HD]
    value_rows = cache[:, :, HD:]
    scores = (
        jnp.einsum("rhd,rpd->rhp", query_heads, key_rows, preferred_element_type=jnp.float32)
        * scaling
    )
    usable = jnp.arange(cache.shape[1], dtype=jnp.int32)[None, :] < lengths[:, None]
    scores = jnp.where(usable[:, None, :], scores, -jnp.inf)
    own_score = (
        jnp.einsum("rhd,rd->rh", query_heads, new_kv[:, :HD], preferred_element_type=jnp.float32)
        * scaling
    )
    peak_score = jnp.maximum(jnp.max(scores, axis=2), own_score)
    cache_weight = jnp.exp(scores - peak_score[:, :, None])
    own_weight = jnp.exp(own_score - peak_score)
    denominator = jnp.sum(cache_weight, axis=2) + own_weight
    probabilities = (cache_weight / denominator[:, :, None]).astype(jnp.bfloat16)
    own_prob = (own_weight / denominator).astype(jnp.bfloat16)
    context = jnp.einsum(
        "rhp,rpd->rhd", probabilities, value_rows, preferred_element_type=jnp.float32
    )
    context = context + own_prob.astype(jnp.float32)[:, :, None] * new_kv[:, None, HD:].astype(
        jnp.float32
    )
    context = context.astype(jnp.bfloat16).reshape(row_count, head_count * HD)
    attn_cols = jnp.dot(
        lax.all_gather(context, "ep", axis=0, tiled=True), w_out, preferred_element_type=jnp.float32
    )
    attn_rows = lax.all_to_all(attn_cols, "ep", split_axis=0, concat_axis=1, tiled=True)
    attention = lax.psum(attn_rows, "tp")
    stream = residual.astype(jnp.float32) + attention
    mean_square = jnp.mean(stream * stream, axis=1, keepdims=True)
    normed = (stream * lax.rsqrt(mean_square + 1e-06) * gain[None, :]).astype(jnp.bfloat16)
    width = normed.shape[1]
    ep_size = lax.axis_size("ep")
    members = ep_size // EXPERTS
    slot_count = EXPERTS * CAP
    flat_ids = route_ids.reshape(-1)
    one_hot = (flat_ids[:, None] == jnp.arange(EXPERTS, dtype=jnp.int32)[None, :]).astype(jnp.int32)
    earlier = jnp.cumsum(one_hot, axis=0) - one_hot
    slot_index = jnp.sum(earlier * one_hot, axis=1)
    target = (flat_ids * CAP + slot_index).reshape(row_count, TOPK)
    placed = (target[:, :, None] == jnp.arange(slot_count, dtype=jnp.int32)[None, None, :]).astype(
        jnp.float32
    )
    chosen = jnp.sum(placed, axis=1).reshape(row_count, EXPERTS, CAP).astype(jnp.bfloat16)
    mixing = jnp.sum(placed * route_weights[:, :, None], axis=1).reshape(row_count, EXPERTS, CAP)
    outgoing = jnp.einsum("rec,rd->ecd", chosen, normed, preferred_element_type=jnp.float32).astype(
        jnp.bfloat16
    )
    outgoing = jnp.broadcast_to(outgoing[:, None], (EXPERTS, members, CAP, width)).reshape(
        ep_size * CAP, width
    )
    arrived = lax.all_to_all(outgoing, "ep", split_axis=0, concat_axis=0, tiled=True)
    gate_act = jnp.dot(arrived, w_gate, preferred_element_type=jnp.float32)
    up_act = jnp.dot(arrived, w_up, preferred_element_type=jnp.float32)
    hidden = (jax.nn.silu(gate_act) * up_act).astype(jnp.bfloat16)
    partial_value = jnp.dot(hidden, w_down, preferred_element_type=jnp.float32)
    halves = lax.psum_scatter(partial_value, "tp", scatter_dimension=1, tiled=True)
    returned = lax.all_to_all(halves, "ep", split_axis=0, concat_axis=0, tiled=True)
    returned = returned.reshape(EXPERTS, members, CAP, returned.shape[1])
    mixed = jnp.einsum("rec,egcw->rw", mixing, returned, precision=lax.Precision.HIGHEST)
    tp_start = lax.axis_index("tp") * mixed.shape[1]
    stream_part = lax.dynamic_slice_in_dim(stream, tp_start, mixed.shape[1], 1)
    return (stream_part + mixed).astype(jnp.bfloat16)


def body(*args):
    ep_size, cols, heads_width = lax.axis_size("ep"), args[5].shape[1], args[5].shape[0]
    if ep_size == 8 and lax.axis_size("tp") == 2 and cols % LANES == 0 and heads_width % (8 * HD) == 0:
        return tuned_body(Grid(ep_size), *args)
    return general_body(*args)


def solution(mesh):
    placed = (
        P(("grp", "ep"), None),
        P(("grp", "ep"), "tp"),
        P(("grp", "ep"), None),
        P(("grp", "ep"), None, None),
        P(("grp", "ep")),
        P("tp", "ep"),
        P(),
        P(("grp", "ep"), None),
        P(("grp", "ep"), None),
        P(None, ("ep", "tp")),
        P(None, ("ep", "tp")),
        P(("ep", "tp"), None),
    )
    return jax.shard_map(
        body, mesh=mesh, in_specs=placed, out_specs=P(("grp", "ep"), "tp"), check_vma=False
    )
```

```python
import functools

import jax
import jax.numpy as jnp
from jax import lax
from jax.experimental import pallas as pl
from jax.experimental.pallas import tpu as pltpu
from jax.sharding import PartitionSpec as P

HD = 256
TOPK = 3
EXPERTS = 4
CAP = 8
LANES = 128


def params(mebibytes):
    return pltpu.CompilerParams(vmem_limit_bytes=mebibytes * 1024 * 1024)


def vmem():
    return pl.BlockSpec(memory_space=pltpu.VMEM)


def anywhere():
    return pl.BlockSpec(memory_space=pl.ANY)


def shape_of(shape, dtype):
    return jax.ShapeDtypeStruct(shape, dtype)


class Grid:
    def __init__(self, ep_size):
        self.ep, self.x, self.z = ep_size, ep_size // 4, 4
        self.steps = [(s, u) for s in range(self.z) for u in range(self.x)]

    def send(self, arr, s, u):
        pairs = [
            (z * self.x + x, (z ^ s) * self.x + (x + u) % self.x)
            for z in range(self.z)
            for x in range(self.x)
        ]
        return lax.ppermute(arr, "ep", pairs)

    def along_x(self, got, s):
        for u in range(1, self.x):
            got[s, u] = self.send(got[s, 0], 0, u)

    def spread(self, own, spaced):
        got = {(0, 0): own[0]}
        got[1, 0] = self.send(own[1], 1, 0)
        got[3, 0] = self.send(own[3], 3, 0)
        self.along_x(got, 0)
        far = own[2]
        if spaced:
            far, *_ = lax.optimization_barrier((far, got[1, 0], got[0, self.x - 1]))
        got[2, 0] = self.send(far, 2, 0)
        self.along_x(got, 1)
        self.along_x(got, 3)
        if not spaced:
            got[2, 0], *_ = lax.optimization_barrier((got[2, 0], got[1, self.x - 1]))
        self.along_x(got, 2)
        return [got[step] for step in self.steps]

    def source(self, step):
        me = lax.axis_index("ep")
        z = (me // self.x) ^ step[0]
        return z * self.x + lax.rem(lax.rem(me, self.x) - step[1] + self.x, self.x)

    def target(self, step):
        return self.source((step[0], -step[1] % self.x))


def swap(arr):
    return lax.ppermute(arr, "tp", [(0, 1), (1, 0)])


def nt_dot(a, b):
    return lax.dot_general(a, b, (((1,), (1,)), ((), ())), preferred_element_type=jnp.float32)


def in_hbm():
    return pl.BlockSpec(memory_space=pltpu.HBM)


def attention(
    grid,
    piece,
    cols,
    queries,
    new_kv,
    cache,
    lengths,
    residual,
    route_ids,
    route_weights,
    gate_t,
    up_t,
    w_down,
):
    rows, width = queries.shape
    heads = width // HD
    ctx = cache.shape[1]
    parts = HD // LANES
    sizes = [grid.x] * grid.z
    note = piece + LANES
    scaling = HD ** (-0.5)
    units, features = gate_t.shape
    out_width = features // 2
    down_blocks = out_width // piece
    packed_rows = (2 * grid.ep + down_blocks) * units

    def kernel(*refs):
        sources, rest = refs[:7], refs[7:]
        gate_ref, up_ref, down_ref, rest = rest[0], rest[1], rest[2], rest[3:]
        out_refs, pack_ref, rest = rest[: len(sizes)], rest[len(sizes)], rest[len(sizes) + 1 :]
        q_ref, kv_ref, res_ref, ids_ref, wts_ref, len_ref, kept, turned, packed, sems, row_sems, pack_sems = rest
        cache_ref = sources[6]
        copies = [
            pltpu.make_async_copy(src, dst, sems.at[i])
            for i, (src, dst) in enumerate(
                zip(sources[:6], (q_ref, kv_ref, res_ref, ids_ref, wts_ref, len_ref))
            )
        ]
        row_copies = [
            pltpu.make_async_copy(cache_ref.at[r], kept.at[r], row_sems.at[r]) for r in range(rows)
        ]
        other = 1 - lax.axis_index("tp")
        blocks = []
        for j in range(grid.ep):
            begin = pl.multiple_of(j * cols + other * (cols - piece), LANES)
            blocks += [ref.at[:, pl.ds(begin, piece)] for ref in (gate_ref, up_ref)]
        for b in range(down_blocks):
            begin = pl.multiple_of(other * out_width + b * piece, LANES)
            blocks.append(down_ref.at[:, pl.ds(begin, piece)])
        packs = [
            pltpu.make_async_copy(block, packed.at[pl.ds(i * units, units), :], pack_sems.at[i])
            for i, block in enumerate(blocks)
        ]
        pack_out = pltpu.make_async_copy(packed, pack_ref, pack_sems.at[len(blocks)])
        for copy in copies[:2] + row_copies + copies[2:] + packs:
            copy.start()

        copies[0].wait()
        copies[1].wait()
        for h in range(heads):
            for c in range(parts):
                at = h * HD + c * LANES
                turned[c, h * rows : (h + 1) * rows, :] = q_ref[:, at : at + LANES].astype(jnp.float32)
        new_k = kv_ref[:, :HD].astype(jnp.float32)
        new_v = kv_ref[:, HD:].astype(jnp.float32)
        scores, owns = [], []
        for r in range(rows):
            q = jnp.concatenate(
                [turned[c, pl.ds(r, heads, stride=rows), :] for c in range(parts)], axis=1
            )
            owns.append(jnp.sum(q * new_k[r : r + 1], axis=1, keepdims=True) * scaling)
            row_copies[r].wait()
            scores.append(nt_dot(q.astype(jnp.bfloat16), kept[r, :, :HD]) * scaling)

        for copy in copies[2:] + packs:
            copy.wait()
        pack_out.start()
        lane = lax.broadcasted_iota(jnp.int32, (rows, LANES), 1)
        square = (rows, rows)
        diagonal = lax.broadcasted_iota(jnp.int32, square, 0) == lax.broadcasted_iota(jnp.int32, square, 1)
        skip = lax.axis_index("tp") * (cols - piece)
        for s, u in grid.steps:
            to = grid.target((s, u))
            begin = pl.multiple_of(to * cols + skip, LANES)
            at = width + u * note
            out_refs[s][:, at : at + piece] = res_ref[:, pl.ds(begin, piece)]
            chosen = ids_ref[...] == to * EXPERTS // grid.ep
            across = jnp.sum(jnp.where(chosen, wts_ref[...], 0.0), axis=0, keepdims=True)
            weight = jnp.sum(
                jnp.where(diagonal, jnp.broadcast_to(across, square), 0.0), axis=1, keepdims=True
            )
            high = weight.astype(jnp.bfloat16).astype(jnp.float32)
            middle = (weight - high).astype(jnp.bfloat16).astype(jnp.float32)
            low = weight - high - middle
            tile = jnp.where(lane == 0, high, 0.0)
            tile = jnp.where(lane == 1, middle, tile)
            tile = jnp.where(lane == 2, low, tile)
            out_refs[s][:, at + piece : at + note] = tile.astype(jnp.bfloat16)

        place = lax.broadcasted_iota(jnp.int32, (heads, ctx), 1)
        probs, own_probs = [], []
        for r in range(rows):
            score = jnp.where(place < len_ref[r], scores[r], -jnp.inf)
            peak = jnp.maximum(jnp.max(score, axis=1, keepdims=True), owns[r])
            exps = jnp.exp(score - peak)
            own_exp = jnp.exp(owns[r] - peak)
            denominator = jnp.sum(exps, axis=1, keepdims=True) + own_exp
            probs.append((exps / denominator).astype(jnp.bfloat16))
            own_probs.append((own_exp / denominator).astype(jnp.bfloat16).astype(jnp.float32))
        for r in range(rows):
            mixed = jnp.dot(probs[r], kept[r, :, HD:], preferred_element_type=jnp.float32)
            mixed = mixed + own_probs[r] * new_v[r : r + 1]
            for c in range(parts):
                turned[c, r * heads : (r + 1) * heads, :] = mixed[:, c * LANES : (c + 1) * LANES]
        for h in range(heads):
            for c in range(parts):
                value = turned[c, pl.ds(h, rows, stride=heads), :].astype(jnp.bfloat16)
                begin = h * HD + c * LANES
                for ref in out_refs:
                    ref[:, begin : begin + LANES] = value
        pack_out.wait()

    return pl.pallas_call(
        kernel,
        name="attention",
        out_shape=[shape_of((rows, width + size * note), jnp.bfloat16) for size in sizes]
        + [shape_of((packed_rows, piece), jnp.bfloat16)],
        in_specs=[in_hbm()] * 10,
        out_specs=[vmem()] * len(sizes) + [in_hbm()],
        scratch_shapes=[
            pltpu.VMEM(queries.shape, jnp.bfloat16),
            pltpu.VMEM(new_kv.shape, jnp.bfloat16),
            pltpu.VMEM(residual.shape, jnp.bfloat16),
            pltpu.VMEM(route_ids.shape, jnp.int32),
            pltpu.VMEM(route_weights.shape, jnp.float32),
            pltpu.SMEM(lengths.shape, jnp.int32),
            pltpu.VMEM(cache.shape, jnp.bfloat16),
            pltpu.VMEM((parts, rows * heads, LANES), jnp.float32),
            pltpu.VMEM((packed_rows, piece), jnp.bfloat16),
            pltpu.SemaphoreType.DMA((6,)),
            pltpu.SemaphoreType.DMA((rows,)),
            pltpu.SemaphoreType.DMA((2 * grid.ep + down_blocks + 1,)),
        ],
        compiler_params=params(60),
    )(
        queries,
        new_kv,
        residual,
        route_ids,
        route_weights,
        lengths,
        cache,
        gate_t,
        up_t,
        w_down,
    )


def project(grid, piece, chunks, w_out):
    rows = chunks[0].shape[0]
    depth, cols = w_out.shape
    count = len(chunks)
    tall = rows * count
    blocks = 8
    block = depth // blocks
    note = piece + LANES

    def kernel(*refs):
        chunk_refs, rest = refs[:count], refs[count:]
        w_ref, ours_ref, theirs_ref, weight_ref, stacked, total = rest
        k = pl.program_id(0)

        @pl.when(k == 0)
        def _():
            both = jnp.concatenate([ref[:, :depth] for ref in chunk_refs], axis=0)
            for i in range(blocks):
                stacked[i] = both[:, i * block : (i + 1) * block]

        product = jnp.dot(stacked[k], w_ref[...], preferred_element_type=jnp.float32)

        @pl.when(k == 0)
        def _():
            total[...] = product

        @pl.when(k > 0)
        def _():
            total[...] += product

        @pl.when(k == blocks - 1)
        def _():
            core = lax.axis_index("tp")
            mine = pl.multiple_of(core * (cols - piece), LANES)
            other = pl.multiple_of((1 - core) * (cols - piece), LANES)
            for i, (s, u) in enumerate(grid.steps):
                here = pl.ds(pl.multiple_of(grid.source((s, u)) * rows, rows), rows)
                at = depth + u * note
                beside = chunk_refs[i][:, at : at + note].astype(jnp.float32)
                block_rows = slice(i * rows, (i + 1) * rows)
                ours_ref[here, :] = total[block_rows, pl.ds(mine, piece)] + beside[:, :piece]
                theirs_ref[here, :] = total[block_rows, pl.ds(other, piece)]
                weight_ref[here, :] = jnp.broadcast_to(
                    jnp.sum(beside[:, piece:], axis=1, keepdims=True), (rows, LANES)
                )

    def whole(arr):
        return pl.BlockSpec(arr.shape, lambda k: (0, 0))

    outs = [shape_of((tall, piece), jnp.float32)] * 2 + [shape_of((tall, LANES), jnp.float32)]
    return pl.pallas_call(
        kernel,
        name="project",
        grid=(blocks,),
        out_shape=outs,
        in_specs=[whole(c) for c in chunks] + [pl.BlockSpec((block, cols), lambda k: (k, 0))],
        out_specs=[whole(o) for o in outs],
        scratch_shapes=[
            pltpu.VMEM((blocks, tall, block), jnp.bfloat16),
            pltpu.VMEM((tall, cols), jnp.float32),
        ],
        cost_estimate=pl.CostEstimate(
            flops=2 * tall * depth * cols,
            bytes_accessed=2 * depth * cols + 2 * tall * depth + 8 * tall * piece,
            transcendentals=0,
        ),
        compiler_params=params(48),
    )(*chunks, w_out)


def gate_up(grid, piece, cols, rows, pieces, gain, gate_t, up_t, other):
    tall = pieces[0].shape[0]
    units = gate_t.shape[0]
    count = grid.ep
    dup = 2 * piece - cols
    per_half = count // 2
    sums_width = 4 * units + LANES
    extra = -(-per_half * piece // sums_width)

    def kernel(*refs):
        piece_refs, rest = refs[:count], refs[count:]
        gain_ref, gate_ref, up_ref, other_ref, sums_ref, home_ref, held, home = rest
        home[1] = jnp.zeros((rows, extra * sums_width), jnp.float32)
        core = lax.axis_index("tp")
        me = lax.axis_index("ep")
        fresh = lax.broadcasted_iota(jnp.int32, (tall, piece), 1) >= core * dup
        square = jnp.zeros((tall, 1), jnp.float32)
        own_gate = jnp.zeros((units, tall), jnp.float32)
        own_up = jnp.zeros((units, tall), jnp.float32)
        far = jnp.zeros((2 * units, tall), jnp.float32)
        for i, step in enumerate(grid.steps):
            j = grid.source(step)
            lanes = pl.ds(pl.multiple_of(j * cols + core * (cols - piece), LANES), piece)
            stream = piece_refs[i][...].astype(jnp.float32)
            held[...] = stream
            mine = held[pl.ds(pl.multiple_of(me * rows, rows), rows), :]
            side = lax.rem(j // per_half + core, 2)
            at = pl.multiple_of(lax.rem(j, per_half) * piece, LANES)
            home[side, :, pl.ds(at, piece)] = mine
            stream = jnp.where(fresh, stream, 0.0)
            square = square + jnp.sum(stream * stream, axis=1, keepdims=True)
            scaled = (stream * gain_ref[:, lanes]).astype(jnp.bfloat16)
            own_gate = own_gate + nt_dot(gate_ref[:, lanes], scaled)
            own_up = own_up + nt_dot(up_ref[:, lanes], scaled)
            block = pl.ds(pl.multiple_of(j * 2 * units, 2 * units), 2 * units)
            far = far + nt_dot(other_ref[block, :], scaled)
        sums_ref[:tall, : 4 * units] = jnp.concatenate([own_gate, own_up, far], axis=0).T
        sums_ref[:tall, 4 * units :] = jnp.broadcast_to(square, (tall, LANES))
        for b in range(extra):
            at = tall + b * rows
            sums_ref[at : at + rows, :] = home[1, :, b * sums_width : (b + 1) * sums_width]
        home_ref[...] = home[0, :, : per_half * piece]

    return pl.pallas_call(
        kernel,
        name="gate_up",
        out_shape=[
            shape_of((tall + extra * rows, sums_width), jnp.float32),
            shape_of((rows, per_half * piece), jnp.float32),
        ],
        in_specs=[vmem()] * (count + 4),
        out_specs=[vmem()] * 2,
        scratch_shapes=[
            pltpu.VMEM((tall, piece), jnp.float32),
            pltpu.VMEM((2, rows, extra * sums_width), jnp.float32),
        ],
        compiler_params=params(8),
    )(*pieces, gain, gate_t, up_t, other)


def down(grid, piece, rows, sums, far_sums, weight, w_down, far_weights):
    tall = weight.shape[0]
    units, width = w_down.shape
    out_width = width // 2
    count = grid.ep

    def kernel(sums_ref, far_ref, weight_ref, down_ref, packed_ref, *rest):
        out_refs, total, down_half, sem = rest[:count], rest[count], rest[count + 1], rest[count + 2]
        begin = pl.multiple_of(lax.axis_index("tp") * out_width, LANES)
        copy = pltpu.make_async_copy(down_ref.at[:, pl.ds(begin, out_width)], down_half, sem)
        copy.start()
        square = (
            sums_ref[:tall, 4 * units : 4 * units + 1] + far_ref[:tall, 4 * units : 4 * units + 1]
        )
        scale = lax.rsqrt(square / width + 1e-06)

        def hidden(a, b):
            both = (
                sums_ref[:tall, a * units : (a + 2) * units]
                + far_ref[:tall, b * units : (b + 2) * units]
            )
            gate, up = both[:, :units] * scale, both[:, units:] * scale
            return (gate / (1.0 + jnp.exp(-gate)) * up).astype(jnp.bfloat16)

        near, far = hidden(0, 2), hidden(2, 0)
        copy.wait()
        for b in range(out_width // piece):
            span = slice(b * piece, (b + 1) * piece)
            block = slice((2 * count + b) * units, (2 * count + b + 1) * units)
            value = jnp.dot(near, down_half[:, span], preferred_element_type=jnp.float32)
            value = value + jnp.dot(far, packed_ref[block, :], preferred_element_type=jnp.float32)
            total[:, span] = value * weight_ref[:, :1]
        for i, step in enumerate(grid.steps):
            there = pl.ds(pl.multiple_of(grid.target(step) * rows, rows), rows)
            out_refs[i][...] = total[there, :].astype(out_refs[i].dtype)

    return pl.pallas_call(
        kernel,
        name="down",
        out_shape=[
            shape_of((rows, out_width), jnp.bfloat16 if i else jnp.float32) for i in range(count)
        ],
        in_specs=[vmem()] * 3 + [pl.BlockSpec(memory_space=pl.ANY), vmem()],
        out_specs=[vmem()] * count,
        scratch_shapes=[
            pltpu.VMEM((tall, out_width), jnp.float32),
            pltpu.VMEM((units, out_width), jnp.bfloat16),
            pltpu.SemaphoreType.DMA(()),
        ],
        compiler_params=params(8),
    )(sums, far_sums, weight, w_down, far_weights)


def finish(piece, cols, near, far_sums, parts):
    rows, out_width = parts[0].shape
    extra = -(-near.shape[1] // far_sums.shape[1])
    top = far_sums.shape[0] - extra * rows
    dup = 2 * piece - cols

    def kernel(near_ref, far_ref, *rest):
        part_refs, out_ref = rest[:-1], rest[-1]
        first = lax.axis_index("tp") == 0
        far = jnp.concatenate(
            [far_ref[top + b * rows : top + (b + 1) * rows, :] for b in range(extra)], axis=1
        )
        for c in range(out_width // cols):
            span = slice(c * piece, (c + 1) * piece)
            a, b = near_ref[:, span], far[:, span]
            low = jnp.where(first, a, b)
            high = jnp.where(first, b, a)[:, dup:]
            value = jnp.concatenate([low, high], axis=1)
            for ref in part_refs:
                value = value + ref[:, c * cols : (c + 1) * cols].astype(jnp.float32)
            out_ref[:, c * cols : (c + 1) * cols] = value.astype(jnp.bfloat16)

    return pl.pallas_call(
        kernel,
        name="finish",
        out_shape=shape_of((rows, out_width), jnp.bfloat16),
        in_specs=[vmem()] * (2 + len(parts)),
        out_specs=vmem(),
        compiler_params=params(4),
    )(near, far_sums, *parts)


def tuned_body(
    grid,
    residual,
    queries,
    new_kv,
    cache,
    lengths,
    w_out,
    gain,
    route_ids,
    route_weights,
    w_gate,
    w_up,
    w_down,
):
    rows, width = residual.shape
    cols = w_out.shape[1]
    piece = -(-cols // (2 * LANES)) * LANES
    gate_t, up_t = w_gate.T, w_up.T
    *outgoing, packed = attention(
        grid,
        piece,
        cols,
        queries,
        new_kv,
        cache,
        lengths,
        residual,
        route_ids.T,
        route_weights.T,
        gate_t,
        up_t,
        w_down,
    )
    chunks = grid.spread(outgoing, spaced=True)
    packed, *_ = lax.optimization_barrier((packed, *chunks))
    far_weights = swap(packed)
    ours, theirs, weight = project(grid, piece, chunks, w_out)
    stream = (ours + swap(theirs)).astype(jnp.bfloat16)
    stream, far_weights = lax.optimization_barrier((stream, far_weights))
    pieces = grid.spread([stream] * grid.z, spaced=False)
    sums, home = gate_up(
        grid, piece, cols, rows, pieces, gain.reshape(1, width), gate_t, up_t, far_weights
    )
    far_sums = swap(sums)
    parts = down(grid, piece, rows, sums, far_sums, weight, w_down, far_weights)
    order = sorted(range(grid.ep), key=lambda i: (grid.steps[i] == (0, 0), -grid.steps[i][0]))
    shares = [grid.send(parts[i], *grid.steps[i]) if any(grid.steps[i]) else parts[i] for i in order]
    return finish(piece, cols, home, far_sums, shares)


def general_body(
    residual,
    queries,
    new_kv,
    cache,
    lengths,
    w_out,
    gain,
    route_ids,
    route_weights,
    w_gate,
    w_up,
    w_down,
):
    row_count = queries.shape[0]
    head_count = queries.shape[1] // HD
    scaling = HD ** (-0.5)
    query_heads = queries.reshape(row_count, head_count, HD)
    key_rows = cache[:, :, :HD]
    value_rows = cache[:, :, HD:]
    scores = (
        jnp.einsum("rhd,rpd->rhp", query_heads, key_rows, preferred_element_type=jnp.float32)
        * scaling
    )
    usable = jnp.arange(cache.shape[1], dtype=jnp.int32)[None, :] < lengths[:, None]
    scores = jnp.where(usable[:, None, :], scores, -jnp.inf)
    own_score = (
        jnp.einsum("rhd,rd->rh", query_heads, new_kv[:, :HD], preferred_element_type=jnp.float32)
        * scaling
    )
    peak_score = jnp.maximum(jnp.max(scores, axis=2), own_score)
    cache_weight = jnp.exp(scores - peak_score[:, :, None])
    own_weight = jnp.exp(own_score - peak_score)
    denominator = jnp.sum(cache_weight, axis=2) + own_weight
    probabilities = (cache_weight / denominator[:, :, None]).astype(jnp.bfloat16)
    own_prob = (own_weight / denominator).astype(jnp.bfloat16)
    context = jnp.einsum(
        "rhp,rpd->rhd", probabilities, value_rows, preferred_element_type=jnp.float32
    )
    context = context + own_prob.astype(jnp.float32)[:, :, None] * new_kv[:, None, HD:].astype(
        jnp.float32
    )
    context = context.astype(jnp.bfloat16).reshape(row_count, head_count * HD)
    attn_cols = jnp.dot(
        lax.all_gather(context, "ep", axis=0, tiled=True), w_out, preferred_element_type=jnp.float32
    )
    attn_rows = lax.all_to_all(attn_cols, "ep", split_axis=0, concat_axis=1, tiled=True)
    attention = lax.psum(attn_rows, "tp")
    stream = residual.astype(jnp.float32) + attention
    mean_square = jnp.mean(stream * stream, axis=1, keepdims=True)
    normed = (stream * lax.rsqrt(mean_square + 1e-06) * gain[None, :]).astype(jnp.bfloat16)
    width = normed.shape[1]
    ep_size = lax.axis_size("ep")
    members = ep_size // EXPERTS
    slot_count = EXPERTS * CAP
    flat_ids = route_ids.reshape(-1)
    one_hot = (flat_ids[:, None] == jnp.arange(EXPERTS, dtype=jnp.int32)[None, :]).astype(jnp.int32)
    earlier = jnp.cumsum(one_hot, axis=0) - one_hot
    slot_index = jnp.sum(earlier * one_hot, axis=1)
    target = (flat_ids * CAP + slot_index).reshape(row_count, TOPK)
    placed = (target[:, :, None] == jnp.arange(slot_count, dtype=jnp.int32)[None, None, :]).astype(
        jnp.float32
    )
    chosen = jnp.sum(placed, axis=1).reshape(row_count, EXPERTS, CAP).astype(jnp.bfloat16)
    mixing = jnp.sum(placed * route_weights[:, :, None], axis=1).reshape(row_count, EXPERTS, CAP)
    outgoing = jnp.einsum("rec,rd->ecd", chosen, normed, preferred_element_type=jnp.float32).astype(
        jnp.bfloat16
    )
    outgoing = jnp.broadcast_to(outgoing[:, None], (EXPERTS, members, CAP, width)).reshape(
        ep_size * CAP, width
    )
    arrived = lax.all_to_all(outgoing, "ep", split_axis=0, concat_axis=0, tiled=True)
    gate_act = jnp.dot(arrived, w_gate, preferred_element_type=jnp.float32)
    up_act = jnp.dot(arrived, w_up, preferred_element_type=jnp.float32)
    hidden = (jax.nn.silu(gate_act) * up_act).astype(jnp.bfloat16)
    partial_value = jnp.dot(hidden, w_down, preferred_element_type=jnp.float32)
    halves = lax.psum_scatter(partial_value, "tp", scatter_dimension=1, tiled=True)
    returned = lax.all_to_all(halves, "ep", split_axis=0, concat_axis=0, tiled=True)
    returned = returned.reshape(EXPERTS, members, CAP, returned.shape[1])
    mixed = jnp.einsum("rec,egcw->rw", mixing, returned, precision=lax.Precision.HIGHEST)
    tp_start = lax.axis_index("tp") * mixed.shape[1]
    stream_part = lax.dynamic_slice_in_dim(stream, tp_start, mixed.shape[1], 1)
    return (stream_part + mixed).astype(jnp.bfloat16)


def body(*args):
    ep_size, cols, heads_width = lax.axis_size("ep"), args[5].shape[1], args[5].shape[0]
    if ep_size == 8 and lax.axis_size("tp") == 2 and cols % LANES == 0 and heads_width % (8 * HD) == 0:
        return tuned_body(Grid(ep_size), *args)
    return general_body(*args)


def solution(mesh):
    placed = (
        P(("grp", "ep"), None),
        P(("grp", "ep"), "tp"),
        P(("grp", "ep"), None),
        P(("grp", "ep"), None, None),
        P(("grp", "ep")),
        P("tp", "ep"),
        P(),
        P(("grp", "ep"), None),
        P(("grp", "ep"), None),
        P(None, ("ep", "tp")),
        P(None, ("ep", "tp")),
        P(("ep", "tp"), None),
    )
    return jax.shard_map(
        body, mesh=mesh, in_specs=placed, out_specs=P(("grp", "ep"), "tp"), check_vma=False
    )
```

```python
import functools

import jax
import jax.numpy as jnp
from jax import lax
from jax.experimental import pallas as pl
from jax.experimental.pallas import tpu as pltpu
from jax.sharding import PartitionSpec as P

HD = 256
TOPK = 3
EXPERTS = 4
CAP = 8
LANES = 128


def params(mebibytes):
    return pltpu.CompilerParams(vmem_limit_bytes=mebibytes * 1024 * 1024)


def vmem():
    return pl.BlockSpec(memory_space=pltpu.VMEM)


def anywhere():
    return pl.BlockSpec(memory_space=pl.ANY)


def shape_of(shape, dtype):
    return jax.ShapeDtypeStruct(shape, dtype)


class Grid:
    def __init__(self, ep_size, pairs):
        self.ep, self.x, self.z, self.pairs = ep_size, ep_size // 4, 4, pairs
        self.steps = [(s, u) for s in range(self.z) for u in range(self.x)]

    def along_z(self, z, s):
        return z ^ s if self.pairs else (z + s) % self.z

    def send(self, arr, s, u):
        pairs = [
            (z * self.x + x, self.along_z(z, s) * self.x + (x + u) % self.x)
            for z in range(self.z)
            for x in range(self.x)
        ]
        return lax.ppermute(arr, "ep", pairs)

    def along_x(self, got, s):
        for u in range(1, self.x):
            got[s, u] = self.send(got[s, 0], 0, u)

    def spread(self, own, spaced):
        got = {(0, 0): own[0]}
        got[1, 0] = self.send(own[1], 1, 0)
        got[3, 0] = self.send(own[3], 3, 0)
        self.along_x(got, 0)
        far = own[2]
        if spaced:
            far, *_ = lax.optimization_barrier((far, got[1, 0], got[0, self.x - 1]))
        got[2, 0] = self.send(far, 2, 0)
        self.along_x(got, 1)
        self.along_x(got, 3)
        if not spaced:
            got[2, 0], *_ = lax.optimization_barrier((got[2, 0], got[1, self.x - 1]))
        self.along_x(got, 2)
        return [got[step] for step in self.steps]

    def source(self, step):
        me = lax.axis_index("ep")
        z = me // self.x
        z = z ^ step[0] if self.pairs else lax.rem(z - step[0] + self.z, self.z)
        return z * self.x + lax.rem(lax.rem(me, self.x) - step[1] + self.x, self.x)

    def target(self, step):
        s = step[0] if self.pairs else -step[0] % self.z
        return self.source((s, -step[1] % self.x))


def swap(arr):
    return lax.ppermute(arr, "tp", [(0, 1), (1, 0)])


def nt_dot(a, b):
    return lax.dot_general(a, b, (((1,), (1,)), ((), ())), preferred_element_type=jnp.float32)


def in_hbm():
    return pl.BlockSpec(memory_space=pltpu.HBM)


def attention(
    grid,
    piece,
    cols,
    queries,
    new_kv,
    cache,
    lengths,
    residual,
    route_ids,
    route_weights,
    gate_t,
    up_t,
    w_down,
):
    rows, width = queries.shape
    heads = width // HD
    ctx = cache.shape[1]
    parts = HD // LANES
    sizes = [grid.x] * grid.z
    note = piece + LANES
    scaling = HD ** (-0.5)
    units, features = gate_t.shape
    out_width = features // 2
    down_blocks = out_width // piece
    packed_rows = (2 * grid.ep + down_blocks) * units

    def kernel(*refs):
        sources, rest = refs[:7], refs[7:]
        gate_ref, up_ref, down_ref, rest = rest[0], rest[1], rest[2], rest[3:]
        out_refs, pack_ref, rest = rest[: len(sizes)], rest[len(sizes)], rest[len(sizes) + 1 :]
        q_ref, kv_ref, res_ref, ids_ref, wts_ref, len_ref, kept, turned, packed, sems, row_sems, pack_sems = rest
        cache_ref = sources[6]
        copies = [
            pltpu.make_async_copy(src, dst, sems.at[i])
            for i, (src, dst) in enumerate(
                zip(sources[:6], (q_ref, kv_ref, res_ref, ids_ref, wts_ref, len_ref))
            )
        ]
        row_copies = [
            pltpu.make_async_copy(cache_ref.at[r], kept.at[r], row_sems.at[r]) for r in range(rows)
        ]
        other = 1 - lax.axis_index("tp")
        blocks = []
        for j in range(grid.ep):
            begin = pl.multiple_of(j * cols + other * (cols - piece), LANES)
            blocks += [ref.at[:, pl.ds(begin, piece)] for ref in (gate_ref, up_ref)]
        for b in range(down_blocks):
            begin = pl.multiple_of(other * out_width + b * piece, LANES)
            blocks.append(down_ref.at[:, pl.ds(begin, piece)])
        packs = [
            pltpu.make_async_copy(block, packed.at[pl.ds(i * units, units), :], pack_sems.at[i])
            for i, block in enumerate(blocks)
        ]
        pack_out = pltpu.make_async_copy(packed, pack_ref, pack_sems.at[len(blocks)])
        for copy in copies[:2] + row_copies:
            copy.start()

        copies[0].wait()
        copies[1].wait()
        for h in range(heads):
            for c in range(parts):
                at = h * HD + c * LANES
                turned[c, h * rows : (h + 1) * rows, :] = q_ref[:, at : at + LANES].astype(jnp.float32)
        for copy in copies[2:] + packs:
            copy.start()
        new_k = kv_ref[:, :HD].astype(jnp.float32)
        new_v = kv_ref[:, HD:].astype(jnp.float32)
        scores, owns = [], []
        for r in range(rows):
            q = jnp.concatenate(
                [turned[c, pl.ds(r, heads, stride=rows), :] for c in range(parts)], axis=1
            )
            owns.append(jnp.sum(q * new_k[r : r + 1], axis=1, keepdims=True) * scaling)
            row_copies[r].wait()
            scores.append(nt_dot(q.astype(jnp.bfloat16), kept[r, :, :HD]) * scaling)

        for copy in copies[2:]:
            copy.wait()
        lane = lax.broadcasted_iota(jnp.int32, (rows, LANES), 1)
        square = (rows, rows)
        diagonal = lax.broadcasted_iota(jnp.int32, square, 0) == lax.broadcasted_iota(jnp.int32, square, 1)
        skip = lax.axis_index("tp") * (cols - piece)
        for s, u in grid.steps:
            to = grid.target((s, u))
            begin = pl.multiple_of(to * cols + skip, LANES)
            at = width + u * note
            out_refs[s][:, at : at + piece] = res_ref[:, pl.ds(begin, piece)]
            chosen = ids_ref[...] == to * EXPERTS // grid.ep
            across = jnp.sum(jnp.where(chosen, wts_ref[...], 0.0), axis=0, keepdims=True)
            weight = jnp.sum(
                jnp.where(diagonal, jnp.broadcast_to(across, square), 0.0), axis=1, keepdims=True
            )
            high = weight.astype(jnp.bfloat16).astype(jnp.float32)
            middle = (weight - high).astype(jnp.bfloat16).astype(jnp.float32)
            low = weight - high - middle
            tile = jnp.where(lane == 0, high, 0.0)
            tile = jnp.where(lane == 1, middle, tile)
            tile = jnp.where(lane == 2, low, tile)
            out_refs[s][:, at + piece : at + note] = tile.astype(jnp.bfloat16)

        place = lax.broadcasted_iota(jnp.int32, (heads, ctx), 1)
        probs, own_probs = [], []
        for r in range(rows):
            score = jnp.where(place < len_ref[r], scores[r], -jnp.inf)
            peak = jnp.maximum(jnp.max(score, axis=1, keepdims=True), owns[r])
            exps = jnp.exp(score - peak)
            own_exp = jnp.exp(owns[r] - peak)
            denominator = jnp.sum(exps, axis=1, keepdims=True) + own_exp
            probs.append((exps / denominator).astype(jnp.bfloat16))
            own_probs.append((own_exp / denominator).astype(jnp.bfloat16).astype(jnp.float32))
        for copy in packs:
            copy.wait()
        pack_out.start()
        for r in range(rows):
            mixed = jnp.dot(probs[r], kept[r, :, HD:], preferred_element_type=jnp.float32)
            mixed = mixed + own_probs[r] * new_v[r : r + 1]
            for c in range(parts):
                turned[c, r * heads : (r + 1) * heads, :] = mixed[:, c * LANES : (c + 1) * LANES]
        for h in range(heads):
            for c in range(parts):
                value = turned[c, pl.ds(h, rows, stride=heads), :].astype(jnp.bfloat16)
                begin = h * HD + c * LANES
                for ref in out_refs:
                    ref[:, begin : begin + LANES] = value
        pack_out.wait()

    return pl.pallas_call(
        kernel,
        name="attention",
        out_shape=[shape_of((rows, width + size * note), jnp.bfloat16) for size in sizes]
        + [shape_of((packed_rows, piece), jnp.bfloat16)],
        in_specs=[in_hbm()] * 10,
        out_specs=[vmem()] * len(sizes) + [in_hbm()],
        scratch_shapes=[
            pltpu.VMEM(queries.shape, jnp.bfloat16),
            pltpu.VMEM(new_kv.shape, jnp.bfloat16),
            pltpu.VMEM(residual.shape, jnp.bfloat16),
            pltpu.VMEM(route_ids.shape, jnp.int32),
            pltpu.VMEM(route_weights.shape, jnp.float32),
            pltpu.SMEM(lengths.shape, jnp.int32),
            pltpu.VMEM(cache.shape, jnp.bfloat16),
            pltpu.VMEM((parts, rows * heads, LANES), jnp.float32),
            pltpu.VMEM((packed_rows, piece), jnp.bfloat16),
            pltpu.SemaphoreType.DMA((6,)),
            pltpu.SemaphoreType.DMA((rows,)),
            pltpu.SemaphoreType.DMA((2 * grid.ep + down_blocks + 1,)),
        ],
        compiler_params=params(60),
    )(
        queries,
        new_kv,
        residual,
        route_ids,
        route_weights,
        lengths,
        cache,
        gate_t,
        up_t,
        w_down,
    )


def project(grid, piece, chunks, w_out):
    rows = chunks[0].shape[0]
    depth, cols = w_out.shape
    count = len(chunks)
    tall = rows * count
    blocks = 8
    block = depth // blocks
    note = piece + LANES

    def kernel(*refs):
        chunk_refs, rest = refs[:count], refs[count:]
        w_ref, ours_ref, theirs_ref, weight_ref, stacked, total = rest
        k = pl.program_id(0)

        @pl.when(k == 0)
        def _():
            both = jnp.concatenate([ref[:, :depth] for ref in chunk_refs], axis=0)
            for i in range(blocks):
                stacked[i] = both[:, i * block : (i + 1) * block]

        product = jnp.dot(stacked[k], w_ref[...], preferred_element_type=jnp.float32)

        @pl.when(k == 0)
        def _():
            total[...] = product

        @pl.when(k > 0)
        def _():
            total[...] += product

        @pl.when(k == blocks - 1)
        def _():
            core = lax.axis_index("tp")
            mine = pl.multiple_of(core * (cols - piece), LANES)
            other = pl.multiple_of((1 - core) * (cols - piece), LANES)
            for i, (s, u) in enumerate(grid.steps):
                here = pl.ds(pl.multiple_of(grid.source((s, u)) * rows, rows), rows)
                at = depth + u * note
                beside = chunk_refs[i][:, at : at + note].astype(jnp.float32)
                block_rows = slice(i * rows, (i + 1) * rows)
                ours_ref[here, :] = total[block_rows, pl.ds(mine, piece)] + beside[:, :piece]
                theirs_ref[here, :] = total[block_rows, pl.ds(other, piece)]
                weight_ref[here, :] = jnp.broadcast_to(
                    jnp.sum(beside[:, piece:], axis=1, keepdims=True), (rows, LANES)
                )

    def whole(arr):
        return pl.BlockSpec(arr.shape, lambda k: (0, 0))

    outs = [shape_of((tall, piece), jnp.float32)] * 2 + [shape_of((tall, LANES), jnp.float32)]
    return pl.pallas_call(
        kernel,
        name="project",
        grid=(blocks,),
        out_shape=outs,
        in_specs=[whole(c) for c in chunks] + [pl.BlockSpec((block, cols), lambda k: (k, 0))],
        out_specs=[whole(o) for o in outs],
        scratch_shapes=[
            pltpu.VMEM((blocks, tall, block), jnp.bfloat16),
            pltpu.VMEM((tall, cols), jnp.float32),
        ],
        cost_estimate=pl.CostEstimate(
            flops=2 * tall * depth * cols,
            bytes_accessed=2 * depth * cols + 2 * tall * depth + 8 * tall * piece,
            transcendentals=0,
        ),
        compiler_params=params(48),
    )(*chunks, w_out)


def gate_up(grid, piece, cols, rows, pieces, gain, gate_t, up_t, other):
    tall = pieces[0].shape[0]
    units = gate_t.shape[0]
    count = grid.ep
    dup = 2 * piece - cols
    per_half = count // 2
    sums_width = 4 * units + LANES
    extra = -(-per_half * piece // sums_width)

    def kernel(*refs):
        piece_refs, rest = refs[:count], refs[count:]
        gain_ref, gate_ref, up_ref, other_ref, sums_ref, home_ref, held, home = rest
        home[1] = jnp.zeros((rows, extra * sums_width), jnp.float32)
        core = lax.axis_index("tp")
        me = lax.axis_index("ep")
        fresh = lax.broadcasted_iota(jnp.int32, (tall, piece), 1) >= core * dup
        square = jnp.zeros((tall, 1), jnp.float32)
        own_gate = jnp.zeros((units, tall), jnp.float32)
        own_up = jnp.zeros((units, tall), jnp.float32)
        far = jnp.zeros((2 * units, tall), jnp.float32)
        for i, step in enumerate(grid.steps):
            j = grid.source(step)
            lanes = pl.ds(pl.multiple_of(j * cols + core * (cols - piece), LANES), piece)
            stream = piece_refs[i][...].astype(jnp.float32)
            held[...] = stream
            mine = held[pl.ds(pl.multiple_of(me * rows, rows), rows), :]
            side = lax.rem(j // per_half + core, 2)
            at = pl.multiple_of(lax.rem(j, per_half) * piece, LANES)
            home[side, :, pl.ds(at, piece)] = mine
            stream = jnp.where(fresh, stream, 0.0)
            square = square + jnp.sum(stream * stream, axis=1, keepdims=True)
            scaled = (stream * gain_ref[:, lanes]).astype(jnp.bfloat16)
            own_gate = own_gate + nt_dot(gate_ref[:, lanes], scaled)
            own_up = own_up + nt_dot(up_ref[:, lanes], scaled)
            block = pl.ds(pl.multiple_of(j * 2 * units, 2 * units), 2 * units)
            far = far + nt_dot(other_ref[block, :], scaled)
        sums_ref[:tall, : 4 * units] = jnp.concatenate([own_gate, own_up, far], axis=0).T
        sums_ref[:tall, 4 * units :] = jnp.broadcast_to(square, (tall, LANES))
        for b in range(extra):
            at = tall + b * rows
            sums_ref[at : at + rows, :] = home[1, :, b * sums_width : (b + 1) * sums_width]
        home_ref[...] = home[0, :, : per_half * piece]

    return pl.pallas_call(
        kernel,
        name="gate_up",
        out_shape=[
            shape_of((tall + extra * rows, sums_width), jnp.float32),
            shape_of((rows, per_half * piece), jnp.float32),
        ],
        in_specs=[vmem()] * (count + 4),
        out_specs=[vmem()] * 2,
        scratch_shapes=[
            pltpu.VMEM((tall, piece), jnp.float32),
            pltpu.VMEM((2, rows, extra * sums_width), jnp.float32),
        ],
        compiler_params=params(8),
    )(*pieces, gain, gate_t, up_t, other)


def down(grid, piece, rows, sums, far_sums, weight, w_down, far_weights):
    tall = weight.shape[0]
    units, width = w_down.shape
    out_width = width // 2
    count = grid.ep

    def kernel(sums_ref, far_ref, weight_ref, down_ref, packed_ref, *rest):
        out_refs, total, down_half, sem = rest[:count], rest[count], rest[count + 1], rest[count + 2]
        begin = pl.multiple_of(lax.axis_index("tp") * out_width, LANES)
        copy = pltpu.make_async_copy(down_ref.at[:, pl.ds(begin, out_width)], down_half, sem)
        copy.start()
        square = (
            sums_ref[:tall, 4 * units : 4 * units + 1] + far_ref[:tall, 4 * units : 4 * units + 1]
        )
        scale = lax.rsqrt(square / width + 1e-06)

        def hidden(a, b):
            both = (
                sums_ref[:tall, a * units : (a + 2) * units]
                + far_ref[:tall, b * units : (b + 2) * units]
            )
            gate, up = both[:, :units] * scale, both[:, units:] * scale
            return (gate / (1.0 + jnp.exp(-gate)) * up).astype(jnp.bfloat16)

        near, far = hidden(0, 2), hidden(2, 0)
        copy.wait()
        for b in range(out_width // piece):
            span = slice(b * piece, (b + 1) * piece)
            block = slice((2 * count + b) * units, (2 * count + b + 1) * units)
            value = jnp.dot(near, down_half[:, span], preferred_element_type=jnp.float32)
            value = value + jnp.dot(far, packed_ref[block, :], preferred_element_type=jnp.float32)
            total[:, span] = value * weight_ref[:, :1]
        for i, step in enumerate(grid.steps):
            there = pl.ds(pl.multiple_of(grid.target(step) * rows, rows), rows)
            out_refs[i][...] = total[there, :].astype(out_refs[i].dtype)

    return pl.pallas_call(
        kernel,
        name="down",
        out_shape=[
            shape_of((rows, out_width), jnp.bfloat16 if i else jnp.float32) for i in range(count)
        ],
        in_specs=[vmem()] * 3 + [pl.BlockSpec(memory_space=pl.ANY), vmem()],
        out_specs=[vmem()] * count,
        scratch_shapes=[
            pltpu.VMEM((tall, out_width), jnp.float32),
            pltpu.VMEM((units, out_width), jnp.bfloat16),
            pltpu.SemaphoreType.DMA(()),
        ],
        compiler_params=params(8),
    )(sums, far_sums, weight, w_down, far_weights)


def finish(piece, cols, near, far_sums, parts):
    rows, out_width = parts[0].shape
    extra = -(-near.shape[1] // far_sums.shape[1])
    top = far_sums.shape[0] - extra * rows
    dup = 2 * piece - cols

    def kernel(near_ref, far_ref, *rest):
        part_refs, out_ref = rest[:-1], rest[-1]
        first = lax.axis_index("tp") == 0
        far = jnp.concatenate(
            [far_ref[top + b * rows : top + (b + 1) * rows, :] for b in range(extra)], axis=1
        )
        for c in range(out_width // cols):
            span = slice(c * piece, (c + 1) * piece)
            a, b = near_ref[:, span], far[:, span]
            low = jnp.where(first, a, b)
            high = jnp.where(first, b, a)[:, dup:]
            value = jnp.concatenate([low, high], axis=1)
            for ref in part_refs:
                value = value + ref[:, c * cols : (c + 1) * cols].astype(jnp.float32)
            out_ref[:, c * cols : (c + 1) * cols] = value.astype(jnp.bfloat16)

    return pl.pallas_call(
        kernel,
        name="finish",
        out_shape=shape_of((rows, out_width), jnp.bfloat16),
        in_specs=[vmem()] * (2 + len(parts)),
        out_specs=vmem(),
        compiler_params=params(4),
    )(near, far_sums, *parts)


def tuned_body(
    ring,
    grid,
    residual,
    queries,
    new_kv,
    cache,
    lengths,
    w_out,
    gain,
    route_ids,
    route_weights,
    w_gate,
    w_up,
    w_down,
):
    rows, width = residual.shape
    cols = w_out.shape[1]
    piece = -(-cols // (2 * LANES)) * LANES
    gate_t, up_t = w_gate.T, w_up.T
    *outgoing, packed = attention(
        ring,
        piece,
        cols,
        queries,
        new_kv,
        cache,
        lengths,
        residual,
        route_ids.T,
        route_weights.T,
        gate_t,
        up_t,
        w_down,
    )
    chunks = ring.spread(outgoing, spaced=True)
    packed, *_ = lax.optimization_barrier((packed, *chunks))
    far_weights = swap(packed)
    ours, theirs, weight = project(ring, piece, chunks, w_out)
    stream = (ours + swap(theirs)).astype(jnp.bfloat16)
    stream, far_weights = lax.optimization_barrier((stream, far_weights))
    pieces = grid.spread([stream] * grid.z, spaced=False)
    sums, home = gate_up(
        grid, piece, cols, rows, pieces, gain.reshape(1, width), gate_t, up_t, far_weights
    )
    far_sums = swap(sums)
    parts = down(grid, piece, rows, sums, far_sums, weight, w_down, far_weights)
    order = sorted(range(grid.ep), key=lambda i: (grid.steps[i] == (0, 0), -grid.steps[i][0]))
    shares = [grid.send(parts[i], *grid.steps[i]) if any(grid.steps[i]) else parts[i] for i in order]
    return finish(piece, cols, home, far_sums, shares)


def general_body(
    residual,
    queries,
    new_kv,
    cache,
    lengths,
    w_out,
    gain,
    route_ids,
    route_weights,
    w_gate,
    w_up,
    w_down,
):
    row_count = queries.shape[0]
    head_count = queries.shape[1] // HD
    scaling = HD ** (-0.5)
    query_heads = queries.reshape(row_count, head_count, HD)
    key_rows = cache[:, :, :HD]
    value_rows = cache[:, :, HD:]
    scores = (
        jnp.einsum("rhd,rpd->rhp", query_heads, key_rows, preferred_element_type=jnp.float32)
        * scaling
    )
    usable = jnp.arange(cache.shape[1], dtype=jnp.int32)[None, :] < lengths[:, None]
    scores = jnp.where(usable[:, None, :], scores, -jnp.inf)
    own_score = (
        jnp.einsum("rhd,rd->rh", query_heads, new_kv[:, :HD], preferred_element_type=jnp.float32)
        * scaling
    )
    peak_score = jnp.maximum(jnp.max(scores, axis=2), own_score)
    cache_weight = jnp.exp(scores - peak_score[:, :, None])
    own_weight = jnp.exp(own_score - peak_score)
    denominator = jnp.sum(cache_weight, axis=2) + own_weight
    probabilities = (cache_weight / denominator[:, :, None]).astype(jnp.bfloat16)
    own_prob = (own_weight / denominator).astype(jnp.bfloat16)
    context = jnp.einsum(
        "rhp,rpd->rhd", probabilities, value_rows, preferred_element_type=jnp.float32
    )
    context = context + own_prob.astype(jnp.float32)[:, :, None] * new_kv[:, None, HD:].astype(
        jnp.float32
    )
    context = context.astype(jnp.bfloat16).reshape(row_count, head_count * HD)
    attn_cols = jnp.dot(
        lax.all_gather(context, "ep", axis=0, tiled=True), w_out, preferred_element_type=jnp.float32
    )
    attn_rows = lax.all_to_all(attn_cols, "ep", split_axis=0, concat_axis=1, tiled=True)
    attention = lax.psum(attn_rows, "tp")
    stream = residual.astype(jnp.float32) + attention
    mean_square = jnp.mean(stream * stream, axis=1, keepdims=True)
    normed = (stream * lax.rsqrt(mean_square + 1e-06) * gain[None, :]).astype(jnp.bfloat16)
    width = normed.shape[1]
    ep_size = lax.axis_size("ep")
    members = ep_size // EXPERTS
    slot_count = EXPERTS * CAP
    flat_ids = route_ids.reshape(-1)
    one_hot = (flat_ids[:, None] == jnp.arange(EXPERTS, dtype=jnp.int32)[None, :]).astype(jnp.int32)
    earlier = jnp.cumsum(one_hot, axis=0) - one_hot
    slot_index = jnp.sum(earlier * one_hot, axis=1)
    target = (flat_ids * CAP + slot_index).reshape(row_count, TOPK)
    placed = (target[:, :, None] == jnp.arange(slot_count, dtype=jnp.int32)[None, None, :]).astype(
        jnp.float32
    )
    chosen = jnp.sum(placed, axis=1).reshape(row_count, EXPERTS, CAP).astype(jnp.bfloat16)
    mixing = jnp.sum(placed * route_weights[:, :, None], axis=1).reshape(row_count, EXPERTS, CAP)
    outgoing = jnp.einsum("rec,rd->ecd", chosen, normed, preferred_element_type=jnp.float32).astype(
        jnp.bfloat16
    )
    outgoing = jnp.broadcast_to(outgoing[:, None], (EXPERTS, members, CAP, width)).reshape(
        ep_size * CAP, width
    )
    arrived = lax.all_to_all(outgoing, "ep", split_axis=0, concat_axis=0, tiled=True)
    gate_act = jnp.dot(arrived, w_gate, preferred_element_type=jnp.float32)
    up_act = jnp.dot(arrived, w_up, preferred_element_type=jnp.float32)
    hidden = (jax.nn.silu(gate_act) * up_act).astype(jnp.bfloat16)
    partial_value = jnp.dot(hidden, w_down, preferred_element_type=jnp.float32)
    halves = lax.psum_scatter(partial_value, "tp", scatter_dimension=1, tiled=True)
    returned = lax.all_to_all(halves, "ep", split_axis=0, concat_axis=0, tiled=True)
    returned = returned.reshape(EXPERTS, members, CAP, returned.shape[1])
    mixed = jnp.einsum("rec,egcw->rw", mixing, returned, precision=lax.Precision.HIGHEST)
    tp_start = lax.axis_index("tp") * mixed.shape[1]
    stream_part = lax.dynamic_slice_in_dim(stream, tp_start, mixed.shape[1], 1)
    return (stream_part + mixed).astype(jnp.bfloat16)


def body(*args):
    ep_size, cols, heads_width = lax.axis_size("ep"), args[5].shape[1], args[5].shape[0]
    if ep_size == 8 and lax.axis_size("tp") == 2 and cols % LANES == 0 and heads_width % (8 * HD) == 0:
        return tuned_body(Grid(ep_size, False), Grid(ep_size, True), *args)
    return general_body(*args)


def solution(mesh):
    placed = (
        P(("grp", "ep"), None),
        P(("grp", "ep"), "tp"),
        P(("grp", "ep"), None),
        P(("grp", "ep"), None, None),
        P(("grp", "ep")),
        P("tp", "ep"),
        P(),
        P(("grp", "ep"), None),
        P(("grp", "ep"), None),
        P(None, ("ep", "tp")),
        P(None, ("ep", "tp")),
        P(("ep", "tp"), None),
    )
    return jax.shard_map(
        body, mesh=mesh, in_specs=placed, out_specs=P(("grp", "ep"), "tp"), check_vma=False
    )
```

```python
import functools

import jax
import jax.numpy as jnp
from jax import lax
from jax.experimental import pallas as pl
from jax.experimental.pallas import tpu as pltpu
from jax.sharding import PartitionSpec as P

HD = 256
TOPK = 3
EXPERTS = 4
CAP = 8
LANES = 128


def params(mebibytes):
    return pltpu.CompilerParams(vmem_limit_bytes=mebibytes * 1024 * 1024)


def vmem():
    return pl.BlockSpec(memory_space=pltpu.VMEM)


def anywhere():
    return pl.BlockSpec(memory_space=pl.ANY)


def shape_of(shape, dtype):
    return jax.ShapeDtypeStruct(shape, dtype)


class Grid:
    def __init__(self, ep_size, pairs):
        self.ep, self.x, self.z, self.pairs = ep_size, ep_size // 4, 4, pairs
        self.steps = [(s, u) for s in range(self.z) for u in range(self.x)]

    def along_z(self, z, s):
        return z ^ s if self.pairs else (z + s) % self.z

    def send(self, arr, s, u):
        pairs = [
            (z * self.x + x, self.along_z(z, s) * self.x + (x + u) % self.x)
            for z in range(self.z)
            for x in range(self.x)
        ]
        return lax.ppermute(arr, "ep", pairs)

    def along_x(self, got, s):
        for u in range(1, self.x):
            got[s, u] = self.send(got[s, 0], 0, u)

    def spread(self, own, spaced):
        early, late = (2, 3) if spaced else (3, 2)
        got = {(0, 0): own[0]}
        got[1, 0] = self.send(own[1], 1, 0)
        got[early, 0] = self.send(own[early], early, 0)
        self.along_x(got, 0)
        leaving = own[late]
        if spaced:
            leaving, *_ = lax.optimization_barrier((leaving, got[1, 0], got[0, self.x - 1]))
        got[late, 0] = self.send(leaving, late, 0)
        self.along_x(got, 1)
        self.along_x(got, early)
        if not spaced:
            got[late, 0], *_ = lax.optimization_barrier((got[late, 0], got[1, self.x - 1]))
        self.along_x(got, late)
        return [got[step] for step in self.steps]

    def source(self, step):
        me = lax.axis_index("ep")
        z = me // self.x
        z = z ^ step[0] if self.pairs else lax.rem(z - step[0] + self.z, self.z)
        return z * self.x + lax.rem(lax.rem(me, self.x) - step[1] + self.x, self.x)

    def target(self, step):
        s = step[0] if self.pairs else -step[0] % self.z
        return self.source((s, -step[1] % self.x))


def swap(arr):
    return lax.ppermute(arr, "tp", [(0, 1), (1, 0)])


def nt_dot(a, b):
    return lax.dot_general(a, b, (((1,), (1,)), ((), ())), preferred_element_type=jnp.float32)


def in_hbm():
    return pl.BlockSpec(memory_space=pltpu.HBM)


def attention(
    grid,
    piece,
    cols,
    queries,
    new_kv,
    cache,
    lengths,
    residual,
    route_ids,
    route_weights,
    gate_t,
    up_t,
    w_down,
):
    rows, width = queries.shape
    heads = width // HD
    ctx = cache.shape[1]
    parts = HD // LANES
    sizes = [grid.x] * grid.z
    note = piece + LANES
    scaling = HD ** (-0.5)
    units, features = gate_t.shape
    out_width = features // 2
    down_blocks = out_width // piece
    packed_rows = (2 * grid.ep + down_blocks) * units

    def kernel(*refs):
        sources, rest = refs[:7], refs[7:]
        gate_ref, up_ref, down_ref, rest = rest[0], rest[1], rest[2], rest[3:]
        out_refs, pack_ref, rest = rest[: len(sizes)], rest[len(sizes)], rest[len(sizes) + 1 :]
        q_ref, kv_ref, res_ref, ids_ref, wts_ref, len_ref, kept, turned, packed, sems, row_sems, pack_sems = rest
        cache_ref = sources[6]
        copies = [
            pltpu.make_async_copy(src, dst, sems.at[i])
            for i, (src, dst) in enumerate(
                zip(sources[:6], (q_ref, kv_ref, res_ref, ids_ref, wts_ref, len_ref))
            )
        ]
        row_copies = [
            pltpu.make_async_copy(cache_ref.at[r], kept.at[r], row_sems.at[r]) for r in range(rows)
        ]
        other = 1 - lax.axis_index("tp")
        blocks = []
        for j in range(grid.ep):
            begin = pl.multiple_of(j * cols + other * (cols - piece), LANES)
            blocks += [ref.at[:, pl.ds(begin, piece)] for ref in (gate_ref, up_ref)]
        for b in range(down_blocks):
            begin = pl.multiple_of(other * out_width + b * piece, LANES)
            blocks.append(down_ref.at[:, pl.ds(begin, piece)])
        packs = [
            pltpu.make_async_copy(block, packed.at[pl.ds(i * units, units), :], pack_sems.at[i])
            for i, block in enumerate(blocks)
        ]
        pack_out = pltpu.make_async_copy(packed, pack_ref, pack_sems.at[len(blocks)])
        for copy in copies[:2] + row_copies:
            copy.start()

        copies[0].wait()
        copies[1].wait()
        for h in range(heads):
            for c in range(parts):
                at = h * HD + c * LANES
                turned[c, h * rows : (h + 1) * rows, :] = q_ref[:, at : at + LANES].astype(jnp.float32)
        for copy in copies[2:] + packs:
            copy.start()
        new_k = kv_ref[:, :HD].astype(jnp.float32)
        new_v = kv_ref[:, HD:].astype(jnp.float32)
        scores, owns = [], []
        for r in range(rows):
            q = jnp.concatenate(
                [turned[c, pl.ds(r, heads, stride=rows), :] for c in range(parts)], axis=1
            )
            owns.append(jnp.sum(q * new_k[r : r + 1], axis=1, keepdims=True) * scaling)
            row_copies[r].wait()
            scores.append(nt_dot(q.astype(jnp.bfloat16), kept[r, :, :HD]) * scaling)

        for copy in copies[2:]:
            copy.wait()
        lane = lax.broadcasted_iota(jnp.int32, (rows, LANES), 1)
        square = (rows, rows)
        diagonal = lax.broadcasted_iota(jnp.int32, square, 0) == lax.broadcasted_iota(jnp.int32, square, 1)
        skip = lax.axis_index("tp") * (cols - piece)
        for s, u in grid.steps:
            to = grid.target((s, u))
            begin = pl.multiple_of(to * cols + skip, LANES)
            at = width + u * note
            out_refs[s][:, at : at + piece] = res_ref[:, pl.ds(begin, piece)]
            chosen = ids_ref[...] == to * EXPERTS // grid.ep
            across = jnp.sum(jnp.where(chosen, wts_ref[...], 0.0), axis=0, keepdims=True)
            weight = jnp.sum(
                jnp.where(diagonal, jnp.broadcast_to(across, square), 0.0), axis=1, keepdims=True
            )
            high = weight.astype(jnp.bfloat16).astype(jnp.float32)
            middle = (weight - high).astype(jnp.bfloat16).astype(jnp.float32)
            low = weight - high - middle
            tile = jnp.where(lane == 0, high, 0.0)
            tile = jnp.where(lane == 1, middle, tile)
            tile = jnp.where(lane == 2, low, tile)
            out_refs[s][:, at + piece : at + note] = tile.astype(jnp.bfloat16)

        place = lax.broadcasted_iota(jnp.int32, (heads, ctx), 1)
        probs, own_probs = [], []
        for r in range(rows):
            score = jnp.where(place < len_ref[r], scores[r], -jnp.inf)
            peak = jnp.maximum(jnp.max(score, axis=1, keepdims=True), owns[r])
            exps = jnp.exp(score - peak)
            own_exp = jnp.exp(owns[r] - peak)
            denominator = jnp.sum(exps, axis=1, keepdims=True) + own_exp
            probs.append((exps / denominator).astype(jnp.bfloat16))
            own_probs.append((own_exp / denominator).astype(jnp.bfloat16).astype(jnp.float32))
        for copy in packs:
            copy.wait()
        pack_out.start()
        for r in range(rows):
            mixed = jnp.dot(probs[r], kept[r, :, HD:], preferred_element_type=jnp.float32)
            mixed = mixed + own_probs[r] * new_v[r : r + 1]
            for c in range(parts):
                turned[c, r * heads : (r + 1) * heads, :] = mixed[:, c * LANES : (c + 1) * LANES]
        for h in range(heads):
            for c in range(parts):
                value = turned[c, pl.ds(h, rows, stride=heads), :].astype(jnp.bfloat16)
                begin = h * HD + c * LANES
                for ref in out_refs:
                    ref[:, begin : begin + LANES] = value
        pack_out.wait()

    return pl.pallas_call(
        kernel,
        name="attention",
        out_shape=[shape_of((rows, width + size * note), jnp.bfloat16) for size in sizes]
        + [shape_of((packed_rows, piece), jnp.bfloat16)],
        in_specs=[in_hbm()] * 10,
        out_specs=[vmem()] * len(sizes) + [in_hbm()],
        scratch_shapes=[
            pltpu.VMEM(queries.shape, jnp.bfloat16),
            pltpu.VMEM(new_kv.shape, jnp.bfloat16),
            pltpu.VMEM(residual.shape, jnp.bfloat16),
            pltpu.VMEM(route_ids.shape, jnp.int32),
            pltpu.VMEM(route_weights.shape, jnp.float32),
            pltpu.SMEM(lengths.shape, jnp.int32),
            pltpu.VMEM(cache.shape, jnp.bfloat16),
            pltpu.VMEM((parts, rows * heads, LANES), jnp.float32),
            pltpu.VMEM((packed_rows, piece), jnp.bfloat16),
            pltpu.SemaphoreType.DMA((6,)),
            pltpu.SemaphoreType.DMA((rows,)),
            pltpu.SemaphoreType.DMA((2 * grid.ep + down_blocks + 1,)),
        ],
        compiler_params=params(60),
    )(
        queries,
        new_kv,
        residual,
        route_ids,
        route_weights,
        lengths,
        cache,
        gate_t,
        up_t,
        w_down,
    )


def project(grid, piece, chunks, w_out):
    rows = chunks[0].shape[0]
    depth, cols = w_out.shape
    count = len(chunks)
    tall = rows * count
    blocks = 8
    block = depth // blocks
    note = piece + LANES

    def kernel(*refs):
        chunk_refs, rest = refs[:count], refs[count:]
        w_ref, ours_ref, theirs_ref, weight_ref, stacked, total = rest
        k = pl.program_id(0)

        @pl.when(k == 0)
        def _():
            both = jnp.concatenate([ref[:, :depth] for ref in chunk_refs], axis=0)
            for i in range(blocks):
                stacked[i] = both[:, i * block : (i + 1) * block]

        product = jnp.dot(stacked[k], w_ref[...], preferred_element_type=jnp.float32)

        @pl.when(k == 0)
        def _():
            total[...] = product

        @pl.when(k > 0)
        def _():
            total[...] += product

        @pl.when(k == blocks - 1)
        def _():
            core = lax.axis_index("tp")
            mine = pl.multiple_of(core * (cols - piece), LANES)
            other = pl.multiple_of((1 - core) * (cols - piece), LANES)
            for i, (s, u) in enumerate(grid.steps):
                here = pl.ds(pl.multiple_of(grid.source((s, u)) * rows, rows), rows)
                at = depth + u * note
                beside = chunk_refs[i][:, at : at + note].astype(jnp.float32)
                block_rows = slice(i * rows, (i + 1) * rows)
                ours_ref[here, :] = total[block_rows, pl.ds(mine, piece)] + beside[:, :piece]
                theirs_ref[here, :] = total[block_rows, pl.ds(other, piece)]
                weight_ref[here, :] = jnp.broadcast_to(
                    jnp.sum(beside[:, piece:], axis=1, keepdims=True), (rows, LANES)
                )

    def whole(arr):
        return pl.BlockSpec(arr.shape, lambda k: (0, 0))

    outs = [shape_of((tall, piece), jnp.float32)] * 2 + [shape_of((tall, LANES), jnp.float32)]
    return pl.pallas_call(
        kernel,
        name="project",
        grid=(blocks,),
        out_shape=outs,
        in_specs=[whole(c) for c in chunks] + [pl.BlockSpec((block, cols), lambda k: (k, 0))],
        out_specs=[whole(o) for o in outs],
        scratch_shapes=[
            pltpu.VMEM((blocks, tall, block), jnp.bfloat16),
            pltpu.VMEM((tall, cols), jnp.float32),
        ],
        cost_estimate=pl.CostEstimate(
            flops=2 * tall * depth * cols,
            bytes_accessed=2 * depth * cols + 2 * tall * depth + 8 * tall * piece,
            transcendentals=0,
        ),
        compiler_params=params(48),
    )(*chunks, w_out)


def gate_up(grid, piece, cols, rows, pieces, gain, gate_t, up_t, other):
    tall = pieces[0].shape[0]
    units = gate_t.shape[0]
    count = grid.ep
    dup = 2 * piece - cols
    per_half = count // 2
    sums_width = 4 * units + LANES
    extra = -(-per_half * piece // sums_width)

    def kernel(*refs):
        piece_refs, rest = refs[:count], refs[count:]
        gain_ref, gate_ref, up_ref, other_ref, sums_ref, home_ref, held, home = rest
        home[1] = jnp.zeros((rows, extra * sums_width), jnp.float32)
        core = lax.axis_index("tp")
        me = lax.axis_index("ep")
        fresh = lax.broadcasted_iota(jnp.int32, (tall, piece), 1) >= core * dup
        square = jnp.zeros((tall, 1), jnp.float32)
        own_gate = jnp.zeros((units, tall), jnp.float32)
        own_up = jnp.zeros((units, tall), jnp.float32)
        far = jnp.zeros((2 * units, tall), jnp.float32)
        for i, step in enumerate(grid.steps):
            j = grid.source(step)
            lanes = pl.ds(pl.multiple_of(j * cols + core * (cols - piece), LANES), piece)
            stream = piece_refs[i][...].astype(jnp.float32)
            held[...] = stream
            mine = held[pl.ds(pl.multiple_of(me * rows, rows), rows), :]
            side = lax.rem(j // per_half + core, 2)
            at = pl.multiple_of(lax.rem(j, per_half) * piece, LANES)
            home[side, :, pl.ds(at, piece)] = mine
            stream = jnp.where(fresh, stream, 0.0)
            square = square + jnp.sum(stream * stream, axis=1, keepdims=True)
            scaled = (stream * gain_ref[:, lanes]).astype(jnp.bfloat16)
            own_gate = own_gate + nt_dot(gate_ref[:, lanes], scaled)
            own_up = own_up + nt_dot(up_ref[:, lanes], scaled)
            block = pl.ds(pl.multiple_of(j * 2 * units, 2 * units), 2 * units)
            far = far + nt_dot(other_ref[block, :], scaled)
        sums_ref[:tall, : 4 * units] = jnp.concatenate([own_gate, own_up, far], axis=0).T
        sums_ref[:tall, 4 * units :] = jnp.broadcast_to(square, (tall, LANES))
        for b in range(extra):
            at = tall + b * rows
            sums_ref[at : at + rows, :] = home[1, :, b * sums_width : (b + 1) * sums_width]
        home_ref[...] = home[0, :, : per_half * piece]

    return pl.pallas_call(
        kernel,
        name="gate_up",
        out_shape=[
            shape_of((tall + extra * rows, sums_width), jnp.float32),
            shape_of((rows, per_half * piece), jnp.float32),
        ],
        in_specs=[vmem()] * (count + 4),
        out_specs=[vmem()] * 2,
        scratch_shapes=[
            pltpu.VMEM((tall, piece), jnp.float32),
            pltpu.VMEM((2, rows, extra * sums_width), jnp.float32),
        ],
        compiler_params=params(8),
    )(*pieces, gain, gate_t, up_t, other)


def down(grid, piece, rows, sums, far_sums, weight, w_down, far_weights):
    tall = weight.shape[0]
    units, width = w_down.shape
    out_width = width // 2
    count = grid.ep

    def kernel(sums_ref, far_ref, weight_ref, down_ref, packed_ref, *rest):
        out_refs, total, down_half, sem = rest[:count], rest[count], rest[count + 1], rest[count + 2]
        begin = pl.multiple_of(lax.axis_index("tp") * out_width, LANES)
        copy = pltpu.make_async_copy(down_ref.at[:, pl.ds(begin, out_width)], down_half, sem)
        copy.start()
        square = (
            sums_ref[:tall, 4 * units : 4 * units + 1] + far_ref[:tall, 4 * units : 4 * units + 1]
        )
        scale = lax.rsqrt(square / width + 1e-06)

        def hidden(a, b):
            both = (
                sums_ref[:tall, a * units : (a + 2) * units]
                + far_ref[:tall, b * units : (b + 2) * units]
            )
            gate, up = both[:, :units] * scale, both[:, units:] * scale
            return (gate / (1.0 + jnp.exp(-gate)) * up).astype(jnp.bfloat16)

        near, far = hidden(0, 2), hidden(2, 0)
        copy.wait()
        for b in range(out_width // piece):
            span = slice(b * piece, (b + 1) * piece)
            block = slice((2 * count + b) * units, (2 * count + b + 1) * units)
            value = jnp.dot(near, down_half[:, span], preferred_element_type=jnp.float32)
            value = value + jnp.dot(far, packed_ref[block, :], preferred_element_type=jnp.float32)
            total[:, span] = value * weight_ref[:, :1]
        for i, step in enumerate(grid.steps):
            there = pl.ds(pl.multiple_of(grid.target(step) * rows, rows), rows)
            out_refs[i][...] = total[there, :].astype(out_refs[i].dtype)

    return pl.pallas_call(
        kernel,
        name="down",
        out_shape=[
            shape_of((rows, out_width), jnp.bfloat16 if i else jnp.float32) for i in range(count)
        ],
        in_specs=[vmem()] * 3 + [pl.BlockSpec(memory_space=pl.ANY), vmem()],
        out_specs=[vmem()] * count,
        scratch_shapes=[
            pltpu.VMEM((tall, out_width), jnp.float32),
            pltpu.VMEM((units, out_width), jnp.bfloat16),
            pltpu.SemaphoreType.DMA(()),
        ],
        compiler_params=params(8),
    )(sums, far_sums, weight, w_down, far_weights)


def finish(piece, cols, near, far_sums, parts):
    rows, out_width = parts[0].shape
    extra = -(-near.shape[1] // far_sums.shape[1])
    top = far_sums.shape[0] - extra * rows
    dup = 2 * piece - cols

    def kernel(near_ref, far_ref, *rest):
        part_refs, out_ref = rest[:-1], rest[-1]
        first = lax.axis_index("tp") == 0
        far = jnp.concatenate(
            [far_ref[top + b * rows : top + (b + 1) * rows, :] for b in range(extra)], axis=1
        )
        for c in range(out_width // cols):
            span = slice(c * piece, (c + 1) * piece)
            a, b = near_ref[:, span], far[:, span]
            low = jnp.where(first, a, b)
            high = jnp.where(first, b, a)[:, dup:]
            value = jnp.concatenate([low, high], axis=1)
            for ref in part_refs:
                value = value + ref[:, c * cols : (c + 1) * cols].astype(jnp.float32)
            out_ref[:, c * cols : (c + 1) * cols] = value.astype(jnp.bfloat16)

    return pl.pallas_call(
        kernel,
        name="finish",
        out_shape=shape_of((rows, out_width), jnp.bfloat16),
        in_specs=[vmem()] * (2 + len(parts)),
        out_specs=vmem(),
        compiler_params=params(4),
    )(near, far_sums, *parts)


def tuned_body(
    ring,
    grid,
    residual,
    queries,
    new_kv,
    cache,
    lengths,
    w_out,
    gain,
    route_ids,
    route_weights,
    w_gate,
    w_up,
    w_down,
):
    rows, width = residual.shape
    cols = w_out.shape[1]
    piece = -(-cols // (2 * LANES)) * LANES
    gate_t, up_t = w_gate.T, w_up.T
    *outgoing, packed = attention(
        ring,
        piece,
        cols,
        queries,
        new_kv,
        cache,
        lengths,
        residual,
        route_ids.T,
        route_weights.T,
        gate_t,
        up_t,
        w_down,
    )
    chunks = ring.spread(outgoing, spaced=True)
    packed, *_ = lax.optimization_barrier((packed, *chunks))
    far_weights = swap(packed)
    ours, theirs, weight = project(ring, piece, chunks, w_out)
    stream = (ours + swap(theirs)).astype(jnp.bfloat16)
    stream, far_weights = lax.optimization_barrier((stream, far_weights))
    pieces = grid.spread([stream] * grid.z, spaced=False)
    sums, home = gate_up(
        grid, piece, cols, rows, pieces, gain.reshape(1, width), gate_t, up_t, far_weights
    )
    far_sums = swap(sums)
    parts = down(grid, piece, rows, sums, far_sums, weight, w_down, far_weights)
    order = sorted(range(grid.ep), key=lambda i: (grid.steps[i] == (0, 0), -grid.steps[i][0]))
    shares = [grid.send(parts[i], *grid.steps[i]) if any(grid.steps[i]) else parts[i] for i in order]
    return finish(piece, cols, home, far_sums, shares)


def general_body(
    residual,
    queries,
    new_kv,
    cache,
    lengths,
    w_out,
    gain,
    route_ids,
    route_weights,
    w_gate,
    w_up,
    w_down,
):
    row_count = queries.shape[0]
    head_count = queries.shape[1] // HD
    scaling = HD ** (-0.5)
    query_heads = queries.reshape(row_count, head_count, HD)
    key_rows = cache[:, :, :HD]
    value_rows = cache[:, :, HD:]
    scores = (
        jnp.einsum("rhd,rpd->rhp", query_heads, key_rows, preferred_element_type=jnp.float32)
        * scaling
    )
    usable = jnp.arange(cache.shape[1], dtype=jnp.int32)[None, :] < lengths[:, None]
    scores = jnp.where(usable[:, None, :], scores, -jnp.inf)
    own_score = (
        jnp.einsum("rhd,rd->rh", query_heads, new_kv[:, :HD], preferred_element_type=jnp.float32)
        * scaling
    )
    peak_score = jnp.maximum(jnp.max(scores, axis=2), own_score)
    cache_weight = jnp.exp(scores - peak_score[:, :, None])
    own_weight = jnp.exp(own_score - peak_score)
    denominator = jnp.sum(cache_weight, axis=2) + own_weight
    probabilities = (cache_weight / denominator[:, :, None]).astype(jnp.bfloat16)
    own_prob = (own_weight / denominator).astype(jnp.bfloat16)
    context = jnp.einsum(
        "rhp,rpd->rhd", probabilities, value_rows, preferred_element_type=jnp.float32
    )
    context = context + own_prob.astype(jnp.float32)[:, :, None] * new_kv[:, None, HD:].astype(
        jnp.float32
    )
    context = context.astype(jnp.bfloat16).reshape(row_count, head_count * HD)
    attn_cols = jnp.dot(
        lax.all_gather(context, "ep", axis=0, tiled=True), w_out, preferred_element_type=jnp.float32
    )
    attn_rows = lax.all_to_all(attn_cols, "ep", split_axis=0, concat_axis=1, tiled=True)
    attention = lax.psum(attn_rows, "tp")
    stream = residual.astype(jnp.float32) + attention
    mean_square = jnp.mean(stream * stream, axis=1, keepdims=True)
    normed = (stream * lax.rsqrt(mean_square + 1e-06) * gain[None, :]).astype(jnp.bfloat16)
    width = normed.shape[1]
    ep_size = lax.axis_size("ep")
    members = ep_size // EXPERTS
    slot_count = EXPERTS * CAP
    flat_ids = route_ids.reshape(-1)
    one_hot = (flat_ids[:, None] == jnp.arange(EXPERTS, dtype=jnp.int32)[None, :]).astype(jnp.int32)
    earlier = jnp.cumsum(one_hot, axis=0) - one_hot
    slot_index = jnp.sum(earlier * one_hot, axis=1)
    target = (flat_ids * CAP + slot_index).reshape(row_count, TOPK)
    placed = (target[:, :, None] == jnp.arange(slot_count, dtype=jnp.int32)[None, None, :]).astype(
        jnp.float32
    )
    chosen = jnp.sum(placed, axis=1).reshape(row_count, EXPERTS, CAP).astype(jnp.bfloat16)
    mixing = jnp.sum(placed * route_weights[:, :, None], axis=1).reshape(row_count, EXPERTS, CAP)
    outgoing = jnp.einsum("rec,rd->ecd", chosen, normed, preferred_element_type=jnp.float32).astype(
        jnp.bfloat16
    )
    outgoing = jnp.broadcast_to(outgoing[:, None], (EXPERTS, members, CAP, width)).reshape(
        ep_size * CAP, width
    )
    arrived = lax.all_to_all(outgoing, "ep", split_axis=0, concat_axis=0, tiled=True)
    gate_act = jnp.dot(arrived, w_gate, preferred_element_type=jnp.float32)
    up_act = jnp.dot(arrived, w_up, preferred_element_type=jnp.float32)
    hidden = (jax.nn.silu(gate_act) * up_act).astype(jnp.bfloat16)
    partial_value = jnp.dot(hidden, w_down, preferred_element_type=jnp.float32)
    halves = lax.psum_scatter(partial_value, "tp", scatter_dimension=1, tiled=True)
    returned = lax.all_to_all(halves, "ep", split_axis=0, concat_axis=0, tiled=True)
    returned = returned.reshape(EXPERTS, members, CAP, returned.shape[1])
    mixed = jnp.einsum("rec,egcw->rw", mixing, returned, precision=lax.Precision.HIGHEST)
    tp_start = lax.axis_index("tp") * mixed.shape[1]
    stream_part = lax.dynamic_slice_in_dim(stream, tp_start, mixed.shape[1], 1)
    return (stream_part + mixed).astype(jnp.bfloat16)


def body(*args):
    ep_size, cols, heads_width = lax.axis_size("ep"), args[5].shape[1], args[5].shape[0]
    if ep_size == 8 and lax.axis_size("tp") == 2 and cols % LANES == 0 and heads_width % (8 * HD) == 0:
        return tuned_body(Grid(ep_size, False), Grid(ep_size, True), *args)
    return general_body(*args)


def solution(mesh):
    placed = (
        P(("grp", "ep"), None),
        P(("grp", "ep"), "tp"),
        P(("grp", "ep"), None),
        P(("grp", "ep"), None, None),
        P(("grp", "ep")),
        P("tp", "ep"),
        P(),
        P(("grp", "ep"), None),
        P(("grp", "ep"), None),
        P(None, ("ep", "tp")),
        P(None, ("ep", "tp")),
        P(("ep", "tp"), None),
    )
    return jax.shard_map(
        body, mesh=mesh, in_specs=placed, out_specs=P(("grp", "ep"), "tp"), check_vma=False
    )
```

```python
import functools

import jax
import jax.numpy as jnp
from jax import lax
from jax.experimental import pallas as pl
from jax.experimental.pallas import tpu as pltpu
from jax.sharding import PartitionSpec as P

HD = 256
TOPK = 3
EXPERTS = 4
CAP = 8
LANES = 128


def params(mebibytes):
    return pltpu.CompilerParams(vmem_limit_bytes=mebibytes * 1024 * 1024)


def vmem():
    return pl.BlockSpec(memory_space=pltpu.VMEM)


def anywhere():
    return pl.BlockSpec(memory_space=pl.ANY)


def shape_of(shape, dtype):
    return jax.ShapeDtypeStruct(shape, dtype)


class Grid:
    def __init__(self, ep_size, pairs):
        self.ep, self.x, self.z, self.pairs = ep_size, ep_size // 4, 4, pairs
        self.steps = [(s, u) for s in range(self.z) for u in range(self.x)]

    def along_z(self, z, s):
        return z ^ s if self.pairs else (z + s) % self.z

    def send(self, arr, s, u):
        pairs = [
            (z * self.x + x, self.along_z(z, s) * self.x + (x + u) % self.x)
            for z in range(self.z)
            for x in range(self.x)
        ]
        return lax.ppermute(arr, "ep", pairs)

    def along_x(self, got, s):
        for u in range(1, self.x):
            got[s, u] = self.send(got[s, 0], 0, u)

    def spread(self, own, spaced):
        got = {(0, 0): own[0]}
        got[1, 0] = self.send(own[1], 1, 0)
        got[3, 0] = self.send(own[3], 3, 0)
        self.along_x(got, 0)
        far = own[2]
        if spaced:
            far, *_ = lax.optimization_barrier((far, got[1, 0], got[0, self.x - 1]))
        got[2, 0] = self.send(far, 2, 0)
        self.along_x(got, 1)
        self.along_x(got, 3)
        if not spaced:
            got[2, 0], *_ = lax.optimization_barrier((got[2, 0], got[1, self.x - 1]))
        self.along_x(got, 2)
        return [got[step] for step in self.steps]

    def source(self, step):
        me = lax.axis_index("ep")
        z = me // self.x
        z = z ^ step[0] if self.pairs else lax.rem(z - step[0] + self.z, self.z)
        return z * self.x + lax.rem(lax.rem(me, self.x) - step[1] + self.x, self.x)

    def target(self, step):
        s = step[0] if self.pairs else -step[0] % self.z
        return self.source((s, -step[1] % self.x))


def swap(arr):
    return lax.ppermute(arr, "tp", [(0, 1), (1, 0)])


def nt_dot(a, b):
    return lax.dot_general(a, b, (((1,), (1,)), ((), ())), preferred_element_type=jnp.float32)


def in_hbm():
    return pl.BlockSpec(memory_space=pltpu.HBM)


def attention(
    grid,
    piece,
    cols,
    queries,
    new_kv,
    cache,
    lengths,
    residual,
    route_ids,
    route_weights,
    gate_t,
    up_t,
    w_down,
):
    rows, width = queries.shape
    heads = width // HD
    ctx = cache.shape[1]
    parts = HD // LANES
    sizes = [grid.x] * grid.z
    note = piece + LANES
    scaling = HD ** (-0.5)
    units, features = gate_t.shape
    out_width = features // 2
    down_blocks = out_width // piece
    packed_rows = (2 * grid.ep + down_blocks) * units

    def kernel(*refs):
        sources, rest = refs[:7], refs[7:]
        gate_ref, up_ref, down_ref, rest = rest[0], rest[1], rest[2], rest[3:]
        out_refs, pack_ref, rest = rest[: len(sizes)], rest[len(sizes)], rest[len(sizes) + 1 :]
        q_ref, kv_ref, res_ref, ids_ref, wts_ref, len_ref, kept, turned, packed, sems, row_sems, pack_sems = rest
        cache_ref = sources[6]
        copies = [
            pltpu.make_async_copy(src, dst, sems.at[i])
            for i, (src, dst) in enumerate(
                zip(sources[:6], (q_ref, kv_ref, res_ref, ids_ref, wts_ref, len_ref))
            )
        ]
        row_copies = [
            pltpu.make_async_copy(cache_ref.at[r], kept.at[r], row_sems.at[r]) for r in range(rows)
        ]
        other = 1 - lax.axis_index("tp")
        blocks = []
        for j in range(grid.ep):
            begin = pl.multiple_of(j * cols + other * (cols - piece), LANES)
            blocks += [ref.at[:, pl.ds(begin, piece)] for ref in (gate_ref, up_ref)]
        for b in range(down_blocks):
            begin = pl.multiple_of(other * out_width + b * piece, LANES)
            blocks.append(down_ref.at[:, pl.ds(begin, piece)])
        packs = [
            pltpu.make_async_copy(block, packed.at[pl.ds(i * units, units), :], pack_sems.at[i])
            for i, block in enumerate(blocks)
        ]
        pack_out = pltpu.make_async_copy(packed, pack_ref, pack_sems.at[len(blocks)])
        for copy in copies[:2] + row_copies:
            copy.start()

        copies[0].wait()
        copies[1].wait()
        for h in range(heads):
            for c in range(parts):
                at = h * HD + c * LANES
                turned[c, h * rows : (h + 1) * rows, :] = q_ref[:, at : at + LANES].astype(jnp.float32)
        for copy in copies[2:] + packs:
            copy.start()
        new_k = kv_ref[:, :HD].astype(jnp.float32)
        new_v = kv_ref[:, HD:].astype(jnp.float32)
        scores, owns = [], []
        for r in range(rows):
            q = jnp.concatenate(
                [turned[c, pl.ds(r, heads, stride=rows), :] for c in range(parts)], axis=1
            )
            owns.append(jnp.sum(q * new_k[r : r + 1], axis=1, keepdims=True) * scaling)
            row_copies[r].wait()
            scores.append(nt_dot(q.astype(jnp.bfloat16), kept[r, :, :HD]) * scaling)

        for copy in copies[2:]:
            copy.wait()
        lane = lax.broadcasted_iota(jnp.int32, (rows, LANES), 1)
        square = (rows, rows)
        diagonal = lax.broadcasted_iota(jnp.int32, square, 0) == lax.broadcasted_iota(jnp.int32, square, 1)
        skip = lax.axis_index("tp") * (cols - piece)
        for s, u in grid.steps:
            to = grid.target((s, u))
            begin = pl.multiple_of(to * cols + skip, LANES)
            at = width + u * note
            out_refs[s][:, at : at + piece] = res_ref[:, pl.ds(begin, piece)]
            chosen = ids_ref[...] == to * EXPERTS // grid.ep
            across = jnp.sum(jnp.where(chosen, wts_ref[...], 0.0), axis=0, keepdims=True)
            weight = jnp.sum(
                jnp.where(diagonal, jnp.broadcast_to(across, square), 0.0), axis=1, keepdims=True
            )
            high = weight.astype(jnp.bfloat16).astype(jnp.float32)
            middle = (weight - high).astype(jnp.bfloat16).astype(jnp.float32)
            low = weight - high - middle
            tile = jnp.where(lane == 0, high, 0.0)
            tile = jnp.where(lane == 1, middle, tile)
            tile = jnp.where(lane == 2, low, tile)
            out_refs[s][:, at + piece : at + note] = tile.astype(jnp.bfloat16)

        place = lax.broadcasted_iota(jnp.int32, (heads, ctx), 1)
        probs, own_probs = [], []
        for r in range(rows):
            score = jnp.where(place < len_ref[r], scores[r], -jnp.inf)
            peak = jnp.maximum(jnp.max(score, axis=1, keepdims=True), owns[r])
            exps = jnp.exp(score - peak)
            own_exp = jnp.exp(owns[r] - peak)
            denominator = jnp.sum(exps, axis=1, keepdims=True) + own_exp
            probs.append((exps / denominator).astype(jnp.bfloat16))
            own_probs.append((own_exp / denominator).astype(jnp.bfloat16).astype(jnp.float32))
        for copy in packs:
            copy.wait()
        pack_out.start()
        for r in range(rows):
            mixed = jnp.dot(probs[r], kept[r, :, HD:], preferred_element_type=jnp.float32)
            mixed = mixed + own_probs[r] * new_v[r : r + 1]
            for c in range(parts):
                turned[c, r * heads : (r + 1) * heads, :] = mixed[:, c * LANES : (c + 1) * LANES]
        for h in range(heads):
            for c in range(parts):
                value = turned[c, pl.ds(h, rows, stride=heads), :].astype(jnp.bfloat16)
                begin = h * HD + c * LANES
                for ref in out_refs:
                    ref[:, begin : begin + LANES] = value
        pack_out.wait()

    return pl.pallas_call(
        kernel,
        name="attention",
        out_shape=[shape_of((rows, width + size * note), jnp.bfloat16) for size in sizes]
        + [shape_of((packed_rows, piece), jnp.bfloat16)],
        in_specs=[in_hbm()] * 10,
        out_specs=[vmem()] * len(sizes) + [in_hbm()],
        scratch_shapes=[
            pltpu.VMEM(queries.shape, jnp.bfloat16),
            pltpu.VMEM(new_kv.shape, jnp.bfloat16),
            pltpu.VMEM(residual.shape, jnp.bfloat16),
            pltpu.VMEM(route_ids.shape, jnp.int32),
            pltpu.VMEM(route_weights.shape, jnp.float32),
            pltpu.SMEM(lengths.shape, jnp.int32),
            pltpu.VMEM(cache.shape, jnp.bfloat16),
            pltpu.VMEM((parts, rows * heads, LANES), jnp.float32),
            pltpu.VMEM((packed_rows, piece), jnp.bfloat16),
            pltpu.SemaphoreType.DMA((6,)),
            pltpu.SemaphoreType.DMA((rows,)),
            pltpu.SemaphoreType.DMA((2 * grid.ep + down_blocks + 1,)),
        ],
        compiler_params=params(60),
    )(
        queries,
        new_kv,
        residual,
        route_ids,
        route_weights,
        lengths,
        cache,
        gate_t,
        up_t,
        w_down,
    )


def project(grid, piece, chunks, w_out):
    rows = chunks[0].shape[0]
    depth, cols = w_out.shape
    count = len(chunks)
    tall = rows * count
    blocks = 8
    block = depth // blocks
    note = piece + LANES

    def kernel(*refs):
        chunk_refs, rest = refs[:count], refs[count:]
        w_ref, ours_ref, theirs_ref, weight_ref, total = rest
        k = pl.program_id(0)

        lanes = pl.ds(pl.multiple_of(k * block, LANES), block)
        stacked = jnp.concatenate([ref[:, lanes] for ref in chunk_refs], axis=0)
        product = jnp.dot(stacked, w_ref[...], preferred_element_type=jnp.float32)

        @pl.when(k == 0)
        def _():
            total[...] = product

        @pl.when(k > 0)
        def _():
            total[...] += product

        @pl.when(k == blocks - 1)
        def _():
            core = lax.axis_index("tp")
            mine = pl.multiple_of(core * (cols - piece), LANES)
            other = pl.multiple_of((1 - core) * (cols - piece), LANES)
            for i, (s, u) in enumerate(grid.steps):
                here = pl.ds(pl.multiple_of(grid.source((s, u)) * rows, rows), rows)
                at = depth + u * note
                beside = chunk_refs[i][:, at : at + note].astype(jnp.float32)
                block_rows = slice(i * rows, (i + 1) * rows)
                ours_ref[here, :] = total[block_rows, pl.ds(mine, piece)] + beside[:, :piece]
                theirs_ref[here, :] = total[block_rows, pl.ds(other, piece)]
                weight_ref[here, :] = jnp.broadcast_to(
                    jnp.sum(beside[:, piece:], axis=1, keepdims=True), (rows, LANES)
                )

    def whole(arr):
        return pl.BlockSpec(arr.shape, lambda k: (0, 0))

    outs = [shape_of((tall, piece), jnp.float32)] * 2 + [shape_of((tall, LANES), jnp.float32)]
    return pl.pallas_call(
        kernel,
        name="project",
        grid=(blocks,),
        out_shape=outs,
        in_specs=[whole(c) for c in chunks] + [pl.BlockSpec((block, cols), lambda k: (k, 0))],
        out_specs=[whole(o) for o in outs],
        scratch_shapes=[
            pltpu.VMEM((tall, cols), jnp.float32),
        ],
        cost_estimate=pl.CostEstimate(
            flops=2 * tall * depth * cols,
            bytes_accessed=2 * depth * cols + 2 * tall * depth + 8 * tall * piece,
            transcendentals=0,
        ),
        compiler_params=params(48),
    )(*chunks, w_out)


def gate_up(grid, piece, cols, rows, pieces, gain, gate_t, up_t, other):
    tall = pieces[0].shape[0]
    units = gate_t.shape[0]
    count = grid.ep
    dup = 2 * piece - cols
    per_half = count // 2
    sums_width = 4 * units + LANES
    extra = -(-per_half * piece // sums_width)

    def kernel(*refs):
        piece_refs, rest = refs[:count], refs[count:]
        gain_ref, gate_ref, up_ref, other_ref, sums_ref, home_ref, held, home = rest
        home[1] = jnp.zeros((rows, extra * sums_width), jnp.float32)
        core = lax.axis_index("tp")
        me = lax.axis_index("ep")
        fresh = lax.broadcasted_iota(jnp.int32, (tall, piece), 1) >= core * dup
        square = jnp.zeros((tall, 1), jnp.float32)
        own_gate = jnp.zeros((units, tall), jnp.float32)
        own_up = jnp.zeros((units, tall), jnp.float32)
        far = jnp.zeros((2 * units, tall), jnp.float32)
        for i, step in enumerate(grid.steps):
            j = grid.source(step)
            lanes = pl.ds(pl.multiple_of(j * cols + core * (cols - piece), LANES), piece)
            stream = piece_refs[i][...].astype(jnp.float32)
            held[...] = stream
            mine = held[pl.ds(pl.multiple_of(me * rows, rows), rows), :]
            side = lax.rem(j // per_half + core, 2)
            at = pl.multiple_of(lax.rem(j, per_half) * piece, LANES)
            home[side, :, pl.ds(at, piece)] = mine
            stream = jnp.where(fresh, stream, 0.0)
            square = square + jnp.sum(stream * stream, axis=1, keepdims=True)
            scaled = (stream * gain_ref[:, lanes]).astype(jnp.bfloat16)
            own_gate = own_gate + nt_dot(gate_ref[:, lanes], scaled)
            own_up = own_up + nt_dot(up_ref[:, lanes], scaled)
            block = pl.ds(pl.multiple_of(j * 2 * units, 2 * units), 2 * units)
            far = far + nt_dot(other_ref[block, :], scaled)
        sums_ref[:tall, : 4 * units] = jnp.concatenate([own_gate, own_up, far], axis=0).T
        sums_ref[:tall, 4 * units :] = jnp.broadcast_to(square, (tall, LANES))
        for b in range(extra):
            at = tall + b * rows
            sums_ref[at : at + rows, :] = home[1, :, b * sums_width : (b + 1) * sums_width]
        home_ref[...] = home[0, :, : per_half * piece]

    return pl.pallas_call(
        kernel,
        name="gate_up",
        out_shape=[
            shape_of((tall + extra * rows, sums_width), jnp.float32),
            shape_of((rows, per_half * piece), jnp.float32),
        ],
        in_specs=[vmem()] * (count + 4),
        out_specs=[vmem()] * 2,
        scratch_shapes=[
            pltpu.VMEM((tall, piece), jnp.float32),
            pltpu.VMEM((2, rows, extra * sums_width), jnp.float32),
        ],
        compiler_params=params(8),
    )(*pieces, gain, gate_t, up_t, other)


def down(grid, piece, rows, sums, far_sums, weight, w_down, far_weights):
    tall = weight.shape[0]
    units, width = w_down.shape
    out_width = width // 2
    count = grid.ep

    def kernel(sums_ref, far_ref, weight_ref, down_ref, packed_ref, *rest):
        out_refs, total, down_half, sem = rest[:count], rest[count], rest[count + 1], rest[count + 2]
        begin = pl.multiple_of(lax.axis_index("tp") * out_width, LANES)
        copy = pltpu.make_async_copy(down_ref.at[:, pl.ds(begin, out_width)], down_half, sem)
        copy.start()
        square = (
            sums_ref[:tall, 4 * units : 4 * units + 1] + far_ref[:tall, 4 * units : 4 * units + 1]
        )
        scale = lax.rsqrt(square / width + 1e-06)

        def hidden(a, b):
            both = (
                sums_ref[:tall, a * units : (a + 2) * units]
                + far_ref[:tall, b * units : (b + 2) * units]
            )
            gate, up = both[:, :units] * scale, both[:, units:] * scale
            return (gate / (1.0 + jnp.exp(-gate)) * up).astype(jnp.bfloat16)

        near, far = hidden(0, 2), hidden(2, 0)
        copy.wait()
        for b in range(out_width // piece):
            span = slice(b * piece, (b + 1) * piece)
            block = slice((2 * count + b) * units, (2 * count + b + 1) * units)
            value = jnp.dot(near, down_half[:, span], preferred_element_type=jnp.float32)
            value = value + jnp.dot(far, packed_ref[block, :], preferred_element_type=jnp.float32)
            total[:, span] = value * weight_ref[:, :1]
        for i, step in enumerate(grid.steps):
            there = pl.ds(pl.multiple_of(grid.target(step) * rows, rows), rows)
            out_refs[i][...] = total[there, :].astype(out_refs[i].dtype)

    return pl.pallas_call(
        kernel,
        name="down",
        out_shape=[
            shape_of((rows, out_width), jnp.bfloat16 if i else jnp.float32) for i in range(count)
        ],
        in_specs=[vmem()] * 3 + [pl.BlockSpec(memory_space=pl.ANY), vmem()],
        out_specs=[vmem()] * count,
        scratch_shapes=[
            pltpu.VMEM((tall, out_width), jnp.float32),
            pltpu.VMEM((units, out_width), jnp.bfloat16),
            pltpu.SemaphoreType.DMA(()),
        ],
        compiler_params=params(8),
    )(sums, far_sums, weight, w_down, far_weights)


def finish(piece, cols, near, far_sums, parts):
    rows, out_width = parts[0].shape
    extra = -(-near.shape[1] // far_sums.shape[1])
    top = far_sums.shape[0] - extra * rows
    dup = 2 * piece - cols

    def kernel(near_ref, far_ref, *rest):
        part_refs, out_ref = rest[:-1], rest[-1]
        first = lax.axis_index("tp") == 0
        far = jnp.concatenate(
            [far_ref[top + b * rows : top + (b + 1) * rows, :] for b in range(extra)], axis=1
        )
        for c in range(out_width // cols):
            span = slice(c * piece, (c + 1) * piece)
            a, b = near_ref[:, span], far[:, span]
            low = jnp.where(first, a, b)
            high = jnp.where(first, b, a)[:, dup:]
            value = jnp.concatenate([low, high], axis=1)
            for ref in part_refs:
                value = value + ref[:, c * cols : (c + 1) * cols].astype(jnp.float32)
            out_ref[:, c * cols : (c + 1) * cols] = value.astype(jnp.bfloat16)

    return pl.pallas_call(
        kernel,
        name="finish",
        out_shape=shape_of((rows, out_width), jnp.bfloat16),
        in_specs=[vmem()] * (2 + len(parts)),
        out_specs=vmem(),
        compiler_params=params(4),
    )(near, far_sums, *parts)


def tuned_body(
    ring,
    grid,
    residual,
    queries,
    new_kv,
    cache,
    lengths,
    w_out,
    gain,
    route_ids,
    route_weights,
    w_gate,
    w_up,
    w_down,
):
    rows, width = residual.shape
    cols = w_out.shape[1]
    piece = -(-cols // (2 * LANES)) * LANES
    gate_t, up_t = w_gate.T, w_up.T
    *outgoing, packed = attention(
        ring,
        piece,
        cols,
        queries,
        new_kv,
        cache,
        lengths,
        residual,
        route_ids.T,
        route_weights.T,
        gate_t,
        up_t,
        w_down,
    )
    chunks = ring.spread(outgoing, spaced=True)
    packed, *_ = lax.optimization_barrier((packed, *chunks))
    far_weights = swap(packed)
    ours, theirs, weight = project(ring, piece, chunks, w_out)
    stream = (ours + swap(theirs)).astype(jnp.bfloat16)
    stream, far_weights = lax.optimization_barrier((stream, far_weights))
    pieces = grid.spread([stream] * grid.z, spaced=False)
    sums, home = gate_up(
        grid, piece, cols, rows, pieces, gain.reshape(1, width), gate_t, up_t, far_weights
    )
    far_sums = swap(sums)
    parts = down(grid, piece, rows, sums, far_sums, weight, w_down, far_weights)
    order = sorted(range(grid.ep), key=lambda i: (grid.steps[i] == (0, 0), -grid.steps[i][0]))
    shares = [grid.send(parts[i], *grid.steps[i]) if any(grid.steps[i]) else parts[i] for i in order]
    return finish(piece, cols, home, far_sums, shares)


def general_body(
    residual,
    queries,
    new_kv,
    cache,
    lengths,
    w_out,
    gain,
    route_ids,
    route_weights,
    w_gate,
    w_up,
    w_down,
):
    row_count = queries.shape[0]
    head_count = queries.shape[1] // HD
    scaling = HD ** (-0.5)
    query_heads = queries.reshape(row_count, head_count, HD)
    key_rows = cache[:, :, :HD]
    value_rows = cache[:, :, HD:]
    scores = (
        jnp.einsum("rhd,rpd->rhp", query_heads, key_rows, preferred_element_type=jnp.float32)
        * scaling
    )
    usable = jnp.arange(cache.shape[1], dtype=jnp.int32)[None, :] < lengths[:, None]
    scores = jnp.where(usable[:, None, :], scores, -jnp.inf)
    own_score = (
        jnp.einsum("rhd,rd->rh", query_heads, new_kv[:, :HD], preferred_element_type=jnp.float32)
        * scaling
    )
    peak_score = jnp.maximum(jnp.max(scores, axis=2), own_score)
    cache_weight = jnp.exp(scores - peak_score[:, :, None])
    own_weight = jnp.exp(own_score - peak_score)
    denominator = jnp.sum(cache_weight, axis=2) + own_weight
    probabilities = (cache_weight / denominator[:, :, None]).astype(jnp.bfloat16)
    own_prob = (own_weight / denominator).astype(jnp.bfloat16)
    context = jnp.einsum(
        "rhp,rpd->rhd", probabilities, value_rows, preferred_element_type=jnp.float32
    )
    context = context + own_prob.astype(jnp.float32)[:, :, None] * new_kv[:, None, HD:].astype(
        jnp.float32
    )
    context = context.astype(jnp.bfloat16).reshape(row_count, head_count * HD)
    attn_cols = jnp.dot(
        lax.all_gather(context, "ep", axis=0, tiled=True), w_out, preferred_element_type=jnp.float32
    )
    attn_rows = lax.all_to_all(attn_cols, "ep", split_axis=0, concat_axis=1, tiled=True)
    attention = lax.psum(attn_rows, "tp")
    stream = residual.astype(jnp.float32) + attention
    mean_square = jnp.mean(stream * stream, axis=1, keepdims=True)
    normed = (stream * lax.rsqrt(mean_square + 1e-06) * gain[None, :]).astype(jnp.bfloat16)
    width = normed.shape[1]
    ep_size = lax.axis_size("ep")
    members = ep_size // EXPERTS
    slot_count = EXPERTS * CAP
    flat_ids = route_ids.reshape(-1)
    one_hot = (flat_ids[:, None] == jnp.arange(EXPERTS, dtype=jnp.int32)[None, :]).astype(jnp.int32)
    earlier = jnp.cumsum(one_hot, axis=0) - one_hot
    slot_index = jnp.sum(earlier * one_hot, axis=1)
    target = (flat_ids * CAP + slot_index).reshape(row_count, TOPK)
    placed = (target[:, :, None] == jnp.arange(slot_count, dtype=jnp.int32)[None, None, :]).astype(
        jnp.float32
    )
    chosen = jnp.sum(placed, axis=1).reshape(row_count, EXPERTS, CAP).astype(jnp.bfloat16)
    mixing = jnp.sum(placed * route_weights[:, :, None], axis=1).reshape(row_count, EXPERTS, CAP)
    outgoing = jnp.einsum("rec,rd->ecd", chosen, normed, preferred_element_type=jnp.float32).astype(
        jnp.bfloat16
    )
    outgoing = jnp.broadcast_to(outgoing[:, None], (EXPERTS, members, CAP, width)).reshape(
        ep_size * CAP, width
    )
    arrived = lax.all_to_all(outgoing, "ep", split_axis=0, concat_axis=0, tiled=True)
    gate_act = jnp.dot(arrived, w_gate, preferred_element_type=jnp.float32)
    up_act = jnp.dot(arrived, w_up, preferred_element_type=jnp.float32)
    hidden = (jax.nn.silu(gate_act) * up_act).astype(jnp.bfloat16)
    partial_value = jnp.dot(hidden, w_down, preferred_element_type=jnp.float32)
    halves = lax.psum_scatter(partial_value, "tp", scatter_dimension=1, tiled=True)
    returned = lax.all_to_all(halves, "ep", split_axis=0, concat_axis=0, tiled=True)
    returned = returned.reshape(EXPERTS, members, CAP, returned.shape[1])
    mixed = jnp.einsum("rec,egcw->rw", mixing, returned, precision=lax.Precision.HIGHEST)
    tp_start = lax.axis_index("tp") * mixed.shape[1]
    stream_part = lax.dynamic_slice_in_dim(stream, tp_start, mixed.shape[1], 1)
    return (stream_part + mixed).astype(jnp.bfloat16)


def body(*args):
    ep_size, cols, heads_width = lax.axis_size("ep"), args[5].shape[1], args[5].shape[0]
    if ep_size == 8 and lax.axis_size("tp") == 2 and cols % LANES == 0 and heads_width % (8 * HD) == 0:
        return tuned_body(Grid(ep_size, False), Grid(ep_size, True), *args)
    return general_body(*args)


def solution(mesh):
    placed = (
        P(("grp", "ep"), None),
        P(("grp", "ep"), "tp"),
        P(("grp", "ep"), None),
        P(("grp", "ep"), None, None),
        P(("grp", "ep")),
        P("tp", "ep"),
        P(),
        P(("grp", "ep"), None),
        P(("grp", "ep"), None),
        P(None, ("ep", "tp")),
        P(None, ("ep", "tp")),
        P(("ep", "tp"), None),
    )
    return jax.shard_map(
        body, mesh=mesh, in_specs=placed, out_specs=P(("grp", "ep"), "tp"), check_vma=False
    )
```

```python
import functools

import jax
import jax.numpy as jnp
from jax import lax
from jax.experimental import pallas as pl
from jax.experimental.pallas import tpu as pltpu
from jax.sharding import PartitionSpec as P

HD = 256
TOPK = 3
EXPERTS = 4
CAP = 8
LANES = 128


def params(mebibytes):
    return pltpu.CompilerParams(vmem_limit_bytes=mebibytes * 1024 * 1024)


def vmem():
    return pl.BlockSpec(memory_space=pltpu.VMEM)


def anywhere():
    return pl.BlockSpec(memory_space=pl.ANY)


def shape_of(shape, dtype):
    return jax.ShapeDtypeStruct(shape, dtype)


class Grid:
    def __init__(self, ep_size, pairs):
        self.ep, self.x, self.z, self.pairs = ep_size, ep_size // 4, 4, pairs
        self.steps = [(s, u) for s in range(self.z) for u in range(self.x)]

    def along_z(self, z, s):
        return z ^ s if self.pairs else (z + s) % self.z

    def send(self, arr, s, u):
        pairs = [
            (z * self.x + x, self.along_z(z, s) * self.x + (x + u) % self.x)
            for z in range(self.z)
            for x in range(self.x)
        ]
        return lax.ppermute(arr, "ep", pairs)

    def along_x(self, got, s):
        for u in range(1, self.x):
            got[s, u] = self.send(got[s, 0], 0, u)

    def spread(self, own, spaced):
        got = {(0, 0): own[0]}
        got[1, 0] = self.send(own[1], 1, 0)
        got[3, 0] = self.send(own[3], 3, 0)
        self.along_x(got, 0)
        far = own[2]
        if spaced:
            far, *_ = lax.optimization_barrier((far, got[1, 0], got[0, self.x - 1]))
        got[2, 0] = self.send(far, 2, 0)
        self.along_x(got, 1)
        self.along_x(got, 3)
        if not spaced:
            got[2, 0], *_ = lax.optimization_barrier((got[2, 0], got[1, self.x - 1]))
        self.along_x(got, 2)
        return [got[step] for step in self.steps]

    def source(self, step):
        me = lax.axis_index("ep")
        z = me // self.x
        z = z ^ step[0] if self.pairs else lax.rem(z - step[0] + self.z, self.z)
        return z * self.x + lax.rem(lax.rem(me, self.x) - step[1] + self.x, self.x)

    def target(self, step):
        s = step[0] if self.pairs else -step[0] % self.z
        return self.source((s, -step[1] % self.x))


def swap(arr):
    return lax.ppermute(arr, "tp", [(0, 1), (1, 0)])


def nt_dot(a, b):
    return lax.dot_general(a, b, (((1,), (1,)), ((), ())), preferred_element_type=jnp.float32)


def in_hbm():
    return pl.BlockSpec(memory_space=pltpu.HBM)


def attention(
    grid,
    piece,
    cols,
    queries,
    new_kv,
    cache,
    lengths,
    residual,
    route_ids,
    route_weights,
    gate_t,
    up_t,
    w_down,
):
    rows, width = queries.shape
    heads = width // HD
    ctx = cache.shape[1]
    parts = HD // LANES
    sizes = [grid.x] * grid.z
    note = piece + LANES
    scaling = HD ** (-0.5)
    units, features = gate_t.shape
    out_width = features // 2
    down_blocks = out_width // piece
    packed_rows = (2 * grid.ep + down_blocks) * units

    def kernel(*refs):
        sources, rest = refs[:7], refs[7:]
        gate_ref, up_ref, down_ref, rest = rest[0], rest[1], rest[2], rest[3:]
        out_refs, pack_ref, rest = rest[: len(sizes)], rest[len(sizes)], rest[len(sizes) + 1 :]
        q_ref, kv_ref, res_ref, ids_ref, wts_ref, len_ref, kept, turned, packed, sems, row_sems, pack_sems = rest
        cache_ref = sources[6]
        copies = [
            pltpu.make_async_copy(src, dst, sems.at[i])
            for i, (src, dst) in enumerate(
                zip(sources[:6], (q_ref, kv_ref, res_ref, ids_ref, wts_ref, len_ref))
            )
        ]
        row_copies = [
            pltpu.make_async_copy(cache_ref.at[r], kept.at[r], row_sems.at[r]) for r in range(rows)
        ]
        other = 1 - lax.axis_index("tp")
        blocks = []
        for j in range(grid.ep):
            begin = pl.multiple_of(j * cols + other * (cols - piece), LANES)
            blocks += [ref.at[:, pl.ds(begin, piece)] for ref in (gate_ref, up_ref)]
        for b in range(down_blocks):
            begin = pl.multiple_of(other * out_width + b * piece, LANES)
            blocks.append(down_ref.at[:, pl.ds(begin, piece)])
        packs = [
            pltpu.make_async_copy(block, packed.at[pl.ds(i * units, units), :], pack_sems.at[i])
            for i, block in enumerate(blocks)
        ]
        pack_out = pltpu.make_async_copy(packed, pack_ref, pack_sems.at[len(blocks)])
        for copy in copies[:2] + row_copies:
            copy.start()

        copies[0].wait()
        copies[1].wait()
        for h in range(heads):
            for c in range(parts):
                at = h * HD + c * LANES
                turned[c, h * rows : (h + 1) * rows, :] = q_ref[:, at : at + LANES].astype(jnp.float32)
        for copy in copies[2:] + packs:
            copy.start()
        new_k = kv_ref[:, :HD].astype(jnp.float32)
        new_v = kv_ref[:, HD:].astype(jnp.float32)
        scores, owns = [], []
        for r in range(rows):
            q = jnp.concatenate(
                [turned[c, pl.ds(r, heads, stride=rows), :] for c in range(parts)], axis=1
            )
            owns.append(jnp.sum(q * new_k[r : r + 1], axis=1, keepdims=True) * scaling)
            row_copies[r].wait()
            scores.append(nt_dot(q.astype(jnp.bfloat16), kept[r, :, :HD]) * scaling)

        for copy in copies[2:]:
            copy.wait()
        lane = lax.broadcasted_iota(jnp.int32, (rows, LANES), 1)
        square = (rows, rows)
        diagonal = lax.broadcasted_iota(jnp.int32, square, 0) == lax.broadcasted_iota(jnp.int32, square, 1)
        skip = lax.axis_index("tp") * (cols - piece)
        for s, u in grid.steps:
            to = grid.target((s, u))
            begin = pl.multiple_of(to * cols + skip, LANES)
            at = width + u * note
            out_refs[s][:, at : at + piece] = res_ref[:, pl.ds(begin, piece)]
            chosen = ids_ref[...] == to * EXPERTS // grid.ep
            across = jnp.sum(jnp.where(chosen, wts_ref[...], 0.0), axis=0, keepdims=True)
            weight = jnp.sum(
                jnp.where(diagonal, jnp.broadcast_to(across, square), 0.0), axis=1, keepdims=True
            )
            high = weight.astype(jnp.bfloat16).astype(jnp.float32)
            middle = (weight - high).astype(jnp.bfloat16).astype(jnp.float32)
            low = weight - high - middle
            tile = jnp.where(lane == 0, high, 0.0)
            tile = jnp.where(lane == 1, middle, tile)
            tile = jnp.where(lane == 2, low, tile)
            out_refs[s][:, at + piece : at + note] = tile.astype(jnp.bfloat16)

        place = lax.broadcasted_iota(jnp.int32, (heads, ctx), 1)
        probs, own_probs = [], []
        for r in range(rows):
            score = jnp.where(place < len_ref[r], scores[r], -jnp.inf)
            peak = jnp.maximum(jnp.max(score, axis=1, keepdims=True), owns[r])
            exps = jnp.exp(score - peak)
            own_exp = jnp.exp(owns[r] - peak)
            denominator = jnp.sum(exps, axis=1, keepdims=True) + own_exp
            probs.append((exps / denominator).astype(jnp.bfloat16))
            own_probs.append((own_exp / denominator).astype(jnp.bfloat16).astype(jnp.float32))
        for copy in packs:
            copy.wait()
        pack_out.start()
        for r in range(rows):
            mixed = jnp.dot(probs[r], kept[r, :, HD:], preferred_element_type=jnp.float32)
            mixed = mixed + own_probs[r] * new_v[r : r + 1]
            for c in range(parts):
                turned[c, r * heads : (r + 1) * heads, :] = mixed[:, c * LANES : (c + 1) * LANES]
        for h in range(heads):
            for c in range(parts):
                value = turned[c, pl.ds(h, rows, stride=heads), :].astype(jnp.bfloat16)
                begin = h * HD + c * LANES
                for ref in out_refs:
                    ref[:, begin : begin + LANES] = value
        pack_out.wait()

    return pl.pallas_call(
        kernel,
        name="attention",
        out_shape=[shape_of((rows, width + size * note), jnp.bfloat16) for size in sizes]
        + [shape_of((packed_rows, piece), jnp.bfloat16)],
        in_specs=[in_hbm()] * 10,
        out_specs=[vmem()] * len(sizes) + [in_hbm()],
        scratch_shapes=[
            pltpu.VMEM(queries.shape, jnp.bfloat16),
            pltpu.VMEM(new_kv.shape, jnp.bfloat16),
            pltpu.VMEM(residual.shape, jnp.bfloat16),
            pltpu.VMEM(route_ids.shape, jnp.int32),
            pltpu.VMEM(route_weights.shape, jnp.float32),
            pltpu.SMEM(lengths.shape, jnp.int32),
            pltpu.VMEM(cache.shape, jnp.bfloat16),
            pltpu.VMEM((parts, rows * heads, LANES), jnp.float32),
            pltpu.VMEM((packed_rows, piece), jnp.bfloat16),
            pltpu.SemaphoreType.DMA((6,)),
            pltpu.SemaphoreType.DMA((rows,)),
            pltpu.SemaphoreType.DMA((2 * grid.ep + down_blocks + 1,)),
        ],
        compiler_params=params(60),
    )(
        queries,
        new_kv,
        residual,
        route_ids,
        route_weights,
        lengths,
        cache,
        gate_t,
        up_t,
        w_down,
    )


def project(grid, piece, chunks, w_out):
    rows = chunks[0].shape[0]
    depth, cols = w_out.shape
    count = len(chunks)
    tall = rows * count
    blocks = 16
    block = depth // blocks
    note = piece + LANES

    def kernel(*refs):
        chunk_refs, rest = refs[:count], refs[count:]
        w_ref, ours_ref, theirs_ref, weight_ref, total = rest
        k = pl.program_id(0)

        lanes = pl.ds(pl.multiple_of(k * block, LANES), block)
        stacked = jnp.concatenate([ref[:, lanes] for ref in chunk_refs], axis=0)
        product = jnp.dot(stacked, w_ref[...], preferred_element_type=jnp.float32)

        @pl.when(k == 0)
        def _():
            total[...] = product

        @pl.when(k > 0)
        def _():
            total[...] += product

        @pl.when(k == blocks - 1)
        def _():
            core = lax.axis_index("tp")
            mine = pl.multiple_of(core * (cols - piece), LANES)
            other = pl.multiple_of((1 - core) * (cols - piece), LANES)
            for i, (s, u) in enumerate(grid.steps):
                here = pl.ds(pl.multiple_of(grid.source((s, u)) * rows, rows), rows)
                at = depth + u * note
                beside = chunk_refs[i][:, at : at + note].astype(jnp.float32)
                block_rows = slice(i * rows, (i + 1) * rows)
                ours_ref[here, :] = total[block_rows, pl.ds(mine, piece)] + beside[:, :piece]
                theirs_ref[here, :] = total[block_rows, pl.ds(other, piece)]
                weight_ref[here, :] = jnp.broadcast_to(
                    jnp.sum(beside[:, piece:], axis=1, keepdims=True), (rows, LANES)
                )

    def whole(arr):
        return pl.BlockSpec(arr.shape, lambda k: (0, 0))

    outs = [shape_of((tall, piece), jnp.float32)] * 2 + [shape_of((tall, LANES), jnp.float32)]
    return pl.pallas_call(
        kernel,
        name="project",
        grid=(blocks,),
        out_shape=outs,
        in_specs=[whole(c) for c in chunks] + [pl.BlockSpec((block, cols), lambda k: (k, 0))],
        out_specs=[whole(o) for o in outs],
        scratch_shapes=[
            pltpu.VMEM((tall, cols), jnp.float32),
        ],
        cost_estimate=pl.CostEstimate(
            flops=2 * tall * depth * cols,
            bytes_accessed=2 * depth * cols + 2 * tall * depth + 8 * tall * piece,
            transcendentals=0,
        ),
        compiler_params=params(48),
    )(*chunks, w_out)


def gate_up(grid, piece, cols, rows, pieces, gain, gate_t, up_t, other):
    tall = pieces[0].shape[0]
    units = gate_t.shape[0]
    count = grid.ep
    dup = 2 * piece - cols
    per_half = count // 2
    sums_width = 4 * units + LANES
    extra = -(-per_half * piece // sums_width)

    def kernel(*refs):
        piece_refs, rest = refs[:count], refs[count:]
        gain_ref, gate_ref, up_ref, other_ref, sums_ref, home_ref, held, home = rest
        home[1] = jnp.zeros((rows, extra * sums_width), jnp.float32)
        core = lax.axis_index("tp")
        me = lax.axis_index("ep")
        fresh = lax.broadcasted_iota(jnp.int32, (tall, piece), 1) >= core * dup
        square = jnp.zeros((tall, 1), jnp.float32)
        own_gate = jnp.zeros((units, tall), jnp.float32)
        own_up = jnp.zeros((units, tall), jnp.float32)
        far = jnp.zeros((2 * units, tall), jnp.float32)
        for i, step in enumerate(grid.steps):
            j = grid.source(step)
            lanes = pl.ds(pl.multiple_of(j * cols + core * (cols - piece), LANES), piece)
            stream = piece_refs[i][...].astype(jnp.float32)
            held[...] = stream
            mine = held[pl.ds(pl.multiple_of(me * rows, rows), rows), :]
            side = lax.rem(j // per_half + core, 2)
            at = pl.multiple_of(lax.rem(j, per_half) * piece, LANES)
            home[side, :, pl.ds(at, piece)] = mine
            stream = jnp.where(fresh, stream, 0.0)
            square = square + jnp.sum(stream * stream, axis=1, keepdims=True)
            scaled = (stream * gain_ref[:, lanes]).astype(jnp.bfloat16)
            own_gate = own_gate + nt_dot(gate_ref[:, lanes], scaled)
            own_up = own_up + nt_dot(up_ref[:, lanes], scaled)
            block = pl.ds(pl.multiple_of(j * 2 * units, 2 * units), 2 * units)
            far = far + nt_dot(other_ref[block, :], scaled)
        sums_ref[:tall, : 4 * units] = jnp.concatenate([own_gate, own_up, far], axis=0).T
        sums_ref[:tall, 4 * units :] = jnp.broadcast_to(square, (tall, LANES))
        for b in range(extra):
            at = tall + b * rows
            sums_ref[at : at + rows, :] = home[1, :, b * sums_width : (b + 1) * sums_width]
        home_ref[...] = home[0, :, : per_half * piece]

    return pl.pallas_call(
        kernel,
        name="gate_up",
        out_shape=[
            shape_of((tall + extra * rows, sums_width), jnp.float32),
            shape_of((rows, per_half * piece), jnp.float32),
        ],
        in_specs=[vmem()] * (count + 4),
        out_specs=[vmem()] * 2,
        scratch_shapes=[
            pltpu.VMEM((tall, piece), jnp.float32),
            pltpu.VMEM((2, rows, extra * sums_width), jnp.float32),
        ],
        compiler_params=params(8),
    )(*pieces, gain, gate_t, up_t, other)


def down(grid, piece, rows, sums, far_sums, weight, w_down, far_weights):
    tall = weight.shape[0]
    units, width = w_down.shape
    out_width = width // 2
    count = grid.ep

    def kernel(sums_ref, far_ref, weight_ref, down_ref, packed_ref, *rest):
        out_refs, total, down_half, sem = rest[:count], rest[count], rest[count + 1], rest[count + 2]
        begin = pl.multiple_of(lax.axis_index("tp") * out_width, LANES)
        copy = pltpu.make_async_copy(down_ref.at[:, pl.ds(begin, out_width)], down_half, sem)
        copy.start()
        square = (
            sums_ref[:tall, 4 * units : 4 * units + 1] + far_ref[:tall, 4 * units : 4 * units + 1]
        )
        scale = lax.rsqrt(square / width + 1e-06)

        def hidden(a, b):
            both = (
                sums_ref[:tall, a * units : (a + 2) * units]
                + far_ref[:tall, b * units : (b + 2) * units]
            )
            gate, up = both[:, :units] * scale, both[:, units:] * scale
            return (gate / (1.0 + jnp.exp(-gate)) * up).astype(jnp.bfloat16)

        near, far = hidden(0, 2), hidden(2, 0)
        copy.wait()
        for b in range(out_width // piece):
            span = slice(b * piece, (b + 1) * piece)
            block = slice((2 * count + b) * units, (2 * count + b + 1) * units)
            value = jnp.dot(near, down_half[:, span], preferred_element_type=jnp.float32)
            value = value + jnp.dot(far, packed_ref[block, :], preferred_element_type=jnp.float32)
            total[:, span] = value * weight_ref[:, :1]
        for i, step in enumerate(grid.steps):
            there = pl.ds(pl.multiple_of(grid.target(step) * rows, rows), rows)
            out_refs[i][...] = total[there, :].astype(out_refs[i].dtype)

    return pl.pallas_call(
        kernel,
        name="down",
        out_shape=[
            shape_of((rows, out_width), jnp.bfloat16 if i else jnp.float32) for i in range(count)
        ],
        in_specs=[vmem()] * 3 + [pl.BlockSpec(memory_space=pl.ANY), vmem()],
        out_specs=[vmem()] * count,
        scratch_shapes=[
            pltpu.VMEM((tall, out_width), jnp.float32),
            pltpu.VMEM((units, out_width), jnp.bfloat16),
            pltpu.SemaphoreType.DMA(()),
        ],
        compiler_params=params(8),
    )(sums, far_sums, weight, w_down, far_weights)


def finish(piece, cols, near, far_sums, parts):
    rows, out_width = parts[0].shape
    extra = -(-near.shape[1] // far_sums.shape[1])
    top = far_sums.shape[0] - extra * rows
    dup = 2 * piece - cols

    def kernel(near_ref, far_ref, *rest):
        part_refs, out_ref = rest[:-1], rest[-1]
        first = lax.axis_index("tp") == 0
        far = jnp.concatenate(
            [far_ref[top + b * rows : top + (b + 1) * rows, :] for b in range(extra)], axis=1
        )
        for c in range(out_width // cols):
            span = slice(c * piece, (c + 1) * piece)
            a, b = near_ref[:, span], far[:, span]
            low = jnp.where(first, a, b)
            high = jnp.where(first, b, a)[:, dup:]
            value = jnp.concatenate([low, high], axis=1)
            for ref in part_refs:
                value = value + ref[:, c * cols : (c + 1) * cols].astype(jnp.float32)
            out_ref[:, c * cols : (c + 1) * cols] = value.astype(jnp.bfloat16)

    return pl.pallas_call(
        kernel,
        name="finish",
        out_shape=shape_of((rows, out_width), jnp.bfloat16),
        in_specs=[vmem()] * (2 + len(parts)),
        out_specs=vmem(),
        compiler_params=params(4),
    )(near, far_sums, *parts)


def tuned_body(
    ring,
    grid,
    residual,
    queries,
    new_kv,
    cache,
    lengths,
    w_out,
    gain,
    route_ids,
    route_weights,
    w_gate,
    w_up,
    w_down,
):
    rows, width = residual.shape
    cols = w_out.shape[1]
    piece = -(-cols // (2 * LANES)) * LANES
    gate_t, up_t = w_gate.T, w_up.T
    *outgoing, packed = attention(
        ring,
        piece,
        cols,
        queries,
        new_kv,
        cache,
        lengths,
        residual,
        route_ids.T,
        route_weights.T,
        gate_t,
        up_t,
        w_down,
    )
    chunks = ring.spread(outgoing, spaced=True)
    packed, *_ = lax.optimization_barrier((packed, *chunks))
    far_weights = swap(packed)
    ours, theirs, weight = project(ring, piece, chunks, w_out)
    stream = (ours + swap(theirs)).astype(jnp.bfloat16)
    stream, far_weights = lax.optimization_barrier((stream, far_weights))
    pieces = grid.spread([stream] * grid.z, spaced=False)
    sums, home = gate_up(
        grid, piece, cols, rows, pieces, gain.reshape(1, width), gate_t, up_t, far_weights
    )
    far_sums = swap(sums)
    parts = down(grid, piece, rows, sums, far_sums, weight, w_down, far_weights)
    order = sorted(range(grid.ep), key=lambda i: (grid.steps[i] == (0, 0), -grid.steps[i][0]))
    shares = [grid.send(parts[i], *grid.steps[i]) if any(grid.steps[i]) else parts[i] for i in order]
    return finish(piece, cols, home, far_sums, shares)


def general_body(
    residual,
    queries,
    new_kv,
    cache,
    lengths,
    w_out,
    gain,
    route_ids,
    route_weights,
    w_gate,
    w_up,
    w_down,
):
    row_count = queries.shape[0]
    head_count = queries.shape[1] // HD
    scaling = HD ** (-0.5)
    query_heads = queries.reshape(row_count, head_count, HD)
    key_rows = cache[:, :, :HD]
    value_rows = cache[:, :, HD:]
    scores = (
        jnp.einsum("rhd,rpd->rhp", query_heads, key_rows, preferred_element_type=jnp.float32)
        * scaling
    )
    usable = jnp.arange(cache.shape[1], dtype=jnp.int32)[None, :] < lengths[:, None]
    scores = jnp.where(usable[:, None, :], scores, -jnp.inf)
    own_score = (
        jnp.einsum("rhd,rd->rh", query_heads, new_kv[:, :HD], preferred_element_type=jnp.float32)
        * scaling
    )
    peak_score = jnp.maximum(jnp.max(scores, axis=2), own_score)
    cache_weight = jnp.exp(scores - peak_score[:, :, None])
    own_weight = jnp.exp(own_score - peak_score)
    denominator = jnp.sum(cache_weight, axis=2) + own_weight
    probabilities = (cache_weight / denominator[:, :, None]).astype(jnp.bfloat16)
    own_prob = (own_weight / denominator).astype(jnp.bfloat16)
    context = jnp.einsum(
        "rhp,rpd->rhd", probabilities, value_rows, preferred_element_type=jnp.float32
    )
    context = context + own_prob.astype(jnp.float32)[:, :, None] * new_kv[:, None, HD:].astype(
        jnp.float32
    )
    context = context.astype(jnp.bfloat16).reshape(row_count, head_count * HD)
    attn_cols = jnp.dot(
        lax.all_gather(context, "ep", axis=0, tiled=True), w_out, preferred_element_type=jnp.float32
    )
    attn_rows = lax.all_to_all(attn_cols, "ep", split_axis=0, concat_axis=1, tiled=True)
    attention = lax.psum(attn_rows, "tp")
    stream = residual.astype(jnp.float32) + attention
    mean_square = jnp.mean(stream * stream, axis=1, keepdims=True)
    normed = (stream * lax.rsqrt(mean_square + 1e-06) * gain[None, :]).astype(jnp.bfloat16)
    width = normed.shape[1]
    ep_size = lax.axis_size("ep")
    members = ep_size // EXPERTS
    slot_count = EXPERTS * CAP
    flat_ids = route_ids.reshape(-1)
    one_hot = (flat_ids[:, None] == jnp.arange(EXPERTS, dtype=jnp.int32)[None, :]).astype(jnp.int32)
    earlier = jnp.cumsum(one_hot, axis=0) - one_hot
    slot_index = jnp.sum(earlier * one_hot, axis=1)
    target = (flat_ids * CAP + slot_index).reshape(row_count, TOPK)
    placed = (target[:, :, None] == jnp.arange(slot_count, dtype=jnp.int32)[None, None, :]).astype(
        jnp.float32
    )
    chosen = jnp.sum(placed, axis=1).reshape(row_count, EXPERTS, CAP).astype(jnp.bfloat16)
    mixing = jnp.sum(placed * route_weights[:, :, None], axis=1).reshape(row_count, EXPERTS, CAP)
    outgoing = jnp.einsum("rec,rd->ecd", chosen, normed, preferred_element_type=jnp.float32).astype(
        jnp.bfloat16
    )
    outgoing = jnp.broadcast_to(outgoing[:, None], (EXPERTS, members, CAP, width)).reshape(
        ep_size * CAP, width
    )
    arrived = lax.all_to_all(outgoing, "ep", split_axis=0, concat_axis=0, tiled=True)
    gate_act = jnp.dot(arrived, w_gate, preferred_element_type=jnp.float32)
    up_act = jnp.dot(arrived, w_up, preferred_element_type=jnp.float32)
    hidden = (jax.nn.silu(gate_act) * up_act).astype(jnp.bfloat16)
    partial_value = jnp.dot(hidden, w_down, preferred_element_type=jnp.float32)
    halves = lax.psum_scatter(partial_value, "tp", scatter_dimension=1, tiled=True)
    returned = lax.all_to_all(halves, "ep", split_axis=0, concat_axis=0, tiled=True)
    returned = returned.reshape(EXPERTS, members, CAP, returned.shape[1])
    mixed = jnp.einsum("rec,egcw->rw", mixing, returned, precision=lax.Precision.HIGHEST)
    tp_start = lax.axis_index("tp") * mixed.shape[1]
    stream_part = lax.dynamic_slice_in_dim(stream, tp_start, mixed.shape[1], 1)
    return (stream_part + mixed).astype(jnp.bfloat16)


def body(*args):
    ep_size, cols, heads_width = lax.axis_size("ep"), args[5].shape[1], args[5].shape[0]
    if ep_size == 8 and lax.axis_size("tp") == 2 and cols % LANES == 0 and heads_width % (8 * HD) == 0:
        return tuned_body(Grid(ep_size, False), Grid(ep_size, True), *args)
    return general_body(*args)


def solution(mesh):
    placed = (
        P(("grp", "ep"), None),
        P(("grp", "ep"), "tp"),
        P(("grp", "ep"), None),
        P(("grp", "ep"), None, None),
        P(("grp", "ep")),
        P("tp", "ep"),
        P(),
        P(("grp", "ep"), None),
        P(("grp", "ep"), None),
        P(None, ("ep", "tp")),
        P(None, ("ep", "tp")),
        P(("ep", "tp"), None),
    )
    return jax.shard_map(
        body, mesh=mesh, in_specs=placed, out_specs=P(("grp", "ep"), "tp"), check_vma=False
    )
```
